512 devices in a mesh: seq: 32 (over z, core), head: 16 (over x, y).
Axes of the slice: x: 4, y: 4, z: 16, core: 2. Of those that a mesh axis runs over, the one named last changes fastest.
Arguments:
- queries: bfloat16 [16384, 8192], P('seq', 'head'), may hold values from -6 to 6
- keys: bfloat16 [16384, 8192], P('seq', 'head'), may hold values from -6 to 6
- values: bfloat16 [16384, 8192], P('seq', 'head'), may hold values from -6 to 6
- rates: float32 [64], P('head'), as said below
- gain: float32 [8192], P('head'), may hold values from 0.1 to 1.9
- cotangent: bfloat16 [16384, 8192], P('seq', 'head'), may hold values from -6 to 6
Outputs:
- attended: bfloat16 [16384, 8192], P('seq', 'head')
- query_grad: bfloat16 [16384, 8192], P('seq', 'head')
- key_grad: bfloat16 [16384, 8192], P('seq', 'head')
- value_grad: bfloat16 [16384, 8192], P('seq', 'head')
- gain_grad: float32 [8192], P('head')
The draws below stay inside these ranges and needn't reach their ends.
Inputs may be any that keep to these rules, and one draw needn't show every extreme that they name: `rates`: every rate is positive.
All inputs are finite; a program needn't handle non-finite values.
Results may differ from the reference program's by a relative error of at most 0.0051.
Values sent between devices are 32-bit elements; how exact they have to be, the bound alone decides.
No kernel may reach another device: no remote copies, remote signals or barrier semaphores. Data moves between devices by JAX's collectives and lax.ppermute only.
A program may use at most 64 MiB of HBM per device.

```python
import jax
import jax.numpy as jnp
from jax import lax

HEAD_DIM = 128
TOK_DEV = 512
HEADS = 64
TOKENS = 16384
N_SEQ = 32


def draw_rates(key, part):
    key = jax.random.fold_in(key, 7)
    key_pick = jax.random.fold_in(key, 1)
    key_fast = jax.random.fold_in(key, 2)
    key_slow = jax.random.fold_in(key, 3)
    share = 0.5
    fast_pick = jax.random.uniform(key_pick, (HEADS,), jnp.float32) < share
    fast_rate = jnp.exp(jax.random.uniform(key_fast, (HEADS,), jnp.float32, jnp.log(1.0 / 50.0), jnp.log(1.0 / 30.0)))
    slow_rate = jnp.exp(jax.random.uniform(key_slow, (HEADS,), jnp.float32, jnp.log(0.3 / TOKENS), jnp.log(2.0 / TOKENS)))
    return jnp.where(fast_pick, fast_rate, slow_rate).astype(jnp.float32)


def levels(own_key, dims, split, smallest, largest):
    level, own = 1.0, jax.random.fold_in(own_key, 6)
    for dim, blocks in split:
        draws = jnp.exp(jax.random.uniform(jax.random.fold_in(own, dim), (blocks,), jnp.float32, smallest / len(split), largest / len(split)))
        level = level * jnp.repeat(draws, dims[dim] // blocks).reshape([-1 if axis == dim else 1 for axis in range(len(dims))])
    return level


def normal_values(stream_key, extent, spread, most, cuts=(), held_as=jnp.bfloat16):
    entries = jax.random.normal(stream_key, extent, jnp.float32) * spread
    if len(cuts) > 0:
        entries = levels(stream_key, extent, cuts, -0.22, 0.18) * entries
    return jnp.clip(entries, min=-most, max=most).astype(held_as)


def setup_inputs(seed: int = 0) -> dict:
    splits = jax.random.split(jax.random.key(seed), 7)
    return {
        "queries": normal_values(splits[0], (TOKENS, HEADS * HEAD_DIM), 1.0, 6.0, ((0, 32), (1, 16))),
        "keys": normal_values(splits[1], (TOKENS, HEADS * HEAD_DIM), 1.0, 6.0, ((0, 32), (1, 16))),
        "values": normal_values(splits[2], (TOKENS, HEADS * HEAD_DIM), 1.0, 6.0, ((0, 32), (1, 16))),
        "rates": draw_rates(jax.random.fold_in(splits[6], 71), 0),
        "gain": jnp.clip(1.0 + 0.18 * jax.random.normal(splits[4], (HEADS * HEAD_DIM,), jnp.float32), 0.1, 1.9),
        "cotangent": normal_values(splits[5], (TOKENS, HEADS * HEAD_DIM), 1.0, 6.0, ((0, 32), (1, 16))),
    }


epsilon = 1e-06
HIGH = lax.Precision.HIGHEST

def rounded(array):
    return lax.optimization_barrier(array.astype(jnp.bfloat16)).astype(jnp.float32)

def decay_parts(rates, length):
    position = jnp.arange(length, dtype=jnp.float32)
    distance = position[:, None] - position[None, :]
    weight = jnp.where(distance[None] >= 0, jnp.exp(-rates[:, None, None] * jnp.maximum(distance, 0.0)[None]), 0.0)
    head_in = jnp.exp(-rates[None, :] * (position[:, None] + 1.0))
    tail_out = jnp.exp(-rates[None, :] * (length - 1.0 - position[:, None]))
    return (weight, head_in, tail_out)

def reference(queries, keys, values, rates, gain, cotangent):
    channels = HEADS * HEAD_DIM
    shape_four = (N_SEQ, TOK_DEV, HEADS, HEAD_DIM)
    query_rows = queries.reshape(shape_four).astype(jnp.float32)
    key_rows = keys.reshape(shape_four).astype(jnp.float32)
    value_rows = values.reshape(shape_four).astype(jnp.float32)
    weight, head_in, tail_out = decay_parts(rates, TOK_DEV)
    factor = jnp.exp(-rates * TOK_DEV)
    empty_state = jnp.zeros((HEADS, HEAD_DIM, HEAD_DIM), jnp.float32)

    def advance(state, block_total):
        return (factor[:, None, None] * state + block_total, state)

    def block_sum(pair_args):
        return jnp.einsum('shd,she->hde', pair_args[0] * tail_out[:, :, None], pair_args[1], precision=HIGH)
    block_sums = lax.map(block_sum, (key_rows, value_rows))
    carried, states_in = lax.scan(advance, empty_state, block_sums)

    def block_forward(inputs):
        query_b, key_b, value_b, state = inputs
        scores = jnp.einsum('thd,shd->hts', query_b, key_b, precision=HIGH)
        weights_bf = rounded(scores * weight)
        inner_part = jnp.einsum('hts,shd->thd', weights_bf, value_b, precision=HIGH)
        outer_part = head_in[:, :, None] * jnp.einsum('thd,hde->the', query_b, state, precision=HIGH)
        return inner_part + outer_part
    mixed = lax.map(block_forward, (query_rows, key_rows, value_rows, states_in))
    inv_rms = lax.rsqrt(lax.optimization_barrier(jnp.sum(mixed * mixed, axis=(2, 3))) / channels + epsilon)
    gain_heads = gain.reshape(HEADS, HEAD_DIM)
    normed = mixed * inv_rms[..., None, None]
    attended = (normed * gain_heads).astype(jnp.bfloat16).reshape(TOKENS, channels)
    upstream = cotangent.reshape(shape_four).astype(jnp.float32)
    gain_grad = lax.optimization_barrier(jnp.sum(upstream * normed, axis=(0, 1))).reshape(channels)
    scaled_up = upstream * gain_heads
    inner = lax.optimization_barrier(jnp.sum(scaled_up * mixed, axis=(2, 3)))
    mixed_grad = rounded(inv_rms[..., None, None] * scaled_up - mixed * (inv_rms ** 3 * inner / channels)[..., None, None])

    def back_sum(pair_args):
        return jnp.einsum('thd,the->hde', pair_args[0] * head_in[:, :, None], pair_args[1], precision=HIGH)
    back_sums = lax.map(back_sum, (query_rows, mixed_grad))
    carried_back, backs_in = lax.scan(advance, empty_state, back_sums, reverse=True)

    def block_backward(inputs):
        query_b, key_b, value_b, grad_b, state, back = inputs
        scores = jnp.einsum('thd,shd->hts', query_b, key_b, precision=HIGH)
        weights_bf = rounded(scores * weight)
        grad_weights = rounded(jnp.einsum('the,she->hts', grad_b, value_b, precision=HIGH) * weight)
        query_part = jnp.einsum('hts,shd->thd', grad_weights, key_b, precision=HIGH) + head_in[:, :, None] * jnp.einsum('the,hde->thd', grad_b, state, precision=HIGH)
        key_part = jnp.einsum('hts,thd->shd', grad_weights, query_b, precision=HIGH) + tail_out[:, :, None] * jnp.einsum('she,hde->shd', value_b, back, precision=HIGH)
        value_part = jnp.einsum('hts,the->she', weights_bf, grad_b, precision=HIGH) + tail_out[:, :, None] * jnp.einsum('shd,hde->she', key_b, back, precision=HIGH)
        return (query_part.astype(jnp.bfloat16), key_part.astype(jnp.bfloat16), value_part.astype(jnp.bfloat16))
    query_grad, key_grad, value_grad = lax.map(block_backward, (query_rows, key_rows, value_rows, mixed_grad, states_in, backs_in))
    return (attended, query_grad.reshape(TOKENS, channels), key_grad.reshape(TOKENS, channels), value_grad.reshape(TOKENS, channels), gain_grad)
```

```python
import jax
import jax.numpy as jnp
from jax import lax
from jax.experimental import pallas as pl
from jax.experimental.pallas import tpu as pltpu
from jax.sharding import PartitionSpec as P

epsilon = 1e-06
F32, BF16 = jnp.float32, jnp.bfloat16
GROUP = 8
EXTRA = 8


def dot(a, b, over_a, over_b):
    return lax.dot_general(a, b, (((over_a,), (over_b,)), ((), ())), preferred_element_type=F32)


def split(x):
    high = x.astype(BF16)
    return high, (x - high.astype(F32)).astype(BF16)


def dot_split_left(x, b, over_a, over_b):
    high, low = split(x)
    return dot(high, b, over_a, over_b) + dot(low, b, over_a, over_b)


def dot_split_right(a, x, over_a, over_b):
    high, low = split(x)
    return dot(a, high, over_a, over_b) + dot(a, low, over_a, over_b)


def rows_of(length, width=128):
    return lax.broadcasted_iota(jnp.int32, (length, width), 0).astype(F32)


def head_in_of(rate, length):
    return jnp.exp(-rate * (rows_of(length) + 1.0))


def tail_out_of(rate, length):
    return jnp.exp(-rate * (length - 1.0 - rows_of(length)))


def tile_weights(rate, half):
    distance = (
        lax.broadcasted_iota(jnp.int32, (half, half), 0) - lax.broadcasted_iota(jnp.int32, (half, half), 1)
    ).astype(F32)
    same = jnp.where(distance >= 0, jnp.exp(-rate * jnp.maximum(distance, 0.0)), 0.0)
    return same, jnp.exp(-rate * (distance + half))


def block_sum_kernel(rates, keys, values, out):
    rate = rates[pl.program_id(0)]
    length, size = keys.shape
    scaled = keys[...].astype(F32) * tail_out_of(rate, length)
    out[...] = dot_split_left(scaled, values[...], 0, 0).reshape(2, size // 2, size)


def intra_kernel(rates, queries, keys, values, out):
    rate = rates[pl.program_id(0)]
    half = queries.shape[0] // 2
    same, across = tile_weights(rate, half)
    first, second = pl.ds(0, half), pl.ds(half, half)

    def probs(t, s, weight):
        return (dot(queries[t, :], keys[s, :], 1, 1) * weight).astype(BF16)

    out[first, :] = dot(probs(first, first, same), values[first, :], 1, 0)
    out[second, :] = dot(probs(second, first, across), values[first, :], 1, 0) + dot(
        probs(second, second, same), values[second, :], 1, 0
    )


def mixed_kernel(rates, queries, state, intra, gain, cotangent, mixed, stats, square, inner):
    head = pl.program_id(0)
    rate = rates[head]
    length, size = queries.shape
    state_in = state[...].reshape(size, size)
    value = intra[...] + head_in_of(rate, length) * dot_split_right(queries[...], state_in, 1, 0)
    mixed[...] = value
    first = head == 0
    square[...] = jnp.where(first, 0.0, square[...]) + value * value
    inner[...] = jnp.where(first, 0.0, inner[...]) + cotangent[...].astype(F32) * gain[...] * value

    @pl.when(head == pl.num_programs(0) - 1)
    def _():
        pieces = []
        for ref in (square, inner):
            for start in range(0, length, 128):
                pieces.append(jnp.sum(ref[pl.ds(start, 128), :].T, axis=0, keepdims=True))
        tile = jnp.concatenate(pieces, axis=0)
        stats[...] = jnp.broadcast_to(tile[None], stats.shape)


def token_scales(received, channels, inv_out, coef_out):
    total = jnp.sum(received[...], axis=0)
    chunks = total.shape[0] // 2
    inv = lax.rsqrt(total[:chunks] / channels + epsilon)
    coef = inv * inv * inv * total[chunks:] / channels
    for chunk in range(chunks):
        rows = pl.ds(chunk * 128, 128)
        inv_out[rows, :] = jnp.broadcast_to(inv[chunk : chunk + 1], (128, 128)).T
        if coef_out is not None:
            coef_out[rows, :] = jnp.broadcast_to(coef[chunk : chunk + 1], (128, 128)).T


def back_sum_kernel(channels, rates, received, mixed, gain, cotangent, queries, grad, sums, inv, coef):
    head = pl.program_id(0)
    rate = rates[head]
    length, size = queries.shape

    @pl.when(head == 0)
    def _():
        token_scales(received, channels, inv, coef)

    upstream = cotangent[...].astype(F32)
    value = mixed[...]
    mixed_grad = (inv[...] * (upstream * gain[...]) - value * coef[...]).astype(BF16)
    grad[...] = mixed_grad
    scaled = queries[...].astype(F32) * head_in_of(rate, length)
    sums[:, pl.ds(0, size // 2), :] = dot_split_left(scaled, mixed_grad, 0, 0).reshape(2, size // 2, size)
    gain_grad = jnp.sum(upstream * (value * inv[...]), axis=0, keepdims=True)
    sums[:, pl.ds(size // 2, EXTRA), :] = jnp.broadcast_to(gain_grad[None], (2, EXTRA, size))


def grads_kernel(
    channels, rates, received, mixed, gain, queries, keys, values, grad, state,
    attended, query_grad, key_part, value_part, inv,
):
    head = pl.program_id(0)
    rate = rates[head]
    length, size = queries.shape
    half = length // 2

    @pl.when(head == 0)
    def _():
        token_scales(received, channels, inv, None)

    attended[...] = (mixed[...] * inv[...] * gain[...]).astype(BF16)
    same, across = tile_weights(rate, half)
    first, second = pl.ds(0, half), pl.ds(half, half)
    state_part = head_in_of(rate, length) * dot_split_right(grad[...], state[...].reshape(size, size), 1, 1)

    def weighted(a, b, t, s, weight):
        return (dot(a[t, :], b[s, :], 1, 1) * weight).astype(BF16)

    grads = [weighted(grad, values, *pair) for pair in ((first, first, same), (second, first, across), (second, second, same))]
    query_grad[first, :] = (dot(grads[0], keys[first, :], 1, 0) + state_part[:half]).astype(BF16)
    query_grad[second, :] = (
        dot(grads[1], keys[first, :], 1, 0) + dot(grads[2], keys[second, :], 1, 0) + state_part[half:]
    ).astype(BF16)
    key_part[first, :] = dot(grads[0], queries[first, :], 0, 0) + dot(grads[1], queries[second, :], 0, 0)
    key_part[second, :] = dot(grads[2], queries[second, :], 0, 0)
    probs = [weighted(queries, keys, *pair) for pair in ((first, first, same), (second, first, across), (second, second, same))]
    value_part[first, :] = dot(probs[0], grad[first, :], 0, 0) + dot(probs[1], grad[second, :], 0, 0)
    value_part[second, :] = dot(probs[2], grad[second, :], 0, 0)


def finish_kernel(rates, back, keys, values, key_part, value_part, key_grad, value_grad, gain_grad):
    rate = rates[pl.program_id(0)]
    length, size = keys.shape
    half = size // 2
    back_in = back[:, pl.ds(0, half), :].reshape(size, size)
    gain_grad[...] = back[0, pl.ds(half, 1), :]
    tail = tail_out_of(rate, length)
    key_grad[...] = (key_part[...] + tail * dot_split_right(values[...], back_in, 1, 1)).astype(BF16)
    value_grad[...] = (value_part[...] + tail * dot_split_right(keys[...], back_in, 1, 0)).astype(BF16)


def shift(x, groups, by):
    count = groups * GROUP
    return lax.ppermute(x, "seq", [(i, (i + by * GROUP) % count) for i in range(count)])


def scan_seq(x, rates, length, reverse, has_extra):
    count = lax.axis_size("seq")
    groups = count // GROUP
    members = [[g * GROUP + j for j in range(GROUP)] for g in range(groups)]
    position = lax.axis_index("seq")
    group, member = position // GROUP, position % GROUP
    rate = lax.dynamic_index_in_dim(rates, member * rates.shape[0] // GROUP, 0, False)
    factor, group_factor = jnp.exp(-rate * length), jnp.exp(-rate * (length * GROUP))
    parts = lax.all_to_all(x, "seq", 0, 0, axis_index_groups=members)
    rows = parts.shape[1] - (EXTRA if has_extra else 0)
    states = parts[:, :rows]
    order = range(GROUP - 1, -1, -1) if reverse else range(GROUP)
    total = jnp.zeros(states.shape[1:], F32)
    for k in order:
        total = factor * total + states[k]
    if has_extra:
        extra = jnp.sum(parts[:, rows:], axis=0)
        total = jnp.concatenate([total, extra], axis=0)
    sign = -1 if reverse else 1
    arrived = [shift(total, groups, sign * by) for by in range(1, groups)]
    carry = jnp.zeros(states.shape[1:], F32)
    for by in range(groups - 1, 0, -1):
        inside = group + by < groups if reverse else group - by >= 0
        carry = group_factor * carry + jnp.where(inside, arrived[by - 1][:rows], 0.0)
    before = [None] * GROUP
    for k in order:
        before[k] = carry
        carry = factor * carry + states[k]
    out = jnp.stack(before)
    if has_extra:
        extra = extra + sum(a[rows:] for a in arrived)
        out = jnp.concatenate([out, jnp.broadcast_to(extra[None], (GROUP,) + extra.shape)], axis=1)
    return lax.all_to_all(out, "seq", 0, 0, axis_index_groups=members)


def body(queries, keys, values, rates, gain, cotangent):
    length, channels = queries.shape
    heads = rates.shape[0]
    size = channels // heads
    head_devices = lax.axis_size("head")
    total_channels = channels * head_devices
    gain_row = gain.reshape(1, channels)

    smem = pl.BlockSpec(memory_space=pltpu.SMEM)
    tokens = pl.BlockSpec((length, size), lambda h: (0, h))
    row = pl.BlockSpec((1, size), lambda h: (0, h))
    shards = pl.BlockSpec((2, size // 2, size), lambda h: (h, 0, 0))
    shards_extra = pl.BlockSpec((2, size // 2 + EXTRA, size), lambda h: (h, 0, 0))
    stats_shape = (head_devices, 2 * length // 128, 128)
    stats_spec = pl.BlockSpec(stats_shape, lambda h: (0, 0, 0))
    column = pltpu.VMEM((length, size), F32)

    def array(kind, *shape):
        return jax.ShapeDtypeStruct(shape, kind)

    def call(kernel, in_specs, out_specs, out_shape, flops, nbytes, scratch=()):
        return pl.pallas_call(
            kernel,
            grid=(heads,),
            in_specs=in_specs,
            out_specs=out_specs,
            out_shape=out_shape,
            scratch_shapes=list(scratch),
            compiler_params=pltpu.CompilerParams(vmem_limit_bytes=32 * 1024 * 1024),
            cost_estimate=pl.CostEstimate(flops=flops, bytes_accessed=nbytes, transcendentals=0),
        )

    square = 2 * heads * length * length * size
    wide = array(F32, length, channels)
    narrow = array(BF16, length, channels)

    sums = call(
        block_sum_kernel, [smem, tokens, tokens], shards,
        array(F32, 2 * heads, size // 2, size), square // 2, 2 << 20,
    )(rates, keys, values)
    intra = call(intra_kernel, [smem, tokens, tokens, tokens], tokens, wide, 2 * square, 4 << 20)(
        rates, queries, keys, values
    )
    state_in = scan_seq(sums, rates, length, False, False)
    mixed, stats = call(
        mixed_kernel, [smem, tokens, shards, tokens, row, tokens], [tokens, stats_spec],
        [wide, array(F32, *stats_shape)], square // 2, 4 << 20, [column, column],
    )(rates, queries, state_in, intra, gain_row, cotangent)
    received = lax.all_to_all(stats, "head", 0, 0)
    grad, back_sums = call(
        lambda *refs: back_sum_kernel(total_channels, *refs),
        [smem, stats_spec, tokens, row, tokens, tokens], [tokens, shards_extra],
        [narrow, array(F32, 2 * heads, size // 2 + EXTRA, size)], square // 2, 4 << 20, [column, column],
    )(rates, received, mixed, gain_row, cotangent, queries)
    attended, query_grad, key_part, value_part = call(
        lambda *refs: grads_kernel(total_channels, *refs),
        [smem, stats_spec, tokens, row, tokens, tokens, tokens, tokens, shards],
        [tokens, tokens, tokens, tokens], [narrow, narrow, wide, wide], 6 * square, 6 << 20, [column],
    )(rates, received, mixed, gain_row, queries, keys, values, grad, state_in)
    back_in = scan_seq(back_sums, rates, length, True, True)
    key_grad, value_grad, gain_grad = call(
        finish_kernel, [smem, shards_extra, tokens, tokens, tokens, tokens], [tokens, tokens, row],
        [narrow, narrow, array(F32, 1, channels)], square, 4 << 20,
    )(rates, back_in, keys, values, key_part, value_part)
    return attended, query_grad, key_grad, value_grad, gain_grad.reshape(channels)


def solution(mesh):
    placed = (
        P("seq", "head"),
        P("seq", "head"),
        P("seq", "head"),
        P("head"),
        P("head"),
        P("seq", "head"),
    )
    return jax.shard_map(
        body,
        mesh=mesh,
        in_specs=placed,
        out_specs=(
            P("seq", "head"),
            P("seq", "head"),
            P("seq", "head"),
            P("seq", "head"),
            P("head"),
        ),
        check_vma=False,
    )
```

```python
import jax
import jax.numpy as jnp
from jax import lax
from jax.experimental import pallas as pl
from jax.experimental.pallas import tpu as pltpu
from jax.sharding import PartitionSpec as P

epsilon = 1e-06
F32, BF16 = jnp.float32, jnp.bfloat16
GROUP = 8
EXTRA = 8
VMEM_LIMIT = 16 * 1024 * 1024


def dot(a, b, over_a, over_b):
    return lax.dot_general(a, b, (((over_a,), (over_b,)), ((), ())), preferred_element_type=F32)


def split(x):
    high = x.astype(BF16)
    return high, (x - high.astype(F32)).astype(BF16)


def dot_split(a, x, over_a, over_x):
    parts = jnp.concatenate(split(x), axis=1 - over_x)
    both = dot(a, parts, over_a, over_x)
    return both[:, : both.shape[1] // 2] + both[:, both.shape[1] // 2 :]


def rows_of(length, width=128):
    return lax.broadcasted_iota(jnp.int32, (length, width), 0).astype(F32)


def exp_scalar(x):
    return jnp.exp(jnp.full((8, 128), x, F32))[:1]


def head_in_of(rate, length):
    base = jnp.exp(-rate * (rows_of(128) + 1.0))
    return jnp.concatenate([base * exp_scalar(-rate * start) for start in range(0, length, 128)], axis=0)


def tail_out_of(rate, length):
    base = jnp.exp(-rate * (127.0 - rows_of(128)))
    return jnp.concatenate([base * exp_scalar(-rate * (length - 128 - start)) for start in range(0, length, 128)], axis=0)


def tile_weights(rate, half):
    distance = (
        lax.broadcasted_iota(jnp.int32, (half, half), 0) - lax.broadcasted_iota(jnp.int32, (half, half), 1)
    ).astype(F32)
    same = jnp.where(distance >= 0, jnp.exp(-rate * jnp.maximum(distance, 0.0)), 0.0)
    column = jnp.exp(-rate * (rows_of(half) + 1.0))
    row = jnp.exp(-rate * (half - 1.0 - lax.broadcasted_iota(jnp.int32, (8, half), 1).astype(F32)))[:1]
    return same, jnp.concatenate([column] * (half // 128), axis=1) * row


def block_sum_kernel(rates, keys, values, out):
    rate = rates[pl.program_id(0)]
    length, size = keys.shape
    scaled = values[...].astype(F32) * tail_out_of(rate, length)
    out[...] = dot_split(keys[...], scaled, 0, 0).reshape(2, size // 2, size)


def intra_kernel(rates, queries, keys, values, out):
    rate = rates[pl.program_id(0)]
    half = queries.shape[0] // 2
    same, across = tile_weights(rate, half)
    first, second = pl.ds(0, half), pl.ds(half, half)

    def probs(t, s, weight):
        return (dot(queries[t, :], keys[s, :], 1, 1) * weight).astype(BF16)

    out[first, :] = dot(probs(first, first, same), values[first, :], 1, 0)
    out[second, :] = dot(probs(second, first, across), values[first, :], 1, 0) + dot(
        probs(second, second, same), values[second, :], 1, 0
    )


def column(h, size):
    return pl.ds(h * size, size)


def mixed_kernel(rates, queries, state, intra, gain, cotangent, mixed, stats, square, inner):
    length = queries.shape[0]
    heads = rates.shape[0]
    size = queries.shape[1] // heads
    for h in range(heads):
        cols = column(h, size)
        state_in = state[pl.ds(2 * h, 2)].reshape(size, size)
        value = intra[:, cols] + head_in_of(rates[h], length) * dot_split(queries[:, cols], state_in, 1, 0)
        mixed[:, cols] = value
        new_square, new_inner = value * value, cotangent[:, cols].astype(F32) * gain[:, cols] * value
        if h > 0:
            new_square, new_inner = new_square + square[...], new_inner + inner[...]
        square[...] = new_square
        inner[...] = new_inner
    pieces = []
    for ref in (square, inner):
        for start in range(0, length, 128):
            pieces.append(jnp.sum(ref[pl.ds(start, 128), :].T, axis=0, keepdims=True))
    tile = jnp.concatenate(pieces, axis=0)
    stats[...] = jnp.broadcast_to(tile[None], stats.shape)


def token_scales(received, channels, inv_out, coef_out):
    total = jnp.sum(received[...], axis=0)
    chunks = total.shape[0] // 2
    inv = lax.rsqrt(total[:chunks] / channels + epsilon)
    coef = inv * inv * inv * total[chunks:] / channels
    for chunk in range(chunks):
        rows = pl.ds(chunk * 128, 128)
        inv_out[rows, :] = jnp.broadcast_to(inv[chunk : chunk + 1], (128, 128)).T
        if coef_out is not None:
            coef_out[rows, :] = jnp.broadcast_to(coef[chunk : chunk + 1], (128, 128)).T


def back_sum_kernel(channels, rates, received, mixed, gain, cotangent, queries, grad, sums, inv, coef):
    length = queries.shape[0]
    heads = rates.shape[0]
    size = queries.shape[1] // heads
    token_scales(received, channels, inv, coef)
    for h in range(heads):
        cols = column(h, size)
        upstream = cotangent[:, cols].astype(F32)
        value = mixed[:, cols]
        mixed_grad = (inv[...] * (upstream * gain[:, cols]) - value * coef[...]).astype(BF16)
        grad[:, cols] = mixed_grad
        scaled = mixed_grad.astype(F32) * head_in_of(rates[h], length)
        shards = pl.ds(2 * h, 2)
        sums[shards, pl.ds(0, size // 2), :] = dot_split(queries[:, cols], scaled, 0, 0).reshape(2, size // 2, size)
        gain_grad = jnp.sum(upstream * (value * inv[...]), axis=0, keepdims=True)
        sums[shards, pl.ds(size // 2, EXTRA), :] = jnp.broadcast_to(gain_grad[None], (2, EXTRA, size))


def grads_kernel(
    channels, rates, received, mixed, gain, queries, keys, values, grad, state,
    attended, query_grad, key_part, value_part, inv,
):
    head = pl.program_id(0)
    rate = rates[head]
    length, size = queries.shape
    half = length // 2

    @pl.when(head == 0)
    def _():
        token_scales(received, channels, inv, None)

    attended[...] = (mixed[...] * inv[...] * gain[...]).astype(BF16)
    same, across = tile_weights(rate, half)
    first, second = pl.ds(0, half), pl.ds(half, half)
    state_part = head_in_of(rate, length) * dot_split(grad[...], state[...].reshape(size, size), 1, 1)

    def weighted(a, b, t, s, weight):
        return (dot(a[t, :], b[s, :], 1, 1) * weight).astype(BF16)

    grads = [weighted(grad, values, *pair) for pair in ((first, first, same), (second, first, across), (second, second, same))]
    query_grad[first, :] = (dot(grads[0], keys[first, :], 1, 0) + state_part[:half]).astype(BF16)
    query_grad[second, :] = (
        dot(grads[1], keys[first, :], 1, 0) + dot(grads[2], keys[second, :], 1, 0) + state_part[half:]
    ).astype(BF16)
    key_part[first, :] = dot(grads[0], queries[first, :], 0, 0) + dot(grads[1], queries[second, :], 0, 0)
    key_part[second, :] = dot(grads[2], queries[second, :], 0, 0)
    probs = [weighted(queries, keys, *pair) for pair in ((first, first, same), (second, first, across), (second, second, same))]
    value_part[first, :] = dot(probs[0], grad[first, :], 0, 0) + dot(probs[1], grad[second, :], 0, 0)
    value_part[second, :] = dot(probs[2], grad[second, :], 0, 0)


def finish_kernel(rates, back, keys, values, key_part, value_part, key_grad, value_grad, gain_grad):
    rate = rates[pl.program_id(0)]
    length, size = keys.shape
    half = size // 2
    back_in = back[:, pl.ds(0, half), :].reshape(size, size)
    gain_grad[...] = back[0, pl.ds(half, 1), :]
    tail = tail_out_of(rate, length)
    key_grad[...] = (key_part[...] + tail * dot_split(values[...], back_in, 1, 1)).astype(BF16)
    value_grad[...] = (value_part[...] + tail * dot_split(keys[...], back_in, 1, 0)).astype(BF16)


def fold_factors(rates, length):
    member = lax.axis_index("seq") % GROUP
    rate = rates[member * rates.shape[0] // GROUP]
    return exp_scalar(-rate * length), exp_scalar(-rate * (length * GROUP))


def totals_kernel(length, rates, parts, out):
    factor, _ = fold_factors(rates, length)
    rows = parts.shape[1] - EXTRA
    total = parts[GROUP - 1, :rows]
    for k in range(GROUP - 2, -1, -1):
        total = factor * total + parts[k, :rows]
    extra = sum(parts[k, rows:] for k in range(GROUP))
    for g in range(out.shape[0]):
        out[g, :rows] = total
        out[g, rows:] = extra


def fold_forward_kernel(length, rates, parts, *refs):
    factor, group_factor = fold_factors(rates, length)
    *arrived, out = refs
    carry = arrived[-1][...]
    for ref in arrived[-2::-1]:
        carry = group_factor * carry + ref[...]
    for k in range(GROUP):
        out[k] = carry
        carry = factor * carry + parts[k]


def fold_back_kernel(length, rates, parts, arrived, out):
    factor, group_factor = fold_factors(rates, length)
    rows = parts.shape[1] - EXTRA
    group = lax.axis_index("seq") // GROUP
    carry = jnp.zeros((rows, parts.shape[2]), F32)
    for g in range(arrived.shape[0] - 1, 0, -1):
        carry = jnp.where(group < g, group_factor * carry + arrived[g, :rows], carry)
    extra = sum(arrived[g, rows:] for g in range(arrived.shape[0]))
    for k in range(GROUP - 1, -1, -1):
        out[k, :rows] = carry
        out[k, rows:] = extra
        carry = factor * carry + parts[k, :rows]


def whole_call(kernel, out_shape, operands, **rest):
    return pl.pallas_call(
        kernel,
        in_specs=[pl.BlockSpec(memory_space=pltpu.SMEM)] + [pl.BlockSpec(memory_space=pltpu.VMEM)] * (len(operands) - 1),
        out_specs=jax.tree.map(lambda _: pl.BlockSpec(memory_space=pltpu.VMEM), out_shape),
        out_shape=out_shape,
        compiler_params=pltpu.CompilerParams(vmem_limit_bytes=VMEM_LIMIT),
        **rest,
    )(*operands)


def scan_forward(x, rates, length):
    count = lax.axis_size("seq")
    groups = count // GROUP
    members = [[g * GROUP + j for j in range(GROUP)] for g in range(groups)]
    parts = lax.all_to_all(x, "seq", 0, 0, axis_index_groups=members)
    rate = lax.dynamic_index_in_dim(rates, lax.axis_index("seq") % GROUP * rates.shape[0] // GROUP, 0, False)
    factor = jnp.exp(-rate * length)
    total = parts[0]
    for k in range(1, GROUP):
        total = factor * total + parts[k]
    arrived = [
        lax.ppermute(total, "seq", [(i, i + by * GROUP) for i in range(count - by * GROUP)]) for by in range(1, groups)
    ]
    out = whole_call(lambda *refs: fold_forward_kernel(length, *refs), like(x), [rates, parts, *arrived])
    return lax.all_to_all(out, "seq", 0, 0, axis_index_groups=members)


def scan_back(x, rates, length):
    groups = lax.axis_size("seq") // GROUP
    members = [[g * GROUP + j for j in range(GROUP)] for g in range(groups)]
    across = [[g * GROUP + j for g in range(groups)] for j in range(GROUP)]
    parts = lax.all_to_all(x, "seq", 0, 0, axis_index_groups=members)
    totals = whole_call(
        lambda *refs: totals_kernel(length, *refs), jax.ShapeDtypeStruct((groups,) + x.shape[1:], F32), [rates, parts]
    )
    arrived = lax.all_to_all(totals, "seq", 0, 0, axis_index_groups=across)
    out = whole_call(lambda *refs: fold_back_kernel(length, *refs), like(x), [rates, parts, arrived])
    return lax.all_to_all(out, "seq", 0, 0, axis_index_groups=members)


def like(x):
    return jax.ShapeDtypeStruct(x.shape, x.dtype)


def body(queries, keys, values, rates, gain, cotangent):
    length, channels = queries.shape
    heads = rates.shape[0]
    size = channels // heads
    head_devices = lax.axis_size("head")
    total_channels = channels * head_devices
    gain_row = gain.reshape(1, channels)

    smem = pl.BlockSpec(memory_space=pltpu.SMEM)
    tokens = pl.BlockSpec((length, size), lambda h: (0, h))
    row = pl.BlockSpec((1, size), lambda h: (0, h))
    shards = pl.BlockSpec((2, size // 2, size), lambda h: (h, 0, 0))
    shards_extra = pl.BlockSpec((2, size // 2 + EXTRA, size), lambda h: (h, 0, 0))
    stats_shape = (head_devices, 2 * length // 128, 128)
    stats_spec = pl.BlockSpec(stats_shape, lambda h: (0, 0, 0))
    scratch = pltpu.VMEM((length, size), F32)

    def array(kind, *shape):
        return jax.ShapeDtypeStruct(shape, kind)

    def call(kernel, in_specs, out_specs, out_shape, flops, nbytes, scratches=()):
        return pl.pallas_call(
            kernel,
            grid=(heads,),
            in_specs=in_specs,
            out_specs=out_specs,
            out_shape=out_shape,
            scratch_shapes=list(scratches),
            compiler_params=pltpu.CompilerParams(vmem_limit_bytes=VMEM_LIMIT),
            cost_estimate=pl.CostEstimate(flops=flops, bytes_accessed=nbytes, transcendentals=0),
        )

    square = 2 * heads * length * length * size
    wide = array(F32, length, channels)
    narrow = array(BF16, length, channels)

    hbm = lambda x: pltpu.with_memory_space_constraint(x, pltpu.HBM)
    sums = call(
        block_sum_kernel, [smem, tokens, tokens], shards,
        array(F32, 2 * heads, size // 2, size), square // 2, 2 << 20,
    )(hbm(rates), hbm(keys), hbm(values))
    intra = call(intra_kernel, [smem, tokens, tokens, tokens], tokens, wide, 2 * square, 4 << 20)(
        rates, queries, keys, values
    )
    state_in = scan_forward(sums, rates, length)
    mixed, stats = whole_call(
        mixed_kernel, [wide, array(F32, *stats_shape)],
        [rates, queries, state_in, intra, gain_row, cotangent], scratch_shapes=[scratch, scratch],
    )
    received = lax.all_to_all(stats, "head", 0, 0)
    grad, back_sums = whole_call(
        lambda *refs: back_sum_kernel(total_channels, *refs),
        [narrow, array(F32, 2 * heads, size // 2 + EXTRA, size)],
        [rates, received, mixed, gain_row, cotangent, queries], scratch_shapes=[scratch, scratch],
    )
    attended, query_grad, key_part, value_part = call(
        lambda *refs: grads_kernel(total_channels, *refs),
        [smem, stats_spec, tokens, row, tokens, tokens, tokens, tokens, shards],
        [tokens, tokens, tokens, tokens], [narrow, narrow, wide, wide], 6 * square, 6 << 20, [scratch],
    )(rates, received, mixed, gain_row, queries, keys, values, grad, state_in)
    back_in = scan_back(back_sums, rates, length)
    key_grad, value_grad, gain_grad = call(
        finish_kernel, [smem, shards_extra, tokens, tokens, tokens, tokens], [tokens, tokens, row],
        [narrow, narrow, array(F32, 1, channels)], square, 4 << 20,
    )(rates, back_in, keys, values, key_part, value_part)
    return attended, query_grad, key_grad, value_grad, gain_grad.reshape(channels)


def solution(mesh):
    placed = (
        P("seq", "head"),
        P("seq", "head"),
        P("seq", "head"),
        P("head"),
        P("head"),
        P("seq", "head"),
    )
    return jax.shard_map(
        body,
        mesh=mesh,
        in_specs=placed,
        out_specs=(
            P("seq", "head"),
            P("seq", "head"),
            P("seq", "head"),
            P("seq", "head"),
            P("head"),
        ),
        check_vma=False,
    )
```

```python
import jax
import jax.numpy as jnp
from jax import lax
from jax.experimental import pallas as pl
from jax.experimental.pallas import tpu as pltpu
from jax.sharding import PartitionSpec as P

epsilon = 1e-06
F32, BF16 = jnp.float32, jnp.bfloat16
GROUP = 8
EXTRA = 8
VMEM_LIMIT = 16 * 1024 * 1024


def dot(a, b, over_a, over_b):
    return lax.dot_general(a, b, (((over_a,), (over_b,)), ((), ())), preferred_element_type=F32)


def split(x):
    high = x.astype(BF16)
    return high, (x - high.astype(F32)).astype(BF16)


def dot_split(a, x, over_a, over_x):
    parts = jnp.concatenate(split(x), axis=1 - over_x)
    both = dot(a, parts, over_a, over_x)
    return both[:, : both.shape[1] // 2] + both[:, both.shape[1] // 2 :]


def rows_of(length, width=128):
    return lax.broadcasted_iota(jnp.int32, (length, width), 0).astype(F32)


def exp_scalar(x):
    return jnp.exp(jnp.full((8, 128), x, F32))[:1]


def head_in_of(rate, length):
    base = jnp.exp(-rate * (rows_of(128) + 1.0))
    return jnp.concatenate([base * exp_scalar(-rate * start) for start in range(0, length, 128)], axis=0)


def tail_out_of(rate, length):
    base = jnp.exp(-rate * (127.0 - rows_of(128)))
    return jnp.concatenate([base * exp_scalar(-rate * (length - 128 - start)) for start in range(0, length, 128)], axis=0)


def tile_weights(rate, half):
    distance = (
        lax.broadcasted_iota(jnp.int32, (half, half), 0) - lax.broadcasted_iota(jnp.int32, (half, half), 1)
    ).astype(F32)
    same = jnp.where(distance >= 0, jnp.exp(-rate * jnp.maximum(distance, 0.0)), 0.0)
    column = jnp.exp(-rate * (rows_of(half) + 1.0))
    row = jnp.exp(-rate * (half - 1.0 - lax.broadcasted_iota(jnp.int32, (8, half), 1).astype(F32)))[:1]
    return same, jnp.concatenate([column] * (half // 128), axis=1) * row


def column(h, size):
    return pl.ds(h * size, size)


def block_sum_kernel(rates, keys, values, out, key_rows, value_rows, arrived):
    length = keys.shape[0]
    heads = rates.shape[0]
    size = keys.shape[1] // heads
    copies = []
    for h in range(heads):
        cols = column(h, size)
        copies.append(
            [
                pltpu.make_async_copy(source.at[:, cols], rows.at[:, cols], arrived.at[2 * h + i])
                for i, (source, rows) in enumerate(((values, value_rows), (keys, key_rows)))
            ]
        )
        for copy in copies[-1]:
            copy.start()
    for h in range(heads):
        cols = column(h, size)
        tail = tail_out_of(rates[h], length)
        for copy in copies[h]:
            copy.wait()
        scaled = value_rows[:, cols].astype(F32) * tail
        out[pl.ds(2 * h, 2)] = dot_split(key_rows[:, cols], scaled, 0, 0).reshape(2, size // 2, size)


def intra_kernel(rates, queries, keys, values, out):
    rate = rates[pl.program_id(0)]
    half = queries.shape[0] // 2
    same, across = tile_weights(rate, half)
    first, second = pl.ds(0, half), pl.ds(half, half)

    def probs(t, s, weight):
        return (dot(queries[t, :], keys[s, :], 1, 1) * weight).astype(BF16)

    out[first, :] = dot(probs(first, first, same), values[first, :], 1, 0)
    out[second, :] = dot(probs(second, first, across), values[first, :], 1, 0) + dot(
        probs(second, second, same), values[second, :], 1, 0
    )


def mixed_kernel(rates, queries, state, intra, gain, cotangent, mixed, stats, square, inner):
    length = queries.shape[0]
    heads = rates.shape[0]
    size = queries.shape[1] // heads
    for h in range(heads):
        cols = column(h, size)
        state_in = state[pl.ds(2 * h, 2)].reshape(size, size)
        value = intra[:, cols] + head_in_of(rates[h], length) * dot_split(queries[:, cols], state_in, 1, 0)
        mixed[:, cols] = value
        new_square, new_inner = value * value, cotangent[:, cols].astype(F32) * gain[:, cols] * value
        if h > 0:
            new_square, new_inner = new_square + square[...], new_inner + inner[...]
        square[...] = new_square
        inner[...] = new_inner
    pieces = []
    for ref in (square, inner):
        for start in range(0, length, 128):
            pieces.append(jnp.sum(ref[pl.ds(start, 128), :].T, axis=0, keepdims=True))
    tile = jnp.concatenate(pieces, axis=0)
    stats[...] = jnp.broadcast_to(tile[None], stats.shape)


def token_scales(received, channels, inv_out, coef_out):
    total = jnp.sum(received[...], axis=0)
    chunks = total.shape[0] // 2
    inv = lax.rsqrt(total[:chunks] / channels + epsilon)
    coef = inv * inv * inv * total[chunks:] / channels
    for chunk in range(chunks):
        rows = pl.ds(chunk * 128, 128)
        inv_out[rows, :] = jnp.broadcast_to(inv[chunk : chunk + 1], (128, 128)).T
        if coef_out is not None:
            coef_out[rows, :] = jnp.broadcast_to(coef[chunk : chunk + 1], (128, 128)).T


def back_sum_kernel(channels, rates, received, mixed, gain, cotangent, queries, grad, sums, inv, coef):
    length = queries.shape[0]
    heads = rates.shape[0]
    size = queries.shape[1] // heads
    token_scales(received, channels, inv, coef)
    for h in range(heads):
        cols = column(h, size)
        upstream = cotangent[:, cols].astype(F32)
        value = mixed[:, cols]
        mixed_grad = (inv[...] * (upstream * gain[:, cols]) - value * coef[...]).astype(BF16)
        grad[:, cols] = mixed_grad
        scaled = mixed_grad.astype(F32) * head_in_of(rates[h], length)
        shards = pl.ds(2 * h, 2)
        sums[shards, pl.ds(0, size // 2), :] = dot_split(queries[:, cols], scaled, 0, 0).reshape(2, size // 2, size)
        gain_grad = jnp.sum(upstream * (value * inv[...]), axis=0, keepdims=True)
        sums[shards, pl.ds(size // 2, EXTRA), :] = jnp.broadcast_to(gain_grad[None], (2, EXTRA, size))


def weighted(a, b, t, s, weight):
    return (dot(a[t, :], b[s, :], 1, 1) * weight).astype(BF16)


def value_part_kernel(rates, queries, keys, grad, value_part, token):
    half = queries.shape[0] // 2
    same, across = tile_weights(rates[pl.program_id(0)], half)
    first, second = pl.ds(0, half), pl.ds(half, half)
    lower = weighted(queries, keys, second, first, across)
    value_part[first, :] = dot(weighted(queries, keys, first, first, same), grad[first, :], 0, 0) + dot(
        lower, grad[second, :], 0, 0
    )
    value_part[second, :] = dot(weighted(queries, keys, second, second, same), grad[second, :], 0, 0)
    token[...] = jnp.zeros_like(token)


def grads_kernel(
    channels, rates, received, mixed, gain, queries, keys, values, grad, state,
    attended, query_grad, key_part, token, inv,
):
    head = pl.program_id(0)
    rate = rates[head]
    length, size = queries.shape
    half = length // 2

    @pl.when(head == 0)
    def _():
        token_scales(received, channels, inv, None)

    attended[...] = (mixed[...] * inv[...] * gain[...]).astype(BF16)
    same, across = tile_weights(rate, half)
    first, second = pl.ds(0, half), pl.ds(half, half)
    state_part = head_in_of(rate, length) * dot_split(grad[...], state[...].reshape(size, size), 1, 1)
    upper = weighted(grad, values, first, first, same)
    lower = weighted(grad, values, second, first, across)
    final = weighted(grad, values, second, second, same)
    query_grad[first, :] = (dot(upper, keys[first, :], 1, 0) + state_part[:half]).astype(BF16)
    query_grad[second, :] = (
        dot(lower, keys[first, :], 1, 0) + dot(final, keys[second, :], 1, 0) + state_part[half:]
    ).astype(BF16)
    key_part[first, :] = dot(upper, queries[first, :], 0, 0) + dot(lower, queries[second, :], 0, 0)
    key_part[second, :] = dot(final, queries[second, :], 0, 0)
    token[...] = jnp.zeros_like(token)


def finish_kernel(
    rates, back, keys, values, key_part, value_part, key_grad, value_grad, gain_grad, key_rows, value_rows, sent
):
    length = keys.shape[0]
    heads = rates.shape[0]
    size = keys.shape[1] // heads
    half = size // 2
    copies = []
    for h in range(heads):
        cols = column(h, size)
        back_in = back[pl.ds(2 * h, 2), pl.ds(0, half), :].reshape(size, size)
        gain_grad[:, cols] = back[2 * h, pl.ds(half, 1), :]
        tail = tail_out_of(rates[h], length)
        key_rows[:, cols] = (key_part[:, cols] + tail * dot_split(values[:, cols], back_in, 1, 1)).astype(BF16)
        value_rows[:, cols] = (value_part[:, cols] + tail * dot_split(keys[:, cols], back_in, 1, 0)).astype(BF16)
        for i, (rows, target) in enumerate(((key_rows, key_grad), (value_rows, value_grad))):
            copy = pltpu.make_async_copy(rows.at[:, cols], target.at[:, cols], sent.at[2 * h + i])
            copy.start()
            copies.append(copy)
    for copy in copies:
        copy.wait()


def fold_factors(rates, length):
    member = lax.axis_index("seq") % GROUP
    rate = rates[member * rates.shape[0] // GROUP]
    return exp_scalar(-rate * length), exp_scalar(-rate * (length * GROUP))


def totals_kernel(length, rates, parts, token, out):
    factor, _ = fold_factors(rates, length)
    rows = parts.shape[1] - EXTRA
    total = parts[GROUP - 1, :rows]
    for k in range(GROUP - 2, -1, -1):
        total = factor * total + parts[k, :rows]
    extra = sum(parts[k, rows:] for k in range(GROUP))
    for g in range(out.shape[0]):
        out[g, :rows] = total
        out[g, rows:] = extra


def fold_forward_kernel(length, rates, parts, *refs):
    factor, group_factor = fold_factors(rates, length)
    *arrived, out = refs
    carry = arrived[-1][...]
    for ref in arrived[-2::-1]:
        carry = group_factor * carry + ref[...]
    for k in range(GROUP):
        out[k] = carry
        carry = factor * carry + parts[k]


def fold_back_kernel(length, rates, parts, arrived, token, out):
    factor, group_factor = fold_factors(rates, length)
    rows = parts.shape[1] - EXTRA
    group = lax.axis_index("seq") // GROUP
    carry = jnp.zeros((rows, parts.shape[2]), F32)
    for g in range(arrived.shape[0] - 1, 0, -1):
        carry = jnp.where(group < g, group_factor * carry + arrived[g, :rows], carry)
    extra = sum(arrived[g, rows:] for g in range(arrived.shape[0]))
    for k in range(GROUP - 1, -1, -1):
        out[k, :rows] = carry
        out[k, rows:] = extra
        carry = factor * carry + parts[k, :rows]


def whole_call(kernel, out_shape, operands, in_specs=None, out_specs=None, **rest):
    vmem = pl.BlockSpec(memory_space=pltpu.VMEM)
    if in_specs is None:
        in_specs = [pl.BlockSpec(memory_space=pltpu.SMEM)] + [vmem] * (len(operands) - 1)
    if out_specs is None:
        out_specs = jax.tree.map(lambda _: vmem, out_shape)
    return pl.pallas_call(
        kernel,
        in_specs=in_specs,
        out_specs=out_specs,
        out_shape=out_shape,
        compiler_params=pltpu.CompilerParams(vmem_limit_bytes=VMEM_LIMIT),
        **rest,
    )(*operands)


def scan_forward(x, rates, length):
    count = lax.axis_size("seq")
    groups = count // GROUP
    members = [[g * GROUP + j for j in range(GROUP)] for g in range(groups)]
    parts = lax.all_to_all(x, "seq", 0, 0, axis_index_groups=members)
    rate = lax.dynamic_index_in_dim(rates, lax.axis_index("seq") % GROUP * rates.shape[0] // GROUP, 0, False)
    factor = jnp.exp(-rate * length)
    total = parts[0]
    for k in range(1, GROUP):
        total = factor * total + parts[k]
    arrived = [
        lax.ppermute(total, "seq", [(i, i + by * GROUP) for i in range(count - by * GROUP)]) for by in range(1, groups)
    ]
    out = whole_call(lambda *refs: fold_forward_kernel(length, *refs), like(x), [rates, parts, *arrived])
    return lax.all_to_all(out, "seq", 0, 0, axis_index_groups=members)


def scan_back(x, rates, length, first_token, second_token):
    groups = lax.axis_size("seq") // GROUP
    members = [[g * GROUP + j for j in range(GROUP)] for g in range(groups)]
    across = [[g * GROUP + j for g in range(groups)] for j in range(GROUP)]
    parts = lax.all_to_all(x, "seq", 0, 0, axis_index_groups=members)
    totals = whole_call(
        lambda *refs: totals_kernel(length, *refs), jax.ShapeDtypeStruct((groups,) + x.shape[1:], F32),
        [rates, parts, first_token],
    )
    arrived = lax.all_to_all(totals, "seq", 0, 0, axis_index_groups=across)
    out = whole_call(lambda *refs: fold_back_kernel(length, *refs), like(x), [rates, parts, arrived, second_token])
    return lax.all_to_all(out, "seq", 0, 0, axis_index_groups=members)


def like(x):
    return jax.ShapeDtypeStruct(x.shape, x.dtype)


def body(queries, keys, values, rates, gain, cotangent):
    length, channels = queries.shape
    heads = rates.shape[0]
    size = channels // heads
    head_devices = lax.axis_size("head")
    total_channels = channels * head_devices
    gain_row = gain.reshape(1, channels)

    smem = pl.BlockSpec(memory_space=pltpu.SMEM)
    tokens = pl.BlockSpec((length, size), lambda h: (0, h))
    row = pl.BlockSpec((1, size), lambda h: (0, h))
    shards = pl.BlockSpec((2, size // 2, size), lambda h: (h, 0, 0))
    shards_extra = pl.BlockSpec((2, size // 2 + EXTRA, size), lambda h: (h, 0, 0))
    stats_shape = (head_devices, 2 * length // 128, 128)
    stats_spec = pl.BlockSpec(stats_shape, lambda h: (0, 0, 0))
    scratch = pltpu.VMEM((length, size), F32)

    def array(kind, *shape):
        return jax.ShapeDtypeStruct(shape, kind)

    def call(kernel, in_specs, out_specs, out_shape, flops, nbytes, scratches=()):
        return pl.pallas_call(
            kernel,
            grid=(heads,),
            in_specs=in_specs,
            out_specs=out_specs,
            out_shape=out_shape,
            scratch_shapes=list(scratches),
            compiler_params=pltpu.CompilerParams(vmem_limit_bytes=VMEM_LIMIT),
            cost_estimate=pl.CostEstimate(flops=flops, bytes_accessed=nbytes, transcendentals=0),
        )

    square = 2 * heads * length * length * size
    wide = array(F32, length, channels)
    narrow = array(BF16, length, channels)

    hbm = lambda x: pltpu.with_memory_space_constraint(x, pltpu.HBM)
    vmem = lambda x: pltpu.with_memory_space_constraint(x, pltpu.VMEM)
    anywhere = pl.BlockSpec(memory_space=pl.ANY)
    in_vmem = pl.BlockSpec(memory_space=pltpu.VMEM)
    rows_scratch = pltpu.VMEM((length, channels), BF16)
    copies = pltpu.SemaphoreType.DMA((2 * heads,))
    sums = whole_call(
        block_sum_kernel, array(F32, 2 * heads, size // 2, size), [hbm(rates), hbm(keys), hbm(values)],
        in_specs=[smem, anywhere, anywhere], scratch_shapes=[rows_scratch, rows_scratch, copies],
    )
    intra = call(intra_kernel, [smem, tokens, tokens, tokens], tokens, wide, 2 * square, 4 << 20)(
        rates, queries, keys, values
    )
    state_in = scan_forward(sums, rates, length)
    mixed, stats = whole_call(
        mixed_kernel, [wide, array(F32, *stats_shape)],
        [rates, queries, state_in, intra, gain_row, cotangent], scratch_shapes=[scratch, scratch],
    )
    received = lax.all_to_all(stats, "head", 0, 0)
    grad, back_sums = whole_call(
        lambda *refs: back_sum_kernel(total_channels, *refs),
        [narrow, array(F32, 2 * heads, size // 2 + EXTRA, size)],
        [rates, received, mixed, gain_row, cotangent, queries], scratch_shapes=[scratch, scratch],
    )
    token = array(F32, 8, 128)
    token_spec = pl.BlockSpec((8, 128), lambda h: (0, 0))
    part = pltpu.VMEM((length, channels), F32)
    value_part, first_token = call(
        value_part_kernel, [smem, tokens, tokens, tokens], [tokens, token_spec],
        [part, token], 2 * square, 4 << 20,
    )(rates, queries, keys, grad)
    attended, query_grad, key_part, second_token = call(
        lambda *refs: grads_kernel(total_channels, *refs),
        [smem, stats_spec, tokens, row, tokens, tokens, tokens, tokens, shards],
        [tokens, tokens, tokens, token_spec], [narrow, narrow, part, token], 4 * square, 6 << 20, [scratch],
    )(rates, received, mixed, gain_row, queries, keys, values, grad, state_in)
    back_in = scan_back(back_sums, rates, length, first_token, second_token)
    key_grad, value_grad, gain_grad = whole_call(
        finish_kernel, [narrow, narrow, array(F32, 1, channels)],
        [rates, back_in, keys, values, vmem(key_part), vmem(value_part)],
        out_specs=[anywhere, anywhere, in_vmem], scratch_shapes=[rows_scratch, rows_scratch, copies],
    )
    return attended, query_grad, key_grad, value_grad, gain_grad.reshape(channels)


def solution(mesh):
    placed = (
        P("seq", "head"),
        P("seq", "head"),
        P("seq", "head"),
        P("head"),
        P("head"),
        P("seq", "head"),
    )
    return jax.shard_map(
        body,
        mesh=mesh,
        in_specs=placed,
        out_specs=(
            P("seq", "head"),
            P("seq", "head"),
            P("seq", "head"),
            P("seq", "head"),
            P("head"),
        ),
        check_vma=False,
    )
```

```python
import jax
import jax.numpy as jnp
from jax import lax
from jax.experimental import pallas as pl
from jax.experimental.pallas import tpu as pltpu
from jax.sharding import PartitionSpec as P

epsilon = 1e-06
F32, BF16 = jnp.float32, jnp.bfloat16
GROUP = 8
EXTRA = 8
VMEM_LIMIT = 16 * 1024 * 1024


def dot(a, b, over_a, over_b):
    return lax.dot_general(a, b, (((over_a,), (over_b,)), ((), ())), preferred_element_type=F32)


def split(x):
    high = x.astype(BF16)
    return high, (x - high.astype(F32)).astype(BF16)


def dot_split(a, x, over_a, over_x):
    parts = jnp.concatenate(split(x), axis=1 - over_x)
    both = dot(a, parts, over_a, over_x)
    return both[:, : both.shape[1] // 2] + both[:, both.shape[1] // 2 :]


def rows_of(length, width=128):
    return lax.broadcasted_iota(jnp.int32, (length, width), 0).astype(F32)


def exp_scalar(x):
    return jnp.exp(jnp.full((8, 128), x, F32))[:1]


def head_in_of(rate, length):
    base = jnp.exp(-rate * (rows_of(128) + 1.0))
    return jnp.concatenate([base * exp_scalar(-rate * start) for start in range(0, length, 128)], axis=0)


def tail_out_of(rate, length):
    base = jnp.exp(-rate * (127.0 - rows_of(128)))
    return jnp.concatenate([base * exp_scalar(-rate * (length - 128 - start)) for start in range(0, length, 128)], axis=0)


def tile_weights(rate, half):
    distance = (
        lax.broadcasted_iota(jnp.int32, (half, half), 0) - lax.broadcasted_iota(jnp.int32, (half, half), 1)
    ).astype(F32)
    same = jnp.where(distance >= 0, jnp.exp(-rate * jnp.maximum(distance, 0.0)), 0.0)
    column = jnp.exp(-rate * (rows_of(half) + 1.0))
    row = jnp.exp(-rate * (half - 1.0 - lax.broadcasted_iota(jnp.int32, (8, half), 1).astype(F32)))[:1]
    return same, jnp.concatenate([column] * (half // 128), axis=1) * row


def column(h, size):
    return pl.ds(h * size, size)


def half_start(mine, heads):
    core = lax.axis_index("seq") % 2
    return (core if mine else 1 - core) * (heads // 2)


def block_sum_kernel(mine, rates, keys, values, out, key_rows, value_rows, arrived):
    length = keys.shape[0]
    heads = rates.shape[0]
    size = keys.shape[1] // heads
    start = half_start(mine, heads)
    copies = []
    for h in range(heads // 2):
        cols = pl.ds(pl.multiple_of((start + h) * size, size), size)
        copies.append(
            [
                pltpu.make_async_copy(source.at[:, cols], rows.at[:, column(h, size)], arrived.at[2 * h + i])
                for i, (source, rows) in enumerate(((values, value_rows), (keys, key_rows)))
            ]
        )
        for copy in copies[-1]:
            copy.start()
    for h in range(heads // 2):
        cols = column(h, size)
        tail = tail_out_of(rates[start + h], length)
        for copy in copies[h]:
            copy.wait()
        scaled = value_rows[:, cols].astype(F32) * tail
        out[h] = dot_split(key_rows[:, cols], scaled, 0, 0)


def intra_kernel(rates, queries, keys, values, out):
    rate = rates[pl.program_id(0)]
    half = queries.shape[0] // 2
    same, across = tile_weights(rate, half)
    first, second = pl.ds(0, half), pl.ds(half, half)

    def probs(t, s, weight):
        return (dot(queries[t, :], keys[s, :], 1, 1) * weight).astype(BF16)

    out[first, :] = dot(probs(first, first, same), values[first, :], 1, 0)
    out[second, :] = dot(probs(second, first, across), values[first, :], 1, 0) + dot(
        probs(second, second, same), values[second, :], 1, 0
    )


def mixed_kernel(rates, queries, mine, other, intra, gain, cotangent, mixed, stats, state, square, inner):
    length = queries.shape[0]
    heads = rates.shape[0]
    size = queries.shape[1] // heads
    start = half_start(True, heads)
    for h in range(heads):
        cols = column(h, size)
        slot = h % (heads // 2)
        state_in = jnp.where(start == h - slot, mine[slot], other[slot])
        state[pl.ds(2 * h, 2)] = state_in.reshape(2, size // 2, size)
        value = intra[:, cols] + head_in_of(rates[h], length) * dot_split(queries[:, cols], state_in, 1, 0)
        mixed[:, cols] = value
        new_square, new_inner = value * value, cotangent[:, cols].astype(F32) * gain[:, cols] * value
        if h > 0:
            new_square, new_inner = new_square + square[...], new_inner + inner[...]
        square[...] = new_square
        inner[...] = new_inner
    pieces = []
    for ref in (square, inner):
        for start in range(0, length, 128):
            pieces.append(jnp.sum(ref[pl.ds(start, 128), :].T, axis=0, keepdims=True))
    tile = jnp.concatenate(pieces, axis=0)
    stats[...] = jnp.broadcast_to(tile[None], stats.shape)


def token_scales(received, channels, inv_out, coef_out):
    total = jnp.sum(received[...], axis=0)
    chunks = total.shape[0] // 2
    inv = lax.rsqrt(total[:chunks] / channels + epsilon)
    coef = inv * inv * inv * total[chunks:] / channels
    for chunk in range(chunks):
        rows = pl.ds(chunk * 128, 128)
        inv_out[rows, :] = jnp.broadcast_to(inv[chunk : chunk + 1], (128, 128)).T
        if coef_out is not None:
            coef_out[rows, :] = jnp.broadcast_to(coef[chunk : chunk + 1], (128, 128)).T


def back_sum_kernel(channels, rates, received, mixed, gain, cotangent, queries, grad, sums, inv, coef):
    length = queries.shape[0]
    heads = rates.shape[0]
    size = queries.shape[1] // heads
    token_scales(received, channels, inv, coef)
    for h in range(heads):
        cols = column(h, size)
        upstream = cotangent[:, cols].astype(F32)
        value = mixed[:, cols]
        mixed_grad = (inv[...] * (upstream * gain[:, cols]) - value * coef[...]).astype(BF16)
        grad[:, cols] = mixed_grad
        scaled = mixed_grad.astype(F32) * head_in_of(rates[h], length)
        shards = pl.ds(2 * h, 2)
        sums[shards, pl.ds(0, size // 2), :] = dot_split(queries[:, cols], scaled, 0, 0).reshape(2, size // 2, size)
        gain_grad = jnp.sum(upstream * (value * inv[...]), axis=0, keepdims=True)
        sums[shards, pl.ds(size // 2, EXTRA), :] = jnp.broadcast_to(gain_grad[None], (2, EXTRA, size))


def weighted(a, b, t, s, weight):
    return (dot(a[t, :], b[s, :], 1, 1) * weight).astype(BF16)


def value_part_kernel(rates, queries, keys, grad, value_part, token):
    half = queries.shape[0] // 2
    same, across = tile_weights(rates[pl.program_id(0)], half)
    first, second = pl.ds(0, half), pl.ds(half, half)
    lower = weighted(queries, keys, second, first, across)
    value_part[first, :] = dot(weighted(queries, keys, first, first, same), grad[first, :], 0, 0) + dot(
        lower, grad[second, :], 0, 0
    )
    value_part[second, :] = dot(weighted(queries, keys, second, second, same), grad[second, :], 0, 0)
    token[...] = jnp.zeros_like(token)


def grads_kernel(
    channels, rates, received, mixed, gain, queries, keys, values, grad, state,
    attended, query_grad, key_part, token, inv,
):
    head = pl.program_id(0)
    rate = rates[head]
    length, size = queries.shape
    half = length // 2

    @pl.when(head == 0)
    def _():
        token_scales(received, channels, inv, None)

    attended[...] = (mixed[...] * inv[...] * gain[...]).astype(BF16)
    same, across = tile_weights(rate, half)
    first, second = pl.ds(0, half), pl.ds(half, half)
    state_part = head_in_of(rate, length) * dot_split(grad[...], state[...].reshape(size, size), 1, 1)
    upper = weighted(grad, values, first, first, same)
    lower = weighted(grad, values, second, first, across)
    final = weighted(grad, values, second, second, same)
    query_grad[first, :] = (dot(upper, keys[first, :], 1, 0) + state_part[:half]).astype(BF16)
    query_grad[second, :] = (
        dot(lower, keys[first, :], 1, 0) + dot(final, keys[second, :], 1, 0) + state_part[half:]
    ).astype(BF16)
    key_part[first, :] = dot(upper, queries[first, :], 0, 0) + dot(lower, queries[second, :], 0, 0)
    key_part[second, :] = dot(final, queries[second, :], 0, 0)
    token[...] = jnp.zeros_like(token)


def finish_kernel(
    rates, back, keys, values, key_part, value_part, key_grad, value_grad, gain_grad, key_rows, value_rows, sent
):
    length = keys.shape[0]
    heads = rates.shape[0]
    size = keys.shape[1] // heads
    half = size // 2
    copies = []
    for h in range(heads):
        cols = column(h, size)
        back_in = back[pl.ds(2 * h, 2), pl.ds(0, half), :].reshape(size, size)
        gain_grad[:, cols] = back[2 * h, pl.ds(half, 1), :]
        tail = tail_out_of(rates[h], length)
        key_rows[:, cols] = (key_part[:, cols] + tail * dot_split(values[:, cols], back_in, 1, 1)).astype(BF16)
        value_rows[:, cols] = (value_part[:, cols] + tail * dot_split(keys[:, cols], back_in, 1, 0)).astype(BF16)
        for i, (rows, target) in enumerate(((key_rows, key_grad), (value_rows, value_grad))):
            copy = pltpu.make_async_copy(rows.at[:, cols], target.at[:, cols], sent.at[2 * h + i])
            copy.start()
            copies.append(copy)
    for copy in copies:
        copy.wait()


def fold_factors(rates, length):
    member = lax.axis_index("seq") % GROUP
    rate = rates[member * rates.shape[0] // GROUP]
    return exp_scalar(-rate * length), exp_scalar(-rate * (length * GROUP))


def totals_kernel(length, rates, parts, token, out):
    factor, _ = fold_factors(rates, length)
    rows = parts.shape[1] - EXTRA
    total = parts[GROUP - 1, :rows]
    for k in range(GROUP - 2, -1, -1):
        total = factor * total + parts[k, :rows]
    extra = sum(parts[k, rows:] for k in range(GROUP))
    for g in range(out.shape[0]):
        out[g, :rows] = total
        out[g, rows:] = extra


def is_first(reverse):
    return (lax.axis_index("seq") % 2) == (1 if reverse else 0)


def chip_sum_kernel(length, reverse, rates, keep, received, out):
    start = half_start(True, rates.shape[0])
    first = is_first(reverse)
    for h in range(keep.shape[0]):
        factor = exp_scalar(-rates[start + h] * length)
        own, other = keep[h], received[h]
        out[h] = jnp.where(first, factor * own + other, factor * other + own)


def fold_chips_kernel(length, reverse, rates, parts, out):
    chips = parts.shape[0]
    heads = rates.shape[0]
    chip = lax.axis_index("seq") // 2
    factor = exp_scalar(-rates[half_start(True, heads) + chip * (heads // 2) // chips] * (2 * length))
    carry = jnp.zeros(parts.shape[1:], F32)
    for k in range(chips - 1, -1, -1) if reverse else range(chips):
        out[k] = carry
        carry = factor * carry + parts[k]


def states_kernel(length, reverse, rates, state, keep, received, mine, give):
    start = half_start(True, rates.shape[0])
    first = is_first(reverse)
    for h in range(keep.shape[0]):
        factor = exp_scalar(-rates[start + h] * length)
        before = state[h]
        after = factor * before + jnp.where(first, keep[h], received[h])
        mine[h] = jnp.where(first, before, after)
        give[h] = jnp.where(first, after, before)


def fold_back_kernel(length, rates, parts, arrived, token, out):
    factor, group_factor = fold_factors(rates, length)
    rows = parts.shape[1] - EXTRA
    group = lax.axis_index("seq") // GROUP
    carry = jnp.zeros((rows, parts.shape[2]), F32)
    for g in range(arrived.shape[0] - 1, 0, -1):
        carry = jnp.where(group < g, group_factor * carry + arrived[g, :rows], carry)
    extra = sum(arrived[g, rows:] for g in range(arrived.shape[0]))
    for k in range(GROUP - 1, -1, -1):
        out[k, :rows] = carry
        out[k, rows:] = extra
        carry = factor * carry + parts[k, :rows]


def whole_call(kernel, out_shape, operands, in_specs=None, out_specs=None, **rest):
    vmem = pl.BlockSpec(memory_space=pltpu.VMEM)
    if in_specs is None:
        in_specs = [pl.BlockSpec(memory_space=pltpu.SMEM)] + [vmem] * (len(operands) - 1)
    if out_specs is None:
        out_specs = jax.tree.map(lambda _: vmem, out_shape)
    return pl.pallas_call(
        kernel,
        in_specs=in_specs,
        out_specs=out_specs,
        out_shape=out_shape,
        compiler_params=pltpu.CompilerParams(vmem_limit_bytes=VMEM_LIMIT),
        **rest,
    )(*operands)


def swap(x):
    return lax.ppermute(x, "seq", [(i, i ^ 1) for i in range(lax.axis_size("seq"))])


def scan_chips(keep, received, rates, length, reverse):
    chips = lax.axis_size("seq") // 2
    members = [[2 * z + core for z in range(chips)] for core in range(2)]
    flat = (chips, keep.shape[0] * keep.shape[1] // chips, keep.shape[2])
    sums = whole_call(
        lambda *refs: chip_sum_kernel(length, reverse, *refs), like(keep), [rates, keep, received]
    )
    parts = lax.all_to_all(sums.reshape(flat), "seq", 0, 0, axis_index_groups=members)
    folded = whole_call(lambda *refs: fold_chips_kernel(length, reverse, *refs), like(parts), [rates, parts])
    state = lax.all_to_all(folded, "seq", 0, 0, axis_index_groups=members).reshape(keep.shape)
    mine, give = whole_call(
        lambda *refs: states_kernel(length, reverse, *refs), [like(keep), like(keep)], [rates, state, keep, received]
    )
    return mine, swap(give)


def scan_back(x, rates, length, first_token, second_token):
    groups = lax.axis_size("seq") // GROUP
    members = [[g * GROUP + j for j in range(GROUP)] for g in range(groups)]
    across = [[g * GROUP + j for g in range(groups)] for j in range(GROUP)]
    parts = lax.all_to_all(x, "seq", 0, 0, axis_index_groups=members)
    totals = whole_call(
        lambda *refs: totals_kernel(length, *refs), jax.ShapeDtypeStruct((groups,) + x.shape[1:], F32),
        [rates, parts, first_token],
    )
    arrived = lax.all_to_all(totals, "seq", 0, 0, axis_index_groups=across)
    out = whole_call(lambda *refs: fold_back_kernel(length, *refs), like(x), [rates, parts, arrived, second_token])
    return lax.all_to_all(out, "seq", 0, 0, axis_index_groups=members)


def like(x):
    return jax.ShapeDtypeStruct(x.shape, x.dtype)


def body(queries, keys, values, rates, gain, cotangent):
    length, channels = queries.shape
    heads = rates.shape[0]
    size = channels // heads
    head_devices = lax.axis_size("head")
    total_channels = channels * head_devices
    gain_row = gain.reshape(1, channels)

    smem = pl.BlockSpec(memory_space=pltpu.SMEM)
    tokens = pl.BlockSpec((length, size), lambda h: (0, h))
    row = pl.BlockSpec((1, size), lambda h: (0, h))
    shards = pl.BlockSpec((2, size // 2, size), lambda h: (h, 0, 0))
    shards_extra = pl.BlockSpec((2, size // 2 + EXTRA, size), lambda h: (h, 0, 0))
    stats_shape = (head_devices, 2 * length // 128, 128)
    stats_spec = pl.BlockSpec(stats_shape, lambda h: (0, 0, 0))
    scratch = pltpu.VMEM((length, size), F32)

    def array(kind, *shape):
        return jax.ShapeDtypeStruct(shape, kind)

    def call(kernel, in_specs, out_specs, out_shape, flops, nbytes, scratches=()):
        return pl.pallas_call(
            kernel,
            grid=(heads,),
            in_specs=in_specs,
            out_specs=out_specs,
            out_shape=out_shape,
            scratch_shapes=list(scratches),
            compiler_params=pltpu.CompilerParams(vmem_limit_bytes=VMEM_LIMIT),
            cost_estimate=pl.CostEstimate(flops=flops, bytes_accessed=nbytes, transcendentals=0),
        )

    square = 2 * heads * length * length * size
    wide = array(F32, length, channels)
    narrow = array(BF16, length, channels)

    hbm = lambda x: pltpu.with_memory_space_constraint(x, pltpu.HBM)
    vmem = lambda x: pltpu.with_memory_space_constraint(x, pltpu.VMEM)
    anywhere = pl.BlockSpec(memory_space=pl.ANY)
    in_vmem = pl.BlockSpec(memory_space=pltpu.VMEM)
    rows_scratch = pltpu.VMEM((length, channels), BF16)
    copies = pltpu.SemaphoreType.DMA((2 * heads,))
    half_scratch = pltpu.VMEM((length, channels // 2), BF16)

    def block_sums(mine):
        return whole_call(
            lambda *refs: block_sum_kernel(mine, *refs), array(F32, heads // 2, size, size),
            [hbm(rates), hbm(keys), hbm(values)], in_specs=[smem, anywhere, anywhere],
            scratch_shapes=[half_scratch, half_scratch, pltpu.SemaphoreType.DMA((heads,))],
        )

    other_sums = swap(block_sums(False))
    own_sums = block_sums(True)
    intra = call(intra_kernel, [smem, tokens, tokens, tokens], tokens, wide, 2 * square, 4 << 20)(
        rates, queries, keys, values
    )
    mine, other = scan_chips(own_sums, other_sums, rates, length, False)
    mixed, stats, state_in = whole_call(
        mixed_kernel, [wide, array(F32, *stats_shape), array(F32, 2 * heads, size // 2, size)],
        [rates, queries, mine, other, intra, gain_row, cotangent], scratch_shapes=[scratch, scratch],
    )
    received = lax.all_to_all(stats, "head", 0, 0)
    grad, back_sums = whole_call(
        lambda *refs: back_sum_kernel(total_channels, *refs),
        [narrow, array(F32, 2 * heads, size // 2 + EXTRA, size)],
        [rates, received, mixed, gain_row, cotangent, queries], scratch_shapes=[scratch, scratch],
    )
    token = array(F32, 8, 128)
    token_spec = pl.BlockSpec((8, 128), lambda h: (0, 0))
    part = pltpu.VMEM((length, channels), F32)
    value_part, first_token = call(
        value_part_kernel, [smem, tokens, tokens, tokens], [tokens, token_spec],
        [part, token], 2 * square, 4 << 20,
    )(rates, queries, keys, grad)
    attended, query_grad, key_part, second_token = call(
        lambda *refs: grads_kernel(total_channels, *refs),
        [smem, stats_spec, tokens, row, tokens, tokens, tokens, tokens, shards],
        [tokens, tokens, tokens, token_spec], [narrow, narrow, part, token], 4 * square, 6 << 20, [scratch],
    )(rates, received, mixed, gain_row, queries, keys, values, grad, state_in)
    back_in = scan_back(back_sums, rates, length, first_token, second_token)
    key_grad, value_grad, gain_grad = whole_call(
        finish_kernel, [narrow, narrow, array(F32, 1, channels)],
        [rates, back_in, keys, values, vmem(key_part), vmem(value_part)],
        out_specs=[anywhere, anywhere, in_vmem], scratch_shapes=[rows_scratch, rows_scratch, copies],
    )
    return attended, query_grad, key_grad, value_grad, gain_grad.reshape(channels)


def solution(mesh):
    placed = (
        P("seq", "head"),
        P("seq", "head"),
        P("seq", "head"),
        P("head"),
        P("head"),
        P("seq", "head"),
    )
    return jax.shard_map(
        body,
        mesh=mesh,
        in_specs=placed,
        out_specs=(
            P("seq", "head"),
            P("seq", "head"),
            P("seq", "head"),
            P("seq", "head"),
            P("head"),
        ),
        check_vma=False,
    )
```

```python
import jax
import jax.numpy as jnp
from jax import lax
from jax.experimental import pallas as pl
from jax.experimental.pallas import tpu as pltpu
from jax.sharding import PartitionSpec as P

epsilon = 1e-06
F32, BF16 = jnp.float32, jnp.bfloat16
GROUP = 8
EXTRA = 8
VMEM_LIMIT = 16 * 1024 * 1024


def dot(a, b, over_a, over_b):
    return lax.dot_general(a, b, (((over_a,), (over_b,)), ((), ())), preferred_element_type=F32)


def split(x):
    high = x.astype(BF16)
    return high, (x - high.astype(F32)).astype(BF16)


def dot_split(a, x, over_a, over_x):
    parts = jnp.concatenate(split(x), axis=1 - over_x)
    both = dot(a, parts, over_a, over_x)
    return both[:, : both.shape[1] // 2] + both[:, both.shape[1] // 2 :]


def rows_of(length, width=128):
    return lax.broadcasted_iota(jnp.int32, (length, width), 0).astype(F32)


def exp_scalar(x):
    return jnp.exp(jnp.full((8, 128), x, F32))[:1]


def head_in_of(rate, length):
    base = jnp.exp(-rate * (rows_of(128) + 1.0))
    return jnp.concatenate([base * exp_scalar(-rate * start) for start in range(0, length, 128)], axis=0)


def tail_out_of(rate, length):
    base = jnp.exp(-rate * (127.0 - rows_of(128)))
    return jnp.concatenate([base * exp_scalar(-rate * (length - 128 - start)) for start in range(0, length, 128)], axis=0)


def tile_weights(rate, half):
    distance = (
        lax.broadcasted_iota(jnp.int32, (half, half), 0) - lax.broadcasted_iota(jnp.int32, (half, half), 1)
    ).astype(F32)
    same = jnp.where(distance >= 0, jnp.exp(-rate * jnp.maximum(distance, 0.0)), 0.0)
    column = jnp.exp(-rate * (rows_of(half) + 1.0))
    row = jnp.exp(-rate * (half - 1.0 - lax.broadcasted_iota(jnp.int32, (8, half), 1).astype(F32)))[:1]
    return same, jnp.concatenate([column] * (half // 128), axis=1) * row


def column(h, size):
    return pl.ds(h * size, size)


def block_sum_kernel(rates_in, keys, values, out, rates, key_rows, value_rows, sums, arrived, sent):
    length = keys.shape[0]
    heads = rates.shape[0]
    size = keys.shape[1] // heads
    copies = []
    for h in range(heads):
        cols = column(h, size)
        copies.append(
            [
                pltpu.make_async_copy(source.at[:, cols], rows.at[:, cols], arrived.at[2 * h + i])
                for i, (source, rows) in enumerate(((values, value_rows), (keys, key_rows)))
            ]
        )
        for copy in copies[-1]:
            copy.start()
        if h == 0:
            fetch = pltpu.make_async_copy(rates_in, rates, arrived.at[2 * heads])
            fetch.start()
    fetch.wait()
    stores = []
    for h in range(heads):
        cols = column(h, size)
        tail = tail_out_of(rates[h], length)
        for copy in copies[h]:
            copy.wait()
        scaled = value_rows[:, cols].astype(F32) * tail
        shards = pl.ds(2 * h, 2)
        sums[shards] = dot_split(key_rows[:, cols], scaled, 0, 0).reshape(2, size // 2, size)
        stores.append(pltpu.make_async_copy(sums.at[shards], out.at[shards], sent.at[h]))
        stores[-1].start()
    for store in stores:
        store.wait()


def intra_kernel(rates, queries, keys, values, out, token):
    rate = rates[pl.program_id(0)]
    half = queries.shape[0] // 2
    same, across = tile_weights(rate, half)
    first, second = pl.ds(0, half), pl.ds(half, half)

    def probs(t, s, weight):
        return (dot(queries[t, :], keys[s, :], 1, 1) * weight).astype(BF16)

    out[first, :] = dot(probs(first, first, same), values[first, :], 1, 0)
    out[second, :] = dot(probs(second, first, across), values[first, :], 1, 0) + dot(
        probs(second, second, same), values[second, :], 1, 0
    )
    token[...] = jnp.zeros_like(token)


def mixed_kernel(rates, queries, state, intra, gain, cotangent, mixed, stats, square, inner):
    length = queries.shape[0]
    heads = rates.shape[0]
    size = queries.shape[1] // heads
    for h in range(heads):
        cols = column(h, size)
        state_in = state[pl.ds(2 * h, 2)].reshape(size, size)
        value = intra[:, cols] + head_in_of(rates[h], length) * dot_split(queries[:, cols], state_in, 1, 0)
        mixed[:, cols] = value
        new_square, new_inner = value * value, cotangent[:, cols].astype(F32) * gain[:, cols] * value
        if h > 0:
            new_square, new_inner = new_square + square[...], new_inner + inner[...]
        square[...] = new_square
        inner[...] = new_inner
    pieces = []
    for ref in (square, inner):
        for start in range(0, length, 128):
            pieces.append(jnp.sum(ref[pl.ds(start, 128), :].T, axis=0, keepdims=True))
    tile = jnp.concatenate(pieces, axis=0)
    stats[...] = jnp.broadcast_to(tile[None], stats.shape)


def token_scales(received, channels, inv_out, coef_out):
    total = jnp.sum(received[...], axis=0)
    chunks = total.shape[0] // 2
    inv = lax.rsqrt(total[:chunks] / channels + epsilon)
    coef = inv * inv * inv * total[chunks:] / channels
    for chunk in range(chunks):
        rows = pl.ds(chunk * 128, 128)
        inv_out[rows, :] = jnp.broadcast_to(inv[chunk : chunk + 1], (128, 128)).T
        if coef_out is not None:
            coef_out[rows, :] = jnp.broadcast_to(coef[chunk : chunk + 1], (128, 128)).T


def back_sum_kernel(
    channels, rates, received, mixed, gain, cotangent, queries, grad_out, sums_out, inv, coef, grad, sums, sent
):
    length = queries.shape[0]
    heads = rates.shape[0]
    size = queries.shape[1] // heads
    token_scales(received, channels, inv, coef)
    stores = []
    for h in range(heads):
        cols = column(h, size)
        shards = pl.ds(2 * h, 2)
        upstream = cotangent[:, cols].astype(F32)
        value = mixed[:, cols]
        mixed_grad = (inv[...] * (upstream * gain[:, cols]) - value * coef[...]).astype(BF16)
        grad[:, cols] = mixed_grad
        scaled = mixed_grad.astype(F32) * head_in_of(rates[h], length)
        sums[shards, pl.ds(0, size // 2), :] = dot_split(queries[:, cols], scaled, 0, 0).reshape(2, size // 2, size)
        gain_grad = jnp.sum(upstream * (value * inv[...]), axis=0, keepdims=True)
        sums[shards, pl.ds(size // 2, EXTRA), :] = jnp.broadcast_to(gain_grad[None], (2, EXTRA, size))
        stores.append(pltpu.make_async_copy(grad.at[:, cols], grad_out.at[:, cols], sent.at[2 * h]))
        stores.append(pltpu.make_async_copy(sums.at[shards], sums_out.at[shards], sent.at[2 * h + 1]))
        stores[-1].start()
        stores[-2].start()
    for store in stores:
        store.wait()


def weighted(a, b, t, s, weight):
    return (dot(a[t, :], b[s, :], 1, 1) * weight).astype(BF16)


def grads_kernel(
    channels, rates, received, mixed, gain, queries, keys, values, grad, state,
    attended, query_grad, key_part, value_part, token, inv,
):
    head = pl.program_id(0)
    rate = rates[head]
    length, size = queries.shape
    half = length // 2

    @pl.when(head == 0)
    def _():
        token_scales(received, channels, inv, None)

    attended[...] = (mixed[...] * inv[...] * gain[...]).astype(BF16)
    same, across = tile_weights(rate, half)
    first, second = pl.ds(0, half), pl.ds(half, half)
    state_part = head_in_of(rate, length) * dot_split(grad[...], state[...].reshape(size, size), 1, 1)
    upper = weighted(grad, values, first, first, same)
    lower = weighted(grad, values, second, first, across)
    final = weighted(grad, values, second, second, same)
    query_grad[first, :] = (dot(upper, keys[first, :], 1, 0) + state_part[:half]).astype(BF16)
    query_grad[second, :] = (
        dot(lower, keys[first, :], 1, 0) + dot(final, keys[second, :], 1, 0) + state_part[half:]
    ).astype(BF16)
    key_part[first, :] = dot(upper, queries[first, :], 0, 0) + dot(lower, queries[second, :], 0, 0)
    key_part[second, :] = dot(final, queries[second, :], 0, 0)
    upper = weighted(queries, keys, first, first, same)
    lower = weighted(queries, keys, second, first, across)
    final = weighted(queries, keys, second, second, same)
    value_part[first, :] = dot(upper, grad[first, :], 0, 0) + dot(lower, grad[second, :], 0, 0)
    value_part[second, :] = dot(final, grad[second, :], 0, 0)
    token[...] = jnp.zeros_like(token)


def finish_kernel(
    rates, back, keys, values, key_part, value_part, key_grad, value_grad, gain_grad, key_rows, value_rows, sent
):
    length = keys.shape[0]
    heads = rates.shape[0]
    size = keys.shape[1] // heads
    half = size // 2
    copies = []
    for h in range(heads):
        cols = column(h, size)
        back_in = back[pl.ds(2 * h, 2), pl.ds(0, half), :].reshape(size, size)
        gain_grad[:, cols] = back[2 * h, pl.ds(half, 1), :]
        tail = tail_out_of(rates[h], length)
        key_rows[:, cols] = (key_part[:, cols] + tail * dot_split(values[:, cols], back_in, 1, 1)).astype(BF16)
        value_rows[:, cols] = (value_part[:, cols] + tail * dot_split(keys[:, cols], back_in, 1, 0)).astype(BF16)
        for i, (rows, target) in enumerate(((key_rows, key_grad), (value_rows, value_grad))):
            copy = pltpu.make_async_copy(rows.at[:, cols], target.at[:, cols], sent.at[2 * h + i])
            copy.start()
            copies.append(copy)
    for copy in copies:
        copy.wait()


def fold_factors(rates, length):
    member = lax.axis_index("seq") % GROUP
    rate = rates[member * rates.shape[0] // GROUP]
    return exp_scalar(-rate * length), exp_scalar(-rate * (length * GROUP))


def totals_kernel(length, rates, parts, token, out):
    factor, _ = fold_factors(rates, length)
    rows = parts.shape[1] - EXTRA
    total = parts[GROUP - 1, :rows]
    for k in range(GROUP - 2, -1, -1):
        total = factor * total + parts[k, :rows]
    extra = sum(parts[k, rows:] for k in range(GROUP))
    for g in range(out.shape[0]):
        out[g, :rows] = total
        out[g, rows:] = extra


def fold_forward_kernel(length, rates, parts, *refs):
    factor, group_factor = fold_factors(rates, length)
    *arrived, out = refs
    carry = arrived[-1][...]
    for ref in arrived[-2::-1]:
        carry = group_factor * carry + ref[...]
    for k in range(GROUP):
        out[k] = carry
        carry = factor * carry + parts[k]


def fold_back_kernel(length, rates, parts, arrived, out):
    factor, group_factor = fold_factors(rates, length)
    rows = parts.shape[1] - EXTRA
    group = lax.axis_index("seq") // GROUP
    carry = jnp.zeros((rows, parts.shape[2]), F32)
    for g in range(arrived.shape[0] - 1, 0, -1):
        carry = jnp.where(group < g, group_factor * carry + arrived[g, :rows], carry)
    extra = sum(arrived[g, rows:] for g in range(arrived.shape[0]))
    for k in range(GROUP - 1, -1, -1):
        out[k, :rows] = carry
        out[k, rows:] = extra
        carry = factor * carry + parts[k, :rows]


def whole_call(kernel, out_shape, operands, in_specs=None, out_specs=None, **rest):
    vmem = pl.BlockSpec(memory_space=pltpu.VMEM)
    if in_specs is None:
        in_specs = [pl.BlockSpec(memory_space=pltpu.SMEM)] + [vmem] * (len(operands) - 1)
    if out_specs is None:
        out_specs = jax.tree.map(lambda _: vmem, out_shape)
    return pl.pallas_call(
        kernel,
        in_specs=in_specs,
        out_specs=out_specs,
        out_shape=out_shape,
        compiler_params=pltpu.CompilerParams(vmem_limit_bytes=VMEM_LIMIT),
        **rest,
    )(*operands)


def scan_forward(x, rates, length, token):
    count = lax.axis_size("seq")
    groups = count // GROUP
    members = [[g * GROUP + j for j in range(GROUP)] for g in range(groups)]
    parts = lax.all_to_all(x, "seq", 0, 0, axis_index_groups=members)
    rate = lax.dynamic_index_in_dim(rates, lax.axis_index("seq") % GROUP * rates.shape[0] // GROUP, 0, False)
    factor = jnp.exp(-rate * length)
    total = parts[0] + token[:1]
    for k in range(1, GROUP):
        total = factor * total + parts[k]
    arrived = [
        lax.ppermute(total, "seq", [(i, i + by * GROUP) for i in range(count - by * GROUP)]) for by in range(1, groups)
    ]
    out = whole_call(lambda *refs: fold_forward_kernel(length, *refs), like(x), [rates, parts, *arrived])
    return lax.all_to_all(out, "seq", 0, 0, axis_index_groups=members)


def scan_back(x, rates, length, token):
    groups = lax.axis_size("seq") // GROUP
    members = [[g * GROUP + j for j in range(GROUP)] for g in range(groups)]
    across = [[g * GROUP + j for g in range(groups)] for j in range(GROUP)]
    parts = lax.all_to_all(x, "seq", 0, 0, axis_index_groups=members)
    totals = whole_call(
        lambda *refs: totals_kernel(length, *refs), jax.ShapeDtypeStruct((groups,) + x.shape[1:], F32),
        [rates, parts, token],
    )
    arrived = lax.all_to_all(totals, "seq", 0, 0, axis_index_groups=across)
    out = whole_call(lambda *refs: fold_back_kernel(length, *refs), like(x), [rates, parts, arrived])
    return lax.all_to_all(out, "seq", 0, 0, axis_index_groups=members)


def like(x):
    return jax.ShapeDtypeStruct(x.shape, x.dtype)


def body(queries, keys, values, rates, gain, cotangent):
    length, channels = queries.shape
    heads = rates.shape[0]
    size = channels // heads
    head_devices = lax.axis_size("head")
    total_channels = channels * head_devices
    gain_row = gain.reshape(1, channels)

    smem = pl.BlockSpec(memory_space=pltpu.SMEM)
    tokens = pl.BlockSpec((length, size), lambda h: (0, h))
    row = pl.BlockSpec((1, size), lambda h: (0, h))
    shards = pl.BlockSpec((2, size // 2, size), lambda h: (h, 0, 0))
    shards_extra = pl.BlockSpec((2, size // 2 + EXTRA, size), lambda h: (h, 0, 0))
    stats_shape = (head_devices, 2 * length // 128, 128)
    stats_spec = pl.BlockSpec(stats_shape, lambda h: (0, 0, 0))
    scratch = pltpu.VMEM((length, size), F32)

    def array(kind, *shape):
        return jax.ShapeDtypeStruct(shape, kind)

    def call(kernel, in_specs, out_specs, out_shape, flops, nbytes, scratches=()):
        return pl.pallas_call(
            kernel,
            grid=(heads,),
            in_specs=in_specs,
            out_specs=out_specs,
            out_shape=out_shape,
            scratch_shapes=list(scratches),
            compiler_params=pltpu.CompilerParams(vmem_limit_bytes=VMEM_LIMIT),
            cost_estimate=pl.CostEstimate(flops=flops, bytes_accessed=nbytes, transcendentals=0),
        )

    square = 2 * heads * length * length * size
    wide = array(F32, length, channels)
    narrow = array(BF16, length, channels)

    hbm = lambda x: pltpu.with_memory_space_constraint(x, pltpu.HBM)
    vmem = lambda x: pltpu.with_memory_space_constraint(x, pltpu.VMEM)
    anywhere = pl.BlockSpec(memory_space=pl.ANY)
    in_vmem = pl.BlockSpec(memory_space=pltpu.VMEM)
    rows_scratch = pltpu.VMEM((length, channels), BF16)
    copies = pltpu.SemaphoreType.DMA((2 * heads,))
    sums_shape = (2 * heads, size // 2, size)
    sums = whole_call(
        block_sum_kernel, pltpu.HBM(sums_shape, F32), [hbm(rates), hbm(keys), hbm(values)],
        in_specs=[anywhere] * 3, out_specs=anywhere,
        scratch_shapes=[
            pltpu.SMEM((heads,), F32), rows_scratch, rows_scratch, pltpu.VMEM(sums_shape, F32),
            pltpu.SemaphoreType.DMA((2 * heads + 1,)), pltpu.SemaphoreType.DMA((heads,)),
        ],
    )
    token = array(F32, 8, 128)
    token_spec = pl.BlockSpec((8, 128), lambda h: (0, 0))
    intra, first_token = call(
        intra_kernel, [smem, tokens, tokens, tokens], [tokens, token_spec], [wide, token], 2 * square, 4 << 20
    )(rates, queries, keys, values)
    state_in = scan_forward(sums, rates, length, first_token)
    mixed, stats = whole_call(
        mixed_kernel, [wide, array(F32, *stats_shape)],
        [rates, queries, state_in, intra, gain_row, cotangent], scratch_shapes=[scratch, scratch],
    )
    received = lax.all_to_all(stats, "head", 0, 0)
    sums_shape = (2 * heads, size // 2 + EXTRA, size)
    grad, back_sums = whole_call(
        lambda *refs: back_sum_kernel(total_channels, *refs),
        [pltpu.HBM((length, channels), BF16), pltpu.HBM(sums_shape, F32)],
        [rates, received, mixed, gain_row, cotangent, queries], out_specs=[anywhere, anywhere],
        scratch_shapes=[scratch, scratch, rows_scratch, pltpu.VMEM(sums_shape, F32), copies],
    )
    part = pltpu.VMEM((length, channels), F32)
    attended, query_grad, key_part, value_part, second_token = call(
        lambda *refs: grads_kernel(total_channels, *refs),
        [smem, stats_spec, tokens, row, tokens, tokens, tokens, tokens, shards],
        [tokens, tokens, tokens, tokens, token_spec], [narrow, narrow, part, part, token],
        6 * square, 6 << 20, [scratch],
    )(rates, received, hbm(mixed), gain_row, queries, keys, values, hbm(grad), state_in)
    back_in = scan_back(back_sums, rates, length, second_token)
    key_grad, value_grad, gain_grad = whole_call(
        finish_kernel, [narrow, narrow, array(F32, 1, channels)],
        [rates, back_in, keys, values, vmem(key_part), vmem(value_part)],
        out_specs=[anywhere, anywhere, in_vmem], scratch_shapes=[rows_scratch, rows_scratch, copies],
    )
    return attended, query_grad, key_grad, value_grad, gain_grad.reshape(channels)


def solution(mesh):
    placed = (
        P("seq", "head"),
        P("seq", "head"),
        P("seq", "head"),
        P("head"),
        P("head"),
        P("seq", "head"),
    )
    return jax.shard_map(
        body,
        mesh=mesh,
        in_specs=placed,
        out_specs=(
            P("seq", "head"),
            P("seq", "head"),
            P("seq", "head"),
            P("seq", "head"),
            P("head"),
        ),
        check_vma=False,
    )
```

```python
import jax
import jax.numpy as jnp
from jax import lax
from jax.experimental import pallas as pl
from jax.experimental.pallas import tpu as pltpu
from jax.sharding import PartitionSpec as P

epsilon = 1e-06
F32, BF16 = jnp.float32, jnp.bfloat16
GROUP = 8
EXTRA = 8
VMEM_LIMIT = 16 * 1024 * 1024


def dot(a, b, over_a, over_b):
    return lax.dot_general(a, b, (((over_a,), (over_b,)), ((), ())), preferred_element_type=F32)


def split(x):
    high = x.astype(BF16)
    return high, (x - high.astype(F32)).astype(BF16)


def dot_split(a, x, over_a, over_x):
    parts = jnp.concatenate(split(x), axis=1 - over_x)
    both = dot(a, parts, over_a, over_x)
    return both[:, : both.shape[1] // 2] + both[:, both.shape[1] // 2 :]


def rows_of(length, width=128):
    return lax.broadcasted_iota(jnp.int32, (length, width), 0).astype(F32)


def head_in_of(rate, length):
    base = jnp.exp(-rate * (rows_of(128) + 1.0))
    return jnp.concatenate([base * jnp.exp(-rate * start) for start in range(0, length, 128)], axis=0)


def tail_out_of(rate, length):
    base = jnp.exp(-rate * (127.0 - rows_of(128)))
    return jnp.concatenate([base * jnp.exp(-rate * (length - 128 - start)) for start in range(0, length, 128)], axis=0)


def tile_weights(rate, half):
    rate = jnp.concatenate([rate] * (half // 128), axis=1)
    distance = (
        lax.broadcasted_iota(jnp.int32, (half, half), 0) - lax.broadcasted_iota(jnp.int32, (half, half), 1)
    ).astype(F32)
    same = jnp.where(distance >= 0, jnp.exp(-rate * jnp.maximum(distance, 0.0)), 0.0)
    column = jnp.exp(-rate * (rows_of(half, half) + 1.0))
    row = jnp.exp(-rate * (half - 1.0 - lax.broadcasted_iota(jnp.int32, (1, half), 1).astype(F32)))
    return same, column * row


def column(h, size):
    return pl.ds(h * size, size)


def block_sum_kernel(rates_in, keys, values, out, rates, key_rows, value_rows, sums, arrived, sent):
    length = keys.shape[0]
    heads = rates.shape[0]
    size = keys.shape[1] // heads
    copies = []
    for h in range(heads):
        cols = column(h, size)
        copies.append(
            [
                pltpu.make_async_copy(source.at[:, cols], rows.at[:, cols], arrived.at[2 * h + i])
                for i, (source, rows) in enumerate(((values, value_rows), (keys, key_rows)))
            ]
        )
        for copy in copies[-1]:
            copy.start()
        if h == 0:
            fetch = pltpu.make_async_copy(rates_in, rates, arrived.at[2 * heads])
            fetch.start()
    fetch.wait()
    stores = []
    for h in range(heads):
        cols = column(h, size)
        tail = tail_out_of(jnp.full((1, size), rates[h], F32), length)
        for copy in copies[h]:
            copy.wait()
        scaled = value_rows[:, cols].astype(F32) * tail
        shards = pl.ds(2 * h, 2)
        sums[shards] = dot_split(key_rows[:, cols], scaled, 0, 0).reshape(2, size // 2, size)
        stores.append(pltpu.make_async_copy(sums.at[shards], out.at[shards], sent.at[h]))
        stores[-1].start()
    for store in stores:
        store.wait()


GAIN, RATE, ZERO = 0, 1, 2


def intra_kernel(rates, gain, queries, keys, values, out, consts):
    rate = jnp.full(gain.shape, rates[pl.program_id(0)], F32)
    consts[...] = jnp.concatenate([gain[...], rate, jnp.zeros((6, rate.shape[1]), F32)], axis=0)
    half = queries.shape[0] // 2
    same, across = tile_weights(rate, half)
    first, second = pl.ds(0, half), pl.ds(half, half)

    def probs(t, s, weight):
        return (dot(queries[t, :], keys[s, :], 1, 1) * weight).astype(BF16)

    out[first, :] = dot(probs(first, first, same), values[first, :], 1, 0)
    out[second, :] = dot(probs(second, first, across), values[first, :], 1, 0) + dot(
        probs(second, second, same), values[second, :], 1, 0
    )


def mixed_kernel(consts, queries, state, intra, cotangent, mixed, stats, square, inner):
    length = queries.shape[0]
    size = 128
    heads = queries.shape[1] // size
    for h in range(heads):
        cols = column(h, size)
        state_in = state[pl.ds(2 * h, 2)].reshape(size, size)
        value = intra[:, cols] + head_in_of(consts[pl.ds(RATE, 1), cols], length) * dot_split(queries[:, cols], state_in, 1, 0)
        mixed[:, cols] = value
        new_square, new_inner = value * value, cotangent[:, cols].astype(F32) * consts[pl.ds(GAIN, 1), cols] * value
        if h > 0:
            new_square, new_inner = new_square + square[...], new_inner + inner[...]
        square[...] = new_square
        inner[...] = new_inner
    pieces = []
    for ref in (square, inner):
        for start in range(0, length, 128):
            pieces.append(jnp.sum(ref[pl.ds(start, 128), :].T, axis=0, keepdims=True))
    tile = jnp.concatenate(pieces, axis=0)
    stats[...] = jnp.broadcast_to(tile[None], stats.shape)


def token_scales(received, channels, inv_out, coef_out):
    total = jnp.sum(received[...], axis=0)
    chunks = total.shape[0] // 2
    inv = lax.rsqrt(total[:chunks] / channels + epsilon)
    coef = inv * inv * inv * total[chunks:] / channels
    for chunk in range(chunks):
        rows = pl.ds(chunk * 128, 128)
        inv_out[rows, :] = jnp.broadcast_to(inv[chunk : chunk + 1], (128, 128)).T
        if coef_out is not None:
            coef_out[rows, :] = jnp.broadcast_to(coef[chunk : chunk + 1], (128, 128)).T


def back_sum_kernel(
    channels, consts, received, mixed, cotangent, queries, grad_out, sums_out, inv, coef, grad, sums, sent
):
    length = queries.shape[0]
    size = 128
    heads = queries.shape[1] // size
    token_scales(received, channels, inv, coef)
    stores = []
    for h in range(heads):
        cols = column(h, size)
        shards = pl.ds(2 * h, 2)
        upstream = cotangent[:, cols].astype(F32)
        value = mixed[:, cols]
        mixed_grad = (inv[...] * (upstream * consts[pl.ds(GAIN, 1), cols]) - value * coef[...]).astype(BF16)
        grad[:, cols] = mixed_grad
        scaled = mixed_grad.astype(F32) * head_in_of(consts[pl.ds(RATE, 1), cols], length)
        sums[shards, pl.ds(0, size // 2), :] = dot_split(queries[:, cols], scaled, 0, 0).reshape(2, size // 2, size)
        gain_grad = jnp.sum(upstream * (value * inv[...]), axis=0, keepdims=True)
        sums[shards, pl.ds(size // 2, EXTRA), :] = jnp.broadcast_to(gain_grad[None], (2, EXTRA, size))
        stores.append(pltpu.make_async_copy(grad.at[:, cols], grad_out.at[:, cols], sent.at[2 * h]))
        stores.append(pltpu.make_async_copy(sums.at[shards], sums_out.at[shards], sent.at[2 * h + 1]))
        stores[-1].start()
        stores[-2].start()
    for store in stores:
        store.wait()


def weighted(a, b, t, s, weight):
    return (dot(a[t, :], b[s, :], 1, 1) * weight).astype(BF16)


def grads_kernel(
    channels, consts, received, mixed, queries, keys, values, grad, state,
    attended, query_grad, key_part, value_part, token, inv,
):
    rate = consts[pl.ds(RATE, 1), :]
    length, size = queries.shape
    half = length // 2

    @pl.when(pl.program_id(0) == 0)
    def _():
        token_scales(received, channels, inv, None)

    attended[...] = (mixed[...] * inv[...] * consts[pl.ds(GAIN, 1), :]).astype(BF16)
    same, across = tile_weights(rate, half)
    first, second = pl.ds(0, half), pl.ds(half, half)
    state_part = head_in_of(rate, length) * dot_split(grad[...], state[...].reshape(size, size), 1, 1)
    upper = weighted(grad, values, first, first, same)
    lower = weighted(grad, values, second, first, across)
    final = weighted(grad, values, second, second, same)
    query_grad[first, :] = (dot(upper, keys[first, :], 1, 0) + state_part[:half]).astype(BF16)
    query_grad[second, :] = (
        dot(lower, keys[first, :], 1, 0) + dot(final, keys[second, :], 1, 0) + state_part[half:]
    ).astype(BF16)
    key_part[first, :] = dot(upper, queries[first, :], 0, 0) + dot(lower, queries[second, :], 0, 0)
    key_part[second, :] = dot(final, queries[second, :], 0, 0)
    upper = weighted(queries, keys, first, first, same)
    lower = weighted(queries, keys, second, first, across)
    final = weighted(queries, keys, second, second, same)
    value_part[first, :] = dot(upper, grad[first, :], 0, 0) + dot(lower, grad[second, :], 0, 0)
    value_part[second, :] = dot(final, grad[second, :], 0, 0)
    token[...] = jnp.zeros_like(token)


def finish_kernel(
    consts, back, keys, values, key_part, value_part, key_grad, value_grad, gain_grad, key_rows, value_rows, sent
):
    length = keys.shape[0]
    size = 128
    heads = keys.shape[1] // size
    half = size // 2
    copies = []
    for h in range(heads):
        cols = column(h, size)
        back_in = back[pl.ds(2 * h, 2), pl.ds(0, half), :].reshape(size, size)
        gain_grad[:, cols] = back[2 * h, pl.ds(half, 1), :]
        tail = tail_out_of(consts[pl.ds(RATE, 1), cols], length)
        key_rows[:, cols] = (key_part[:, cols] + tail * dot_split(values[:, cols], back_in, 1, 1)).astype(BF16)
        value_rows[:, cols] = (value_part[:, cols] + tail * dot_split(keys[:, cols], back_in, 1, 0)).astype(BF16)
        for i, (rows, target) in enumerate(((key_rows, key_grad), (value_rows, value_grad))):
            copy = pltpu.make_async_copy(rows.at[:, cols], target.at[:, cols], sent.at[2 * h + i])
            copy.start()
            copies.append(copy)
    for copy in copies:
        copy.wait()


def fold_factors(consts, length):
    member = lax.axis_index("seq") % GROUP
    head = member * (consts.shape[1] // 128) // GROUP
    rate = consts[pl.ds(RATE, 1), pl.ds(pl.multiple_of(head * 128, 128), 128)]
    return jnp.exp(-rate * length), jnp.exp(-rate * (length * GROUP))


def totals_kernel(length, consts, parts, token, out):
    factor, _ = fold_factors(consts, length)
    rows = parts.shape[1] - EXTRA
    total = parts[GROUP - 1, :rows]
    for k in range(GROUP - 2, -1, -1):
        total = factor * total + parts[k, :rows]
    out[:rows] = total
    out[rows:] = sum(parts[k, rows:] for k in range(GROUP))


def fold_forward_kernel(length, consts, parts, *refs):
    factor, group_factor = fold_factors(consts, length)
    *arrived, out = refs
    carry = arrived[-1][...]
    for ref in arrived[-2::-1]:
        carry = group_factor * carry + ref[...]
    for k in range(GROUP):
        out[k] = carry
        carry = factor * carry + parts[k]


def fold_back_kernel(length, consts, parts, arrived, out):
    factor, group_factor = fold_factors(consts, length)
    rows = parts.shape[1] - EXTRA
    group = lax.axis_index("seq") // GROUP
    carry = jnp.zeros((rows, parts.shape[2]), F32)
    for g in range(arrived.shape[0] - 1, 0, -1):
        carry = jnp.where(group < g, group_factor * carry + arrived[g, :rows], carry)
    extra = sum(arrived[g, rows:] for g in range(arrived.shape[0]))
    for k in range(GROUP - 1, -1, -1):
        out[k, :rows] = carry
        out[k, rows:] = extra
        carry = factor * carry + parts[k, :rows]


def whole_call(kernel, out_shape, operands, in_specs=None, out_specs=None, **rest):
    vmem = pl.BlockSpec(memory_space=pltpu.VMEM)
    if in_specs is None:
        in_specs = [vmem] * len(operands)
    if out_specs is None:
        out_specs = jax.tree.map(lambda _: vmem, out_shape)
    return pl.pallas_call(
        kernel,
        in_specs=in_specs,
        out_specs=out_specs,
        out_shape=out_shape,
        compiler_params=pltpu.CompilerParams(vmem_limit_bytes=VMEM_LIMIT),
        **rest,
    )(*operands)


def scan_forward(x, rates, consts, length):
    count = lax.axis_size("seq")
    groups = count // GROUP
    members = [[g * GROUP + j for j in range(GROUP)] for g in range(groups)]
    parts = lax.all_to_all(x, "seq", 0, 0, axis_index_groups=members)
    rate = lax.dynamic_index_in_dim(rates, lax.axis_index("seq") % GROUP * rates.shape[0] // GROUP, 0, False)
    factor = jnp.exp(-rate * length)
    total = parts[0] + consts[ZERO : ZERO + 1, :128]
    for k in range(1, GROUP):
        total = factor * total + parts[k]
    arrived = [
        lax.ppermute(total, "seq", [(i, i + by * GROUP) for i in range(count - by * GROUP)]) for by in range(1, groups)
    ]
    out = whole_call(lambda *refs: fold_forward_kernel(length, *refs), like(x), [consts, parts, *arrived])
    return lax.all_to_all(out, "seq", 0, 0, axis_index_groups=members)


def scan_back(x, consts, length, token):
    groups = lax.axis_size("seq") // GROUP
    members = [[g * GROUP + j for j in range(GROUP)] for g in range(groups)]
    across = [[g * GROUP + j for g in range(groups)] for j in range(GROUP)]
    parts = lax.all_to_all(x, "seq", 0, 0, axis_index_groups=members)
    totals = whole_call(
        lambda *refs: totals_kernel(length, *refs), jax.ShapeDtypeStruct(x.shape[1:], F32),
        [consts, parts, token],
    )
    arrived = lax.all_gather(totals, "seq", axis_index_groups=across)
    out = whole_call(lambda *refs: fold_back_kernel(length, *refs), like(x), [consts, parts, arrived])
    return lax.all_to_all(out, "seq", 0, 0, axis_index_groups=members)


def like(x):
    return jax.ShapeDtypeStruct(x.shape, x.dtype)


def body(queries, keys, values, rates, gain, cotangent):
    length, channels = queries.shape
    heads = rates.shape[0]
    size = channels // heads
    head_devices = lax.axis_size("head")
    total_channels = channels * head_devices

    smem = pl.BlockSpec(memory_space=pltpu.SMEM)
    tokens = pl.BlockSpec((length, size), lambda h: (0, h))
    row = pl.BlockSpec((1, size), lambda h: (0, h))
    shards = pl.BlockSpec((2, size // 2, size), lambda h: (h, 0, 0))
    shards_extra = pl.BlockSpec((2, size // 2 + EXTRA, size), lambda h: (h, 0, 0))
    stats_shape = (head_devices, 2 * length // 128, 128)
    stats_spec = pl.BlockSpec(stats_shape, lambda h: (0, 0, 0))
    scratch = pltpu.VMEM((length, size), F32)

    def array(kind, *shape):
        return jax.ShapeDtypeStruct(shape, kind)

    def call(kernel, in_specs, out_specs, out_shape, flops, nbytes, scratches=()):
        return pl.pallas_call(
            kernel,
            grid=(heads,),
            in_specs=in_specs,
            out_specs=out_specs,
            out_shape=out_shape,
            scratch_shapes=list(scratches),
            compiler_params=pltpu.CompilerParams(vmem_limit_bytes=VMEM_LIMIT),
            cost_estimate=pl.CostEstimate(flops=flops, bytes_accessed=nbytes, transcendentals=0),
        )

    square = 2 * heads * length * length * size
    wide = array(F32, length, channels)
    narrow = array(BF16, length, channels)

    hbm = lambda x: pltpu.with_memory_space_constraint(x, pltpu.HBM)
    vmem = lambda x: pltpu.with_memory_space_constraint(x, pltpu.VMEM)
    anywhere = pl.BlockSpec(memory_space=pl.ANY)
    in_vmem = pl.BlockSpec(memory_space=pltpu.VMEM)
    rows_scratch = pltpu.VMEM((length, channels), BF16)
    copies = pltpu.SemaphoreType.DMA((2 * heads,))
    sums_shape = (2 * heads, size // 2, size)
    sums = whole_call(
        block_sum_kernel, pltpu.HBM(sums_shape, F32), [hbm(rates), hbm(keys), hbm(values)],
        in_specs=[anywhere] * 3, out_specs=anywhere,
        scratch_shapes=[
            pltpu.SMEM((heads,), F32), rows_scratch, rows_scratch, pltpu.VMEM(sums_shape, F32),
            pltpu.SemaphoreType.DMA((2 * heads + 1,)), pltpu.SemaphoreType.DMA((heads,)),
        ],
    )
    consts_spec = pl.BlockSpec((8, size), lambda h: (0, h))
    intra, consts = call(
        intra_kernel, [smem, row, tokens, tokens, tokens], [tokens, consts_spec],
        [wide, array(F32, 8, channels)], 2 * square, 4 << 20,
    )(rates, gain.reshape(1, channels), queries, keys, values)
    state_in = scan_forward(sums, rates, consts, length)
    mixed, stats = whole_call(
        mixed_kernel, [wide, array(F32, *stats_shape)],
        [consts, queries, state_in, intra, cotangent], scratch_shapes=[scratch, scratch],
    )
    received = lax.all_to_all(stats, "head", 0, 0)
    sums_shape = (2 * heads, size // 2 + EXTRA, size)
    grad, back_sums = whole_call(
        lambda *refs: back_sum_kernel(total_channels, *refs),
        [pltpu.HBM((length, channels), BF16), pltpu.HBM(sums_shape, F32)],
        [consts, received, mixed, cotangent, queries], out_specs=[anywhere, anywhere],
        scratch_shapes=[scratch, scratch, rows_scratch, pltpu.VMEM(sums_shape, F32), copies],
    )
    part = pltpu.VMEM((length, channels), F32)
    attended, query_grad, key_part, value_part, token = call(
        lambda *refs: grads_kernel(total_channels, *refs),
        [consts_spec, stats_spec, tokens, tokens, tokens, tokens, tokens, shards],
        [tokens, tokens, tokens, tokens, pl.BlockSpec((8, 128), lambda h: (0, 0))],
        [narrow, narrow, part, part, array(F32, 8, 128)],
        6 * square, 6 << 20, [scratch],
    )(consts, received, hbm(mixed), queries, keys, values, hbm(grad), state_in)
    back_in = scan_back(back_sums, consts, length, token)
    key_grad, value_grad, gain_grad = whole_call(
        finish_kernel, [narrow, narrow, array(F32, 1, channels)],
        [consts, back_in, keys, values, vmem(key_part), vmem(value_part)],
        out_specs=[anywhere, anywhere, in_vmem], scratch_shapes=[rows_scratch, rows_scratch, copies],
    )
    return attended, query_grad, key_grad, value_grad, gain_grad.reshape(channels)


def solution(mesh):
    placed = (
        P("seq", "head"),
        P("seq", "head"),
        P("seq", "head"),
        P("head"),
        P("head"),
        P("seq", "head"),
    )
    return jax.shard_map(
        body,
        mesh=mesh,
        in_specs=placed,
        out_specs=(
            P("seq", "head"),
            P("seq", "head"),
            P("seq", "head"),
            P("seq", "head"),
            P("head"),
        ),
        check_vma=False,
    )
```

```python
import jax
import jax.numpy as jnp
from jax import lax
from jax.experimental import pallas as pl
from jax.experimental.pallas import tpu as pltpu
from jax.sharding import PartitionSpec as P

epsilon = 1e-06
F32, BF16 = jnp.float32, jnp.bfloat16
GROUP = 8
EXTRA = 8
VMEM_LIMIT = 16 * 1024 * 1024


def dot(a, b, over_a, over_b):
    return lax.dot_general(a, b, (((over_a,), (over_b,)), ((), ())), preferred_element_type=F32)


def split(x):
    high = x.astype(BF16)
    return high, (x - high.astype(F32)).astype(BF16)


def dot_split(a, x, over_a, over_x):
    parts = jnp.concatenate(split(x), axis=1 - over_x)
    both = dot(a, parts, over_a, over_x)
    return both[:, : both.shape[1] // 2] + both[:, both.shape[1] // 2 :]


def rows_of(length, width=128):
    return lax.broadcasted_iota(jnp.int32, (length, width), 0).astype(F32)


def head_in_of(rate, length):
    base = jnp.exp(-rate * (rows_of(128) + 1.0))
    return jnp.concatenate([base * jnp.exp(-rate * start) for start in range(0, length, 128)], axis=0)


def tail_out_of(rate, length):
    base = jnp.exp(-rate * (127.0 - rows_of(128)))
    return jnp.concatenate([base * jnp.exp(-rate * (length - 128 - start)) for start in range(0, length, 128)], axis=0)


def tile_weights(rate, half):
    rate = jnp.concatenate([rate] * (half // 128), axis=1)
    distance = (
        lax.broadcasted_iota(jnp.int32, (half, half), 0) - lax.broadcasted_iota(jnp.int32, (half, half), 1)
    ).astype(F32)
    same = jnp.where(distance >= 0, jnp.exp(-rate * jnp.maximum(distance, 0.0)), 0.0)
    column = jnp.exp(-rate * (rows_of(half, half) + 1.0))
    row = jnp.exp(-rate * (half - 1.0 - lax.broadcasted_iota(jnp.int32, (1, half), 1).astype(F32)))
    return same, column * row


def column(h, size):
    return pl.ds(h * size, size)


def block_sum_kernel(rates_in, keys, values, out, rates, key_rows, value_rows, sums, arrived, sent):
    length = keys.shape[0]
    heads = rates.shape[0]
    size = keys.shape[1] // heads
    copies = []
    for h in range(heads):
        cols = column(h, size)
        copies.append(
            [
                pltpu.make_async_copy(source.at[:, cols], rows.at[:, cols], arrived.at[2 * h + i])
                for i, (source, rows) in enumerate(((values, value_rows), (keys, key_rows)))
            ]
        )
        for copy in copies[-1]:
            copy.start()
        if h == 0:
            fetch = pltpu.make_async_copy(rates_in, rates, arrived.at[2 * heads])
            fetch.start()
    fetch.wait()
    stores = []
    for h in range(heads):
        cols = column(h, size)
        tail = tail_out_of(jnp.full((1, size), rates[h], F32), length)
        for copy in copies[h]:
            copy.wait()
        scaled = value_rows[:, cols].astype(F32) * tail
        shards = pl.ds(2 * h, 2)
        sums[shards] = dot_split(key_rows[:, cols], scaled, 0, 0).reshape(2, size // 2, size)
        stores.append(pltpu.make_async_copy(sums.at[shards], out.at[shards], sent.at[h]))
        stores[-1].start()
    for store in stores:
        store.wait()


GAIN, RATE = 0, 1


def weighted(a, b, t, s, weight):
    return (dot(a[t, :], b[s, :], 1, 1) * weight).astype(BF16)


def intra_kernel(rates, gain, queries, keys, values, out, consts):
    length = queries.shape[0]
    size = 128
    half = length // 2
    first, second = pl.ds(0, half), pl.ds(half, half)
    for h in range(queries.shape[1] // size):
        cols = column(h, size)
        rate = jnp.full((1, size), rates[h], F32)
        consts[:, cols] = jnp.concatenate([gain[:, cols], rate, jnp.zeros((6, size), F32)], axis=0)
        same, across = tile_weights(rate, half)
        q, k, v = (ref.at[:, cols] for ref in (queries, keys, values))
        out[first, cols] = dot(weighted(q, k, first, first, same), v[first, :], 1, 0)
        out[second, cols] = dot(weighted(q, k, second, first, across), v[first, :], 1, 0) + dot(
            weighted(q, k, second, second, same), v[second, :], 1, 0
        )


def mixed_kernel(consts, queries, state, intra, cotangent, mixed, stats, square, inner):
    length = queries.shape[0]
    size = 128
    heads = queries.shape[1] // size
    for h in range(heads):
        cols = column(h, size)
        state_in = state[pl.ds(2 * h, 2)].reshape(size, size)
        value = intra[:, cols] + head_in_of(consts[pl.ds(RATE, 1), cols], length) * dot_split(queries[:, cols], state_in, 1, 0)
        mixed[:, cols] = value
        new_square, new_inner = value * value, cotangent[:, cols].astype(F32) * consts[pl.ds(GAIN, 1), cols] * value
        if h > 0:
            new_square, new_inner = new_square + square[...], new_inner + inner[...]
        square[...] = new_square
        inner[...] = new_inner
    pieces = []
    for ref in (square, inner):
        for start in range(0, length, 128):
            pieces.append(jnp.sum(ref[pl.ds(start, 128), :].T, axis=0, keepdims=True))
    tile = jnp.concatenate(pieces, axis=0)
    stats[...] = jnp.broadcast_to(tile[None], stats.shape)


def token_scales(received, channels, inv_out, coef_out):
    total = jnp.sum(received[...], axis=0)
    chunks = total.shape[0] // 2
    inv = lax.rsqrt(total[:chunks] / channels + epsilon)
    coef = inv * inv * inv * total[chunks:] / channels
    for chunk in range(chunks):
        rows = pl.ds(chunk * 128, 128)
        inv_out[rows, :] = jnp.broadcast_to(inv[chunk : chunk + 1], (128, 128)).T
        if coef_out is not None:
            coef_out[rows, :] = jnp.broadcast_to(coef[chunk : chunk + 1], (128, 128)).T


def back_sum_kernel(
    channels, consts, received, mixed, cotangent, queries, grad_out, sums_out, inv, coef, grad, sums, sent
):
    length = queries.shape[0]
    size = 128
    heads = queries.shape[1] // size
    token_scales(received, channels, inv, coef)
    stores = []
    for h in range(heads):
        cols = column(h, size)
        shards = pl.ds(2 * h, 2)
        upstream = cotangent[:, cols].astype(F32)
        value = mixed[:, cols]
        mixed_grad = (inv[...] * (upstream * consts[pl.ds(GAIN, 1), cols]) - value * coef[...]).astype(BF16)
        grad[:, cols] = mixed_grad
        scaled = mixed_grad.astype(F32) * head_in_of(consts[pl.ds(RATE, 1), cols], length)
        sums[shards, pl.ds(0, size // 2), :] = dot_split(queries[:, cols], scaled, 0, 0).reshape(2, size // 2, size)
        gain_grad = jnp.sum(upstream * (value * inv[...]), axis=0, keepdims=True)
        sums[shards, pl.ds(size // 2, EXTRA), :] = jnp.broadcast_to(gain_grad[None], (2, EXTRA, size))
        stores.append(pltpu.make_async_copy(grad.at[:, cols], grad_out.at[:, cols], sent.at[2 * h]))
        stores.append(pltpu.make_async_copy(sums.at[shards], sums_out.at[shards], sent.at[2 * h + 1]))
        stores[-1].start()
        stores[-2].start()
    for store in stores:
        store.wait()


def grads_kernel(
    channels, consts, received, mixed_in, queries, keys, values, grad_in, state,
    attended_out, query_out, key_part, value_part, token,
    inv, mixed, grad, attended, query_grad, arrived, sent,
):
    length = queries.shape[0]
    size = 128
    heads = queries.shape[1] // size
    half = length // 2
    first, second = pl.ds(0, half), pl.ds(half, half)
    copies, stores = [], []
    for h in range(heads):
        cols = column(h, size)
        copies.append(
            [
                pltpu.make_async_copy(source.at[:, cols], rows.at[:, cols], arrived.at[2 * h + i])
                for i, (source, rows) in enumerate(((grad_in, grad), (mixed_in, mixed)))
            ]
        )
        for copy in copies[-1]:
            copy.start()
    token[...] = jnp.zeros_like(token)
    token_scales(received, channels, inv, None)
    for h in range(heads):
        cols = column(h, size)
        rate = consts[pl.ds(RATE, 1), cols]
        same, across = tile_weights(rate, half)
        q, k, v, g = (ref.at[:, cols] for ref in (queries, keys, values, grad))
        for copy in copies[h]:
            copy.wait()
        attended[:, cols] = (mixed[:, cols] * inv[...] * consts[pl.ds(GAIN, 1), cols]).astype(BF16)
        state_in = state[pl.ds(2 * h, 2)].reshape(size, size)
        state_part = head_in_of(rate, length) * dot_split(g[...], state_in, 1, 1)
        upper = weighted(g, v, first, first, same)
        lower = weighted(g, v, second, first, across)
        final = weighted(g, v, second, second, same)
        query_grad[first, cols] = (dot(upper, k[first, :], 1, 0) + state_part[:half]).astype(BF16)
        query_grad[second, cols] = (
            dot(lower, k[first, :], 1, 0) + dot(final, k[second, :], 1, 0) + state_part[half:]
        ).astype(BF16)
        for i, (rows, target) in enumerate(((attended, attended_out), (query_grad, query_out))):
            stores.append(pltpu.make_async_copy(rows.at[:, cols], target.at[:, cols], sent.at[2 * h + i]))
            stores[-1].start()
        key_part[first, cols] = dot(upper, q[first, :], 0, 0) + dot(lower, q[second, :], 0, 0)
        key_part[second, cols] = dot(final, q[second, :], 0, 0)
        upper = weighted(q, k, first, first, same)
        lower = weighted(q, k, second, first, across)
        final = weighted(q, k, second, second, same)
        value_part[first, cols] = dot(upper, g[first, :], 0, 0) + dot(lower, g[second, :], 0, 0)
        value_part[second, cols] = dot(final, g[second, :], 0, 0)
    for store in stores:
        store.wait()


def finish_kernel(
    consts, back, keys, values, key_part, value_part, key_grad, value_grad, gain_grad, key_rows, value_rows, sent
):
    length = keys.shape[0]
    size = 128
    heads = keys.shape[1] // size
    half = size // 2
    copies = []
    for h in range(heads):
        cols = column(h, size)
        back_in = back[pl.ds(2 * h, 2), pl.ds(0, half), :].reshape(size, size)
        gain_grad[:, cols] = back[2 * h, pl.ds(half, 1), :]
        tail = tail_out_of(consts[pl.ds(RATE, 1), cols], length)
        key_rows[:, cols] = (key_part[:, cols] + tail * dot_split(values[:, cols], back_in, 1, 1)).astype(BF16)
        value_rows[:, cols] = (value_part[:, cols] + tail * dot_split(keys[:, cols], back_in, 1, 0)).astype(BF16)
        for i, (rows, target) in enumerate(((key_rows, key_grad), (value_rows, value_grad))):
            copy = pltpu.make_async_copy(rows.at[:, cols], target.at[:, cols], sent.at[2 * h + i])
            copy.start()
            copies.append(copy)
    for copy in copies:
        copy.wait()


def fold_factors(consts, length):
    member = lax.axis_index("seq") % GROUP
    head = member * (consts.shape[1] // 128) // GROUP
    rate = consts[pl.ds(RATE, 1), pl.ds(pl.multiple_of(head * 128, 128), 128)]
    return jnp.exp(-rate * length), jnp.exp(-rate * (length * GROUP))


def totals_kernel(length, consts, parts, token, out):
    factor, _ = fold_factors(consts, length)
    rows = parts.shape[1] - EXTRA
    total = parts[GROUP - 1, :rows]
    for k in range(GROUP - 2, -1, -1):
        total = factor * total + parts[k, :rows]
    out[:rows] = total
    out[rows:] = sum(parts[k, rows:] for k in range(GROUP))


def forward_totals_kernel(length, consts, parts, out):
    factor, _ = fold_factors(consts, length)
    total = parts[0]
    for k in range(1, GROUP):
        total = factor * total + parts[k]
    out[...] = total


def join_kernel(length, consts, total, before, out):
    _, group_factor = fold_factors(consts, length)
    out[...] = total[...] + group_factor * before[...]


def fold_forward_kernel(length, consts, parts, nearest, near, far, out):
    factor, group_factor = fold_factors(consts, length)
    carry = nearest[...] + near[...] + group_factor * far[...]
    for k in range(GROUP):
        out[k] = carry
        carry = factor * carry + parts[k]


def fold_back_kernel(length, consts, parts, arrived, out):
    factor, group_factor = fold_factors(consts, length)
    rows = parts.shape[1] - EXTRA
    group = lax.axis_index("seq") // GROUP
    carry = jnp.zeros((rows, parts.shape[2]), F32)
    for g in range(arrived.shape[0] - 1, 0, -1):
        carry = jnp.where(group < g, group_factor * carry + arrived[g, :rows], carry)
    extra = sum(arrived[g, rows:] for g in range(arrived.shape[0]))
    for k in range(GROUP - 1, -1, -1):
        out[k, :rows] = carry
        out[k, rows:] = extra
        carry = factor * carry + parts[k, :rows]


def whole_call(kernel, out_shape, operands, in_specs=None, out_specs=None, **rest):
    vmem = pl.BlockSpec(memory_space=pltpu.VMEM)
    if in_specs is None:
        in_specs = [vmem] * len(operands)
    if out_specs is None:
        out_specs = jax.tree.map(lambda _: vmem, out_shape)
    return pl.pallas_call(
        kernel,
        in_specs=in_specs,
        out_specs=out_specs,
        out_shape=out_shape,
        compiler_params=pltpu.CompilerParams(vmem_limit_bytes=VMEM_LIMIT),
        **rest,
    )(*operands)


def send(x, pairs):
    return lax.ppermute(x, "seq", [(a * GROUP + j, b * GROUP + j) for a, b in pairs for j in range(GROUP)])


def scan_forward(x, consts, length):
    groups = lax.axis_size("seq") // GROUP
    members = [[g * GROUP + j for j in range(GROUP)] for g in range(groups)]
    parts = lax.all_to_all(x, "seq", 0, 0, axis_index_groups=members)
    one = jax.ShapeDtypeStruct(x.shape[1:], F32)
    total = whole_call(lambda *refs: forward_totals_kernel(length, *refs), one, [consts, parts])
    nearest = send(total, [(0, 1)])
    total = whole_call(lambda *refs: join_kernel(length, *refs), one, [consts, total, nearest])
    far = send(total, [(1, 3)])
    near = send(total, [(1, 2), (2, 3)])
    out = whole_call(lambda *refs: fold_forward_kernel(length, *refs), like(x), [consts, parts, nearest, near, far])
    return lax.all_to_all(out, "seq", 0, 0, axis_index_groups=members)


def scan_back(x, consts, length, token):
    groups = lax.axis_size("seq") // GROUP
    members = [[g * GROUP + j for j in range(GROUP)] for g in range(groups)]
    across = [[g * GROUP + j for g in range(groups)] for j in range(GROUP)]
    parts = lax.all_to_all(x, "seq", 0, 0, axis_index_groups=members)
    totals = whole_call(
        lambda *refs: totals_kernel(length, *refs), jax.ShapeDtypeStruct(x.shape[1:], F32),
        [consts, parts, token],
    )
    arrived = lax.all_gather(totals, "seq", axis_index_groups=across)
    out = whole_call(lambda *refs: fold_back_kernel(length, *refs), like(x), [consts, parts, arrived])
    return lax.all_to_all(out, "seq", 0, 0, axis_index_groups=members)


def like(x):
    return jax.ShapeDtypeStruct(x.shape, x.dtype)


def body(queries, keys, values, rates, gain, cotangent):
    length, channels = queries.shape
    heads = rates.shape[0]
    size = channels // heads
    head_devices = lax.axis_size("head")
    total_channels = channels * head_devices

    smem = pl.BlockSpec(memory_space=pltpu.SMEM)
    stats_shape = (head_devices, 2 * length // 128, 128)
    scratch = pltpu.VMEM((length, size), F32)

    def array(kind, *shape):
        return jax.ShapeDtypeStruct(shape, kind)

    square = 2 * heads * length * length * size
    wide = array(F32, length, channels)
    narrow = array(BF16, length, channels)

    hbm = lambda x: pltpu.with_memory_space_constraint(x, pltpu.HBM)
    vmem = lambda x: pltpu.with_memory_space_constraint(x, pltpu.VMEM)
    anywhere = pl.BlockSpec(memory_space=pl.ANY)
    in_vmem = pl.BlockSpec(memory_space=pltpu.VMEM)
    rows_scratch = pltpu.VMEM((length, channels), BF16)
    copies = pltpu.SemaphoreType.DMA((2 * heads,))
    sums_shape = (2 * heads, size // 2, size)
    sums = whole_call(
        block_sum_kernel, pltpu.HBM(sums_shape, F32), [hbm(rates), hbm(keys), hbm(values)],
        in_specs=[anywhere] * 3, out_specs=anywhere,
        scratch_shapes=[
            pltpu.SMEM((heads,), F32), rows_scratch, rows_scratch, pltpu.VMEM(sums_shape, F32),
            pltpu.SemaphoreType.DMA((2 * heads + 1,)), pltpu.SemaphoreType.DMA((heads,)),
        ],
    )
    def cost(flops):
        return pl.CostEstimate(flops=flops, bytes_accessed=6 << 20, transcendentals=0)

    intra, consts = whole_call(
        intra_kernel, [wide, array(F32, 8, channels)], [rates, gain.reshape(1, channels), queries, keys, values],
        in_specs=[smem] + [in_vmem] * 4, cost_estimate=cost(2 * square),
    )
    state_in = scan_forward(sums, consts, length)
    mixed, stats = whole_call(
        mixed_kernel, [wide, array(F32, *stats_shape)],
        [consts, queries, state_in, intra, cotangent], scratch_shapes=[scratch, scratch],
    )
    received = lax.all_to_all(stats, "head", 0, 0)
    sums_shape = (2 * heads, size // 2 + EXTRA, size)
    grad, back_sums = whole_call(
        lambda *refs: back_sum_kernel(total_channels, *refs),
        [pltpu.HBM((length, channels), BF16), pltpu.HBM(sums_shape, F32)],
        [consts, received, mixed, cotangent, queries], out_specs=[anywhere, anywhere],
        scratch_shapes=[scratch, scratch, rows_scratch, pltpu.VMEM(sums_shape, F32), copies],
    )
    part = pltpu.VMEM((length, channels), F32)
    attended, query_grad, key_part, value_part, token = whole_call(
        lambda *refs: grads_kernel(total_channels, *refs), [narrow, narrow, part, part, array(F32, 8, 128)],
        [consts, received, hbm(mixed), queries, keys, values, hbm(grad), state_in],
        in_specs=[in_vmem, in_vmem, anywhere, in_vmem, in_vmem, in_vmem, anywhere, in_vmem],
        out_specs=[anywhere, anywhere, in_vmem, in_vmem, in_vmem],
        scratch_shapes=[scratch, pltpu.VMEM((length, channels), F32), rows_scratch, rows_scratch, rows_scratch, copies, copies],
        cost_estimate=cost(6 * square),
    )
    back_in = scan_back(back_sums, consts, length, token)
    key_grad, value_grad, gain_grad = whole_call(
        finish_kernel, [narrow, narrow, array(F32, 1, channels)],
        [consts, back_in, keys, values, vmem(key_part), vmem(value_part)],
        out_specs=[anywhere, anywhere, in_vmem], scratch_shapes=[rows_scratch, rows_scratch, copies],
    )
    return attended, query_grad, key_grad, value_grad, gain_grad.reshape(channels)


def solution(mesh):
    placed = (
        P("seq", "head"),
        P("seq", "head"),
        P("seq", "head"),
        P("head"),
        P("head"),
        P("seq", "head"),
    )
    return jax.shard_map(
        body,
        mesh=mesh,
        in_specs=placed,
        out_specs=(
            P("seq", "head"),
            P("seq", "head"),
            P("seq", "head"),
            P("seq", "head"),
            P("head"),
        ),
        check_vma=False,
    )
```

```python
import jax
import jax.numpy as jnp
from jax import lax
from jax.experimental import pallas as pl
from jax.experimental.pallas import tpu as pltpu
from jax.sharding import PartitionSpec as P

epsilon = 1e-06
F32, BF16 = jnp.float32, jnp.bfloat16
SIZE = 128
CHIPS = 4
EXTRA = 8
GAIN, RATE = 0, 1
VMEM_LIMIT = 16 * 1024 * 1024


def dot(a, b, over_a, over_b):
    return lax.dot_general(a, b, (((over_a,), (over_b,)), ((), ())), preferred_element_type=F32)


def dot_split(a, x, over_a, over_x):
    high = x.astype(BF16)
    low = (x - high.astype(F32)).astype(BF16)
    both = dot(a, jnp.concatenate([high, low], axis=1 - over_x), over_a, over_x)
    return both[:, : both.shape[1] // 2] + both[:, both.shape[1] // 2 :]


def rows_of(length):
    return lax.broadcasted_iota(jnp.int32, (length, SIZE), 0).astype(F32)


def lanes_of():
    return lax.broadcasted_iota(jnp.int32, (1, SIZE), 1).astype(F32)


def head_in_of(rate, length):
    base = jnp.exp(-rate * (rows_of(SIZE) + 1.0))
    return jnp.concatenate([base * jnp.exp(-rate * start) for start in range(0, length, SIZE)], axis=0)


def tail_out_of(rate, length):
    base = jnp.exp(-rate * (SIZE - 1.0 - rows_of(SIZE)))
    return jnp.concatenate([base * jnp.exp(-rate * (length - SIZE - start)) for start in range(0, length, SIZE)], axis=0)


def tile_weights(rate, turned):
    rows, lanes = rows_of(SIZE), lanes_of()
    distance = lanes - rows if turned else rows - lanes
    near = jnp.where(distance >= 0, jnp.exp(-rate * jnp.maximum(distance, 0.0)), 0.0)
    if turned:
        far = jnp.exp(-rate * (SIZE - 1.0 - rows)) * jnp.exp(-rate * (lanes + 1.0))
    else:
        far = jnp.exp(-rate * (rows + 1.0)) * jnp.exp(-rate * (SIZE - 1.0 - lanes))
    step = jnp.exp(-rate * SIZE)
    farther = far * step
    farthest = farther * step
    none = jnp.zeros_like(near)

    def square(a, b, c, d):
        return jnp.concatenate([jnp.concatenate([a, b], axis=1), jnp.concatenate([c, d], axis=1)], axis=0)

    if turned:
        return square(near, far, none, near), square(farther, farthest, far, farther)
    return square(near, none, far, near), square(farther, far, farthest, farther)


def weighted(a, b, rows_a, rows_b, weight):
    return (dot(a[rows_a, :], b[rows_b, :], 1, 1) * weight).astype(BF16)


def column(h):
    return pl.ds(h * SIZE, SIZE)


def heads_of(mine, heads):
    core = lax.axis_index("seq") % 2
    start = (core if mine else 1 - core) * (heads // 2)
    return [pl.ds(pl.multiple_of((start + slot) * SIZE, SIZE), SIZE) for slot in range(heads // 2)]


def first_sums_kernel(
    rates_in, gain_in, keys, values, out, consts, rates, gain, key_rows, value_rows, arrived
):
    length = keys.shape[0]
    heads = rates.shape[0]
    copies = []
    for slot, cols in enumerate(heads_of(False, heads)):
        copies.append(
            [
                pltpu.make_async_copy(source.at[:, cols], rows.at[:, column(slot)], arrived.at[2 * slot + i])
                for i, (source, rows) in enumerate(((values, value_rows), (keys, key_rows)))
            ]
        )
        for copy in copies[-1]:
            copy.start()
    small = [
        pltpu.make_async_copy(rates_in, rates, arrived.at[heads]),
        pltpu.make_async_copy(gain_in, gain, arrived.at[heads + 1]),
    ]
    for copy in small:
        copy.start()
    for copy in small:
        copy.wait()
    for h in range(heads):
        rate = jnp.full((1, SIZE), rates[h], F32)
        consts[:, column(h)] = jnp.concatenate([gain[:, column(h)], rate, jnp.zeros((6, SIZE), F32)], axis=0)
    for slot, cols in enumerate(heads_of(False, heads)):
        tail = tail_out_of(consts[pl.ds(RATE, 1), cols], length)
        for copy in copies[slot]:
            copy.wait()
        scaled = value_rows[:, column(slot)].astype(F32) * tail
        out[slot] = dot_split(key_rows[:, column(slot)], scaled, 0, 0)


def own_sums_kernel(consts, keys, values, out):
    length = keys.shape[0]
    for slot, cols in enumerate(heads_of(True, keys.shape[1] // SIZE)):
        scaled = values[:, cols].astype(F32) * tail_out_of(consts[pl.ds(RATE, 1), cols], length)
        out[slot] = dot_split(keys[:, cols], scaled, 0, 0)


def intra_kernel(consts, queries, keys, values, token_in, out, token):
    half = queries.shape[0] // 2
    first, second = pl.ds(0, half), pl.ds(half, half)
    for h in range(queries.shape[1] // SIZE):
        cols = column(h)
        same, across = tile_weights(consts[pl.ds(RATE, 1), cols], False)
        q, k, v = (ref.at[:, cols] for ref in (queries, keys, values))
        out[first, cols] = dot(weighted(q, k, first, first, same), v[first, :], 1, 0)
        out[second, cols] = dot(weighted(q, k, second, first, across), v[first, :], 1, 0) + dot(
            weighted(q, k, second, second, same), v[second, :], 1, 0
        )
    token[...] = jnp.zeros_like(token)


def mixed_kernel(consts, queries, mine, other, intra, cotangent, mixed, stats, square, inner):
    length = queries.shape[0]
    heads = queries.shape[1] // SIZE
    core = lax.axis_index("seq") % 2
    for h in range(heads):
        cols = column(h)
        slot = h % (heads // 2)
        state_in = jnp.where(core == h // (heads // 2), mine[slot], other[slot])
        head_in = head_in_of(consts[pl.ds(RATE, 1), cols], length)
        value = intra[:, cols] + head_in * dot_split(queries[:, cols], state_in, 1, 0)
        mixed[:, cols] = value
        new_square = value * value
        new_inner = cotangent[:, cols].astype(F32) * consts[pl.ds(GAIN, 1), cols] * value
        if h > 0:
            new_square, new_inner = new_square + square[...], new_inner + inner[...]
        square[...] = new_square
        inner[...] = new_inner
    pieces = []
    for ref in (square, inner):
        for start in range(0, length, SIZE):
            pieces.append(jnp.sum(ref[pl.ds(start, SIZE), :].T, axis=0, keepdims=True))
    stats[...] = jnp.broadcast_to(jnp.concatenate(pieces, axis=0)[None], stats.shape)


def token_scales(received, channels, inv_out, coef_out):
    total = jnp.sum(received[...], axis=0)
    chunks = total.shape[0] // 2
    inv = lax.rsqrt(total[:chunks] / channels + epsilon)
    coef = inv * inv * inv * total[chunks:] / channels
    for chunk in range(chunks):
        rows = pl.ds(chunk * SIZE, SIZE)
        inv_out[rows, :] = jnp.broadcast_to(inv[chunk : chunk + 1], (SIZE, SIZE)).T
        coef_out[rows, :] = jnp.broadcast_to(coef[chunk : chunk + 1], (SIZE, SIZE)).T


def mixed_grad_of(consts, cols, upstream, value, inv, coef):
    return (inv * (upstream * consts[pl.ds(GAIN, 1), cols]) - value * coef).astype(BF16)


def back_sum_kernel(mine, channels, consts, received, mixed, cotangent, queries, sums, inv, coef):
    length = queries.shape[0]
    token_scales(received, channels, inv, coef)
    for slot, cols in enumerate(heads_of(mine, queries.shape[1] // SIZE)):
        upstream = cotangent[:, cols].astype(F32)
        value = mixed[:, cols]
        mixed_grad = mixed_grad_of(consts, cols, upstream, value, inv[...], coef[...])
        scaled = mixed_grad.astype(F32) * head_in_of(consts[pl.ds(RATE, 1), cols], length)
        sums[slot, pl.ds(0, SIZE), :] = dot_split(queries[:, cols], scaled, 0, 0)
        gain_grad = jnp.sum(upstream * (value * inv[...]), axis=0, keepdims=True)
        sums[slot, pl.ds(SIZE, EXTRA), :] = jnp.broadcast_to(gain_grad, (EXTRA, SIZE))


def grads_kernel(
    channels, consts, received, mixed_in, cotangent, queries, keys, values, mine, other,
    attended_out, query_out, key_out, value_out, token,
    inv, coef, mixed, grad, attended, query_grad, key_part, value_part, arrived, sent,
):
    length = queries.shape[0]
    heads = queries.shape[1] // SIZE
    half = length // 2
    first, second = pl.ds(0, half), pl.ds(half, half)
    copies, stores = [], []
    for h in range(heads):
        copies.append(pltpu.make_async_copy(mixed_in.at[:, column(h)], mixed.at[:, column(h)], arrived.at[h]))
        copies[-1].start()
    token[...] = jnp.zeros_like(token)
    token_scales(received, channels, inv, coef)
    core = lax.axis_index("seq") % 2
    for h in range(heads):
        cols = column(h)
        slot = h % (heads // 2)
        rate = consts[pl.ds(RATE, 1), cols]
        state_in = jnp.where(core == h // (heads // 2), mine[slot], other[slot])
        same, across = tile_weights(rate, False)
        same_turned, across_turned = tile_weights(rate, True)
        copies[h].wait()
        value = mixed[:, cols]
        attended[:, cols] = (value * inv[...] * consts[pl.ds(GAIN, 1), cols]).astype(BF16)
        grad[:, cols] = mixed_grad_of(consts, cols, cotangent[:, cols].astype(F32), value, inv[...], coef[...])
        q, k, v, g = (ref.at[:, cols] for ref in (queries, keys, values, grad))
        state_part = head_in_of(rate, length) * dot_split(g[...], state_in, 1, 1)
        query_grad[first, cols] = (
            dot(weighted(g, v, first, first, same), k[first, :], 1, 0) + state_part[:half]
        ).astype(BF16)
        query_grad[second, cols] = (
            dot(weighted(g, v, second, first, across), k[first, :], 1, 0)
            + dot(weighted(g, v, second, second, same), k[second, :], 1, 0)
            + state_part[half:]
        ).astype(BF16)
        key_part[first, cols] = dot(weighted(v, g, first, first, same_turned), q[first, :], 1, 0) + dot(
            weighted(v, g, first, second, across_turned), q[second, :], 1, 0
        )
        key_part[second, cols] = dot(weighted(v, g, second, second, same_turned), q[second, :], 1, 0)
        value_part[first, cols] = dot(weighted(k, q, first, first, same_turned), g[first, :], 1, 0) + dot(
            weighted(k, q, first, second, across_turned), g[second, :], 1, 0
        )
        value_part[second, cols] = dot(weighted(k, q, second, second, same_turned), g[second, :], 1, 0)
        targets = ((attended, attended_out), (query_grad, query_out), (key_part, key_out), (value_part, value_out))
        for i, (rows, target) in enumerate(targets):
            stores.append(pltpu.make_async_copy(rows.at[:, cols], target.at[:, cols], sent.at[4 * h + i]))
            stores[-1].start()
    for store in stores:
        store.wait()


def finish_kernel(
    mine, consts, back, keys, values, key_part, value_part, *refs
):
    key_grad, value_grad, key_rows, value_rows, sent = refs[-5:]
    length = keys.shape[0]
    copies = []
    for slot, cols in enumerate(heads_of(mine, keys.shape[1] // SIZE)):
        back_in = back[slot, pl.ds(0, SIZE), :]
        tail = tail_out_of(consts[pl.ds(RATE, 1), cols], length)
        to = column(slot)
        key_rows[:, to] = (key_part[:, cols] + tail * dot_split(values[:, cols], back_in, 1, 1)).astype(BF16)
        value_rows[:, to] = (value_part[:, cols] + tail * dot_split(keys[:, cols], back_in, 1, 0)).astype(BF16)
        for i, (rows, target) in enumerate(((key_rows, key_grad), (value_rows, value_grad))):
            copies.append(pltpu.make_async_copy(rows.at[:, to], target.at[:, cols], sent.at[2 * slot + i]))
            copies[-1].start()
    for copy in copies:
        copy.wait()


def gain_kernel(mine, other, out):
    heads = out.shape[1] // SIZE
    core = lax.axis_index("seq") % 2
    for h in range(heads):
        slot = h % (heads // 2)
        rows = pl.ds(SIZE, 1)
        out[:, column(h)] = jnp.where(core == h // (heads // 2), mine[slot, rows, :], other[slot, rows, :])


def is_first(reverse):
    return (lax.axis_index("seq") % 2) == (1 if reverse else 0)


def chip_sum_kernel(length, reverse, consts, keep, received, out):
    first = is_first(reverse)
    half = SIZE // 2
    extra = keep.shape[1] - SIZE
    for slot, cols in enumerate(heads_of(True, consts.shape[1] // SIZE)):
        factor = jnp.exp(-consts[pl.ds(RATE, 1), cols] * length)
        own, other = keep[slot, pl.ds(0, SIZE), :], received[slot, pl.ds(0, SIZE), :]
        total = jnp.where(first, factor * own + other, factor * other + own)
        for i in range(2):
            out[2 * slot + i, pl.ds(0, half), :] = total[i * half : (i + 1) * half]
            if extra:
                out[2 * slot + i, pl.ds(half, extra), :] = keep[slot, pl.ds(SIZE, extra), :] + received[slot, pl.ds(SIZE, extra), :]


def shard_factors(consts, length):
    position = lax.axis_index("seq")
    heads = consts.shape[1] // SIZE
    head = position % 2 * (heads // 2) + position // 2 % CHIPS * (heads // 2) // CHIPS
    rate = consts[pl.ds(RATE, 1), pl.ds(pl.multiple_of(head * SIZE, SIZE), SIZE)]
    return jnp.exp(-rate * (2 * length)), jnp.exp(-rate * (2 * length * CHIPS))


def chip_order(reverse):
    return range(CHIPS - 1, -1, -1) if reverse else range(CHIPS)


def totals_kernel(length, reverse, consts, parts, token, out):
    factor, _ = shard_factors(consts, length)
    rows = SIZE // 2
    total = jnp.zeros((rows, SIZE), F32)
    for k in chip_order(reverse):
        total = factor * total + parts[k, :rows]
    out[:rows] = total
    if parts.shape[1] > rows:
        out[rows:] = sum(parts[k, rows:] for k in range(CHIPS))


def fold_forward_kernel(length, consts, parts, nearest, near, far, token, out):
    factor, group_factor = shard_factors(consts, length)
    carry = nearest[...] + group_factor * (near[...] + group_factor * far[...])
    for k in chip_order(False):
        out[k] = carry
        carry = factor * carry + parts[k]


def fold_back_kernel(length, consts, parts, arrived, out):
    factor, group_factor = shard_factors(consts, length)
    rows = SIZE // 2
    group = lax.axis_index("seq") // (2 * CHIPS)
    carry = jnp.zeros((rows, SIZE), F32)
    for g in range(arrived.shape[0] - 1, 0, -1):
        carry = jnp.where(group < g, group_factor * carry + arrived[g, :rows], carry)
    extra = sum(arrived[g, rows:] for g in range(arrived.shape[0]))
    for k in chip_order(True):
        out[k, :rows] = carry
        out[k, rows:] = extra
        carry = factor * carry + parts[k, :rows]


def states_kernel(length, reverse, consts, shards, keep, received, mine, give):
    first = is_first(reverse)
    half = SIZE // 2
    extra = keep.shape[1] - SIZE
    rows = pl.ds(0, SIZE)
    for slot, cols in enumerate(heads_of(True, consts.shape[1] // SIZE)):
        factor = jnp.exp(-consts[pl.ds(RATE, 1), cols] * length)
        before = shards[pl.ds(2 * slot, 2), pl.ds(0, half), :].reshape(SIZE, SIZE)
        after = factor * before + jnp.where(first, keep[slot, rows, :], received[slot, rows, :])
        mine[slot, rows, :] = jnp.where(first, before, after)
        give[slot, rows, :] = jnp.where(first, after, before)
        if extra:
            total = shards[2 * slot, pl.ds(half, extra), :]
            mine[slot, pl.ds(SIZE, extra), :] = total
            give[slot, pl.ds(SIZE, extra), :] = total


def like(x):
    return jax.ShapeDtypeStruct(x.shape, x.dtype)


def array(kind, *shape):
    return jax.ShapeDtypeStruct(shape, kind)


def whole_call(kernel, out_shape, operands, in_specs=None, out_specs=None, **rest):
    vmem = pl.BlockSpec(memory_space=pltpu.VMEM)
    return pl.pallas_call(
        kernel,
        in_specs=in_specs or [vmem] * len(operands),
        out_specs=out_specs or jax.tree.map(lambda _: vmem, out_shape),
        out_shape=out_shape,
        compiler_params=pltpu.CompilerParams(vmem_limit_bytes=VMEM_LIMIT),
        **rest,
    )(*operands)


def swap(x):
    return lax.ppermute(x, "seq", [(i, i ^ 1) for i in range(lax.axis_size("seq"))])


def exchange(x):
    groups = lax.axis_size("seq") // (2 * CHIPS)
    members = [[2 * (g * CHIPS + c) + core for c in range(CHIPS)] for g in range(groups) for core in range(2)]
    return lax.all_to_all(x, "seq", 0, 0, axis_index_groups=members)


def onward(x, by):
    count, step = lax.axis_size("seq"), by * 2 * CHIPS
    return lax.ppermute(x, "seq", [(i, i + step) for i in range(count - step)])


def among_groups(x):
    groups = lax.axis_size("seq") // (2 * CHIPS)
    return lax.all_gather(
        x, "seq", axis_index_groups=[[g * 2 * CHIPS + j for g in range(groups)] for j in range(2 * CHIPS)]
    )


def body(queries, keys, values, rates, gain, cotangent):
    length, channels = queries.shape
    heads = rates.shape[0]
    head_devices = lax.axis_size("head")
    total_channels = channels * head_devices

    anywhere = pl.BlockSpec(memory_space=pl.ANY)
    in_vmem = pl.BlockSpec(memory_space=pltpu.VMEM)
    hbm = lambda x: pltpu.with_memory_space_constraint(x, pltpu.HBM)
    vmem = lambda x: pltpu.with_memory_space_constraint(x, pltpu.VMEM)
    wide = array(F32, length, channels)
    narrow = array(BF16, length, channels)
    scratch = pltpu.VMEM((length, SIZE), F32)
    half_rows = pltpu.VMEM((length, channels // 2), BF16)
    rows = pltpu.VMEM((length, channels), BF16)
    wide_rows = pltpu.VMEM((length, channels), F32)
    dma = pltpu.SemaphoreType.DMA
    token_shape = array(F32, 8, SIZE)
    states_shape = array(F32, heads // 2, SIZE, SIZE)
    shards = (CHIPS, SIZE // 2, SIZE)
    square = 2 * heads * length * length * SIZE

    def cost(flops):
        return pl.CostEstimate(flops=flops, bytes_accessed=6 << 20, transcendentals=0)

    other_sums, consts = whole_call(
        first_sums_kernel, [states_shape, array(F32, 8, channels)],
        [hbm(rates), hbm(gain.reshape(1, channels)), hbm(keys), hbm(values)], in_specs=[anywhere] * 4,
        scratch_shapes=[pltpu.SMEM((heads,), F32), pltpu.VMEM((1, channels), F32), half_rows, half_rows, dma((heads + 2,))],
    )
    received = swap(other_sums)
    keep = whole_call(own_sums_kernel, states_shape, [consts, keys, values])
    sums = whole_call(
        lambda *refs: chip_sum_kernel(length, False, *refs), array(F32, *shards), [consts, keep, received]
    )
    parts = exchange(sums)
    total = whole_call(
        lambda *refs: totals_kernel(length, False, *refs), array(F32, *shards[1:]), [consts, parts, consts]
    )
    intra, token = whole_call(
        intra_kernel, [wide, token_shape], [consts, queries, keys, values, total], cost_estimate=cost(2 * square)
    )
    near = onward(total, 2)
    nearest, far = onward(total, 1), onward(total, 3)
    folded = whole_call(
        lambda *refs: fold_forward_kernel(length, *refs), array(F32, *shards),
        [consts, parts, nearest, near, far, token],
    )
    mine, give = whole_call(
        lambda *refs: states_kernel(length, False, *refs), [states_shape, states_shape],
        [consts, exchange(folded), keep, received],
    )
    other = swap(give)
    stats_shape = (head_devices, 2 * length // SIZE, SIZE)
    mixed, stats = whole_call(
        mixed_kernel, [wide, array(F32, *stats_shape)],
        [consts, queries, mine, other, intra, cotangent], scratch_shapes=[scratch, scratch],
    )
    stats = lax.all_to_all(stats, "head", 0, 0)

    sums_shape = array(F32, heads // 2, SIZE + EXTRA, SIZE)
    shards = (CHIPS, SIZE // 2 + EXTRA, SIZE)

    def back_sums(mine):
        return whole_call(
            lambda *refs: back_sum_kernel(mine, total_channels, *refs), sums_shape,
            [consts, stats, mixed, cotangent, queries], scratch_shapes=[scratch, scratch],
        )

    received = swap(back_sums(False))
    keep = back_sums(True)
    sums = whole_call(
        lambda *refs: chip_sum_kernel(length, True, *refs), array(F32, *shards), [consts, keep, received]
    )
    parts = exchange(sums)
    part = pltpu.HBM((length, channels), F32)
    attended, query_grad, key_part, value_part, token = whole_call(
        lambda *refs: grads_kernel(total_channels, *refs), [narrow, narrow, part, part, token_shape],
        [consts, stats, hbm(mixed), cotangent, queries, keys, values, mine, other],
        in_specs=[in_vmem, in_vmem, anywhere] + [in_vmem] * 6, out_specs=[anywhere] * 4 + [in_vmem],
        scratch_shapes=[scratch, scratch, wide_rows, rows, rows, rows, wide_rows, wide_rows, dma((heads,)), dma((4 * heads,))],
        cost_estimate=cost(6 * square),
    )
    total = whole_call(
        lambda *refs: totals_kernel(length, True, *refs), array(F32, *shards[1:]), [consts, parts, token]
    )
    folded = whole_call(
        lambda *refs: fold_back_kernel(length, *refs), array(F32, *shards), [consts, parts, among_groups(total)]
    )
    mine, give = whole_call(
        lambda *refs: states_kernel(length, True, *refs), [sums_shape, sums_shape],
        [consts, exchange(folded), keep, received],
    )
    other = swap(give)

    def finish(is_mine, back, *begun):
        return whole_call(
            lambda *refs: finish_kernel(is_mine, *refs), [narrow, narrow],
            [consts, back, keys, values, vmem(key_part), vmem(value_part), *begun],
            in_specs=[in_vmem] * 6 + [anywhere] * len(begun), out_specs=[anywhere] * 2,
            scratch_shapes=[half_rows, half_rows, dma((heads,))],
            input_output_aliases={6: 0, 7: 1} if begun else {},
        )

    key_grad, value_grad = finish(False, other, *finish(True, mine))
    gain_grad = whole_call(gain_kernel, array(F32, 1, channels), [mine, other])
    return attended, query_grad, key_grad, value_grad, gain_grad.reshape(channels)


def solution(mesh):
    placed = (
        P("seq", "head"),
        P("seq", "head"),
        P("seq", "head"),
        P("head"),
        P("head"),
        P("seq", "head"),
    )
    return jax.shard_map(
        body,
        mesh=mesh,
        in_specs=placed,
        out_specs=(
            P("seq", "head"),
            P("seq", "head"),
            P("seq", "head"),
            P("seq", "head"),
            P("head"),
        ),
        check_vma=False,
    )
```

```python
import jax
import jax.numpy as jnp
from jax import lax
from jax.experimental import pallas as pl
from jax.experimental.pallas import tpu as pltpu
from jax.sharding import PartitionSpec as P

epsilon = 1e-06
F32, BF16 = jnp.float32, jnp.bfloat16
SIZE = 128
CHIPS = 4
EXTRA = 8
GAIN, RATE = 0, 1
VMEM_LIMIT = 16 * 1024 * 1024


def dot(a, b, over_a, over_b):
    return lax.dot_general(a, b, (((over_a,), (over_b,)), ((), ())), preferred_element_type=F32)


def dot_split(a, x, over_a, over_x):
    high = x.astype(BF16)
    low = (x - high.astype(F32)).astype(BF16)
    both = dot(a, jnp.concatenate([high, low], axis=1 - over_x), over_a, over_x)
    return both[:, : both.shape[1] // 2] + both[:, both.shape[1] // 2 :]


def rows_of(length):
    return lax.broadcasted_iota(jnp.int32, (length, SIZE), 0).astype(F32)


def lanes_of():
    return lax.broadcasted_iota(jnp.int32, (1, SIZE), 1).astype(F32)


def head_in_of(rate, length):
    base = jnp.exp(-rate * (rows_of(SIZE) + 1.0))
    return jnp.concatenate([base * jnp.exp(-rate * start) for start in range(0, length, SIZE)], axis=0)


def tail_out_of(rate, length):
    base = jnp.exp(-rate * (SIZE - 1.0 - rows_of(SIZE)))
    return jnp.concatenate([base * jnp.exp(-rate * (length - SIZE - start)) for start in range(0, length, SIZE)], axis=0)


def tile_weights(rate):
    rows, lanes = rows_of(SIZE), lanes_of()
    distance = rows - lanes
    near = jnp.where(distance >= 0, jnp.exp(-rate * jnp.maximum(distance, 0.0)), 0.0)
    far = jnp.exp(-rate * (rows + 1.0)) * jnp.exp(-rate * (SIZE - 1.0 - lanes))
    step = jnp.exp(-rate * SIZE)
    farther = far * step

    def square(a, b, c, d):
        return jnp.concatenate([jnp.concatenate([a, b], axis=1), jnp.concatenate([c, d], axis=1)], axis=0)

    return square(near, jnp.zeros_like(near), far, near), square(farther, far, farther * step, farther)


def weighted(a, b, rows_a, rows_b, weight):
    return (dot(a[rows_a, :], b[rows_b, :], 1, 1) * weight).astype(BF16)


def column(h):
    return pl.ds(h * SIZE, SIZE)


def heads_of(mine, heads):
    core = lax.axis_index("seq") % 2
    start = (core if mine else 1 - core) * (heads // 2)
    return [pl.ds(pl.multiple_of((start + slot) * SIZE, SIZE), SIZE) for slot in range(heads // 2)]


def first_sums_kernel(
    rates_in, gain_in, keys, values, out, consts, rates, gain, key_rows, value_rows, arrived
):
    length = keys.shape[0]
    heads = rates.shape[0]
    copies = []
    for slot, cols in enumerate(heads_of(False, heads)):
        copies.append(
            [
                pltpu.make_async_copy(source.at[:, cols], rows.at[:, column(slot)], arrived.at[2 * slot + i])
                for i, (source, rows) in enumerate(((values, value_rows), (keys, key_rows)))
            ]
        )
        for copy in copies[-1]:
            copy.start()
    small = [
        pltpu.make_async_copy(rates_in, rates, arrived.at[heads]),
        pltpu.make_async_copy(gain_in, gain, arrived.at[heads + 1]),
    ]
    for copy in small:
        copy.start()
    for copy in small:
        copy.wait()
    for h in range(heads):
        rate = jnp.full((1, SIZE), rates[h], F32)
        consts[:, column(h)] = jnp.concatenate([gain[:, column(h)], rate, jnp.zeros((6, SIZE), F32)], axis=0)
    for slot, cols in enumerate(heads_of(False, heads)):
        tail = tail_out_of(consts[pl.ds(RATE, 1), cols], length)
        for copy in copies[slot]:
            copy.wait()
        scaled = value_rows[:, column(slot)].astype(F32) * tail
        out[slot] = dot_split(key_rows[:, column(slot)], scaled, 0, 0)


def own_sums_kernel(consts, keys, values, out):
    length = keys.shape[0]
    for slot, cols in enumerate(heads_of(True, keys.shape[1] // SIZE)):
        scaled = values[:, cols].astype(F32) * tail_out_of(consts[pl.ds(RATE, 1), cols], length)
        out[slot] = dot_split(keys[:, cols], scaled, 0, 0)


def intra_kernel(consts, queries, keys, values, token_in, out, token):
    half = queries.shape[0] // 2
    first, second = pl.ds(0, half), pl.ds(half, half)
    for h in range(queries.shape[1] // SIZE):
        cols = column(h)
        same, across = tile_weights(consts[pl.ds(RATE, 1), cols])
        q, k, v = (ref.at[:, cols] for ref in (queries, keys, values))
        out[first, cols] = dot(weighted(q, k, first, first, same), v[first, :], 1, 0)
        out[second, cols] = dot(weighted(q, k, second, first, across), v[first, :], 1, 0) + dot(
            weighted(q, k, second, second, same), v[second, :], 1, 0
        )
    token[...] = jnp.zeros_like(token)


def mixed_kernel(consts, queries, mine, other, intra, cotangent, mixed, stats, square, inner):
    length = queries.shape[0]
    heads = queries.shape[1] // SIZE
    core = lax.axis_index("seq") % 2
    for h in range(heads):
        cols = column(h)
        slot = h % (heads // 2)
        state_in = jnp.where(core == h // (heads // 2), mine[slot], other[slot])
        head_in = head_in_of(consts[pl.ds(RATE, 1), cols], length)
        value = intra[:, cols] + head_in * dot_split(queries[:, cols], state_in, 1, 0)
        mixed[:, cols] = value
        new_square = value * value
        new_inner = cotangent[:, cols].astype(F32) * consts[pl.ds(GAIN, 1), cols] * value
        if h > 0:
            new_square, new_inner = new_square + square[...], new_inner + inner[...]
        square[...] = new_square
        inner[...] = new_inner
    pieces = []
    for ref in (square, inner):
        for start in range(0, length, SIZE):
            pieces.append(jnp.sum(ref[pl.ds(start, SIZE), :].T, axis=0, keepdims=True))
    stats[...] = jnp.broadcast_to(jnp.concatenate(pieces, axis=0)[None], stats.shape)


def token_scales(received, channels, inv_out, coef_out):
    total = jnp.sum(received[...], axis=0)
    chunks = total.shape[0] // 2
    inv = lax.rsqrt(total[:chunks] / channels + epsilon)
    coef = inv * inv * inv * total[chunks:] / channels
    for chunk in range(chunks):
        rows = pl.ds(chunk * SIZE, SIZE)
        inv_out[rows, :] = jnp.broadcast_to(inv[chunk : chunk + 1], (SIZE, SIZE)).T
        coef_out[rows, :] = jnp.broadcast_to(coef[chunk : chunk + 1], (SIZE, SIZE)).T


def mixed_grad_of(consts, cols, upstream, value, inv, coef):
    return (inv * (upstream * consts[pl.ds(GAIN, 1), cols]) - value * coef).astype(BF16)


def back_sum_kernel(mine, channels, consts, received, mixed, cotangent, queries, sums, inv, coef):
    length = queries.shape[0]
    token_scales(received, channels, inv, coef)
    for slot, cols in enumerate(heads_of(mine, queries.shape[1] // SIZE)):
        upstream = cotangent[:, cols].astype(F32)
        value = mixed[:, cols]
        mixed_grad = mixed_grad_of(consts, cols, upstream, value, inv[...], coef[...])
        scaled = mixed_grad.astype(F32) * head_in_of(consts[pl.ds(RATE, 1), cols], length)
        sums[slot, pl.ds(0, SIZE), :] = dot_split(queries[:, cols], scaled, 0, 0)
        gain_grad = jnp.sum(upstream * (value * inv[...]), axis=0, keepdims=True)
        sums[slot, pl.ds(SIZE, EXTRA), :] = jnp.broadcast_to(gain_grad, (EXTRA, SIZE))


def grads_kernel(
    channels, consts, received, mixed_in, cotangent, queries, keys, values, mine, other, totals,
    attended_out, query_out, key_part, value_part, token,
    inv, coef, mixed, grad, attended, query_grad, arrived, sent,
):
    length = queries.shape[0]
    heads = queries.shape[1] // SIZE
    half = length // 2
    first, second = pl.ds(0, half), pl.ds(half, half)
    copies, stores = [], []
    for h in range(heads):
        copies.append(pltpu.make_async_copy(mixed_in.at[:, column(h)], mixed.at[:, column(h)], arrived.at[h]))
        copies[-1].start()
    token[...] = jnp.zeros_like(token)
    token_scales(received, channels, inv, coef)
    core = lax.axis_index("seq") % 2
    for h in range(heads):
        cols = column(h)
        slot = h % (heads // 2)
        rate = consts[pl.ds(RATE, 1), cols]
        state_in = jnp.where(core == h // (heads // 2), mine[slot], other[slot])
        same, across = tile_weights(rate)
        copies[h].wait()
        value = mixed[:, cols]
        attended[:, cols] = (value * inv[...] * consts[pl.ds(GAIN, 1), cols]).astype(BF16)
        grad[:, cols] = mixed_grad_of(consts, cols, cotangent[:, cols].astype(F32), value, inv[...], coef[...])
        q, k, v, g = (ref.at[:, cols] for ref in (queries, keys, values, grad))
        state_part = head_in_of(rate, length) * dot_split(g[...], state_in, 1, 1)
        upper = weighted(g, v, first, first, same)
        lower = weighted(g, v, second, first, across)
        final = weighted(g, v, second, second, same)
        query_grad[first, cols] = (dot(upper, k[first, :], 1, 0) + state_part[:half]).astype(BF16)
        query_grad[second, cols] = (
            dot(lower, k[first, :], 1, 0) + dot(final, k[second, :], 1, 0) + state_part[half:]
        ).astype(BF16)
        for i, (rows, target) in enumerate(((attended, attended_out), (query_grad, query_out))):
            stores.append(pltpu.make_async_copy(rows.at[:, cols], target.at[:, cols], sent.at[2 * h + i]))
            stores[-1].start()
        key_part[first, cols] = dot(upper, q[first, :], 0, 0) + dot(lower, q[second, :], 0, 0)
        key_part[second, cols] = dot(final, q[second, :], 0, 0)
        upper = weighted(q, k, first, first, same)
        lower = weighted(q, k, second, first, across)
        final = weighted(q, k, second, second, same)
        value_part[first, cols] = dot(upper, g[first, :], 0, 0) + dot(lower, g[second, :], 0, 0)
        value_part[second, cols] = dot(final, g[second, :], 0, 0)
    for store in stores:
        store.wait()


def finish_kernel(mine, consts, back, keys, values, key_part, value_part, *refs):
    key_grad, value_grad, gain_grad, key_rows, value_rows, sent = refs[-6:]
    half = keys.shape[1] // SIZE // 2
    if mine:
        gain_grad[...] = jnp.zeros_like(gain_grad)
    else:
        for states, heads in ((refs[0], heads_of(True, 2 * half)), (back, heads_of(False, 2 * half))):
            for slot, cols in enumerate(heads):
                gain_grad[:, cols] = states[slot, pl.ds(SIZE, 1), :]
    length = keys.shape[0]
    copies = []
    for slot, cols in enumerate(heads_of(mine, keys.shape[1] // SIZE)):
        back_in = back[slot, pl.ds(0, SIZE), :]
        tail = tail_out_of(consts[pl.ds(RATE, 1), cols], length)
        to = column(slot)
        key_rows[:, to] = (key_part[:, cols] + tail * dot_split(values[:, cols], back_in, 1, 1)).astype(BF16)
        value_rows[:, to] = (value_part[:, cols] + tail * dot_split(keys[:, cols], back_in, 1, 0)).astype(BF16)
        for i, (rows, target) in enumerate(((key_rows, key_grad), (value_rows, value_grad))):
            copies.append(pltpu.make_async_copy(rows.at[:, to], target.at[:, cols], sent.at[2 * slot + i]))
            copies[-1].start()
    for copy in copies:
        copy.wait()


def is_first(reverse):
    return (lax.axis_index("seq") % 2) == (1 if reverse else 0)


def chip_sum_kernel(length, reverse, consts, keep, received, out):
    first = is_first(reverse)
    half = SIZE // 2
    extra = keep.shape[1] - SIZE
    for slot, cols in enumerate(heads_of(True, consts.shape[1] // SIZE)):
        factor = jnp.exp(-consts[pl.ds(RATE, 1), cols] * length)
        own, other = keep[slot, pl.ds(0, SIZE), :], received[slot, pl.ds(0, SIZE), :]
        total = jnp.where(first, factor * own + other, factor * other + own)
        for i in range(2):
            out[2 * slot + i, pl.ds(0, half), :] = total[i * half : (i + 1) * half]
            if extra:
                out[2 * slot + i, pl.ds(half, extra), :] = keep[slot, pl.ds(SIZE, extra), :] + received[slot, pl.ds(SIZE, extra), :]


def shard_factors(consts, length):
    position = lax.axis_index("seq")
    heads = consts.shape[1] // SIZE
    head = position % 2 * (heads // 2) + position // 2 % CHIPS * (heads // 2) // CHIPS
    rate = consts[pl.ds(RATE, 1), pl.ds(pl.multiple_of(head * SIZE, SIZE), SIZE)]
    return jnp.exp(-rate * (2 * length)), jnp.exp(-rate * (2 * length * CHIPS))


def chip_order(reverse):
    return range(CHIPS - 1, -1, -1) if reverse else range(CHIPS)


def totals_kernel(length, reverse, consts, parts, out):
    factor, _ = shard_factors(consts, length)
    rows = SIZE // 2
    total = jnp.zeros((rows, SIZE), F32)
    for k in chip_order(reverse):
        total = factor * total + parts[k, :rows]
    if parts.shape[1] == rows:
        out[...] = total
        return
    extra = sum(parts[k, rows:] for k in range(CHIPS))
    for g in range(out.shape[0]):
        out[g, :rows] = total
        out[g, rows:] = extra


def fold_forward_kernel(length, consts, parts, nearest, near, far, token, out):
    factor, group_factor = shard_factors(consts, length)
    carry = nearest[...] + group_factor * (near[...] + group_factor * far[...])
    for k in chip_order(False):
        out[k] = carry
        carry = factor * carry + parts[k]


def fold_back_kernel(length, consts, parts, arrived, token, out):
    factor, group_factor = shard_factors(consts, length)
    rows = SIZE // 2
    group = lax.axis_index("seq") // (2 * CHIPS)
    carry = jnp.zeros((rows, SIZE), F32)
    for g in range(arrived.shape[0] - 1, 0, -1):
        carry = jnp.where(group < g, group_factor * carry + arrived[g, :rows], carry)
    extra = sum(arrived[g, rows:] for g in range(arrived.shape[0]))
    for k in chip_order(True):
        out[k, :rows] = carry
        out[k, rows:] = extra
        carry = factor * carry + parts[k, :rows]


def states_kernel(length, reverse, consts, shards, keep, received, mine, give):
    first = is_first(reverse)
    half = SIZE // 2
    extra = keep.shape[1] - SIZE
    rows = pl.ds(0, SIZE)
    for slot, cols in enumerate(heads_of(True, consts.shape[1] // SIZE)):
        factor = jnp.exp(-consts[pl.ds(RATE, 1), cols] * length)
        before = shards[pl.ds(2 * slot, 2), pl.ds(0, half), :].reshape(SIZE, SIZE)
        after = factor * before + jnp.where(first, keep[slot, rows, :], received[slot, rows, :])
        mine[slot, rows, :] = jnp.where(first, before, after)
        give[slot, rows, :] = jnp.where(first, after, before)
        if extra:
            total = shards[2 * slot, pl.ds(half, extra), :]
            mine[slot, pl.ds(SIZE, extra), :] = total
            give[slot, pl.ds(SIZE, extra), :] = total


def like(x):
    return jax.ShapeDtypeStruct(x.shape, x.dtype)


def array(kind, *shape):
    return jax.ShapeDtypeStruct(shape, kind)


def whole_call(kernel, out_shape, operands, in_specs=None, out_specs=None, **rest):
    vmem = pl.BlockSpec(memory_space=pltpu.VMEM)
    return pl.pallas_call(
        kernel,
        in_specs=in_specs or [vmem] * len(operands),
        out_specs=out_specs or jax.tree.map(lambda _: vmem, out_shape),
        out_shape=out_shape,
        compiler_params=pltpu.CompilerParams(vmem_limit_bytes=VMEM_LIMIT),
        **rest,
    )(*operands)


def swap(x):
    return lax.ppermute(x, "seq", [(i, i ^ 1) for i in range(lax.axis_size("seq"))])


def exchange(x):
    groups = lax.axis_size("seq") // (2 * CHIPS)
    members = [[2 * (g * CHIPS + c) + core for c in range(CHIPS)] for g in range(groups) for core in range(2)]
    return lax.all_to_all(x, "seq", 0, 0, axis_index_groups=members)


def onward(x, by):
    count, step = lax.axis_size("seq"), by * 2 * CHIPS
    return lax.ppermute(x, "seq", [(i, i + step) for i in range(count - step)])


def among_groups(x):
    groups = lax.axis_size("seq") // (2 * CHIPS)
    members = [[g * 2 * CHIPS + j for g in range(groups)] for j in range(2 * CHIPS)]
    return lax.all_to_all(x, "seq", 0, 0, axis_index_groups=members)


def body(queries, keys, values, rates, gain, cotangent):
    length, channels = queries.shape
    heads = rates.shape[0]
    head_devices = lax.axis_size("head")
    total_channels = channels * head_devices

    anywhere = pl.BlockSpec(memory_space=pl.ANY)
    in_vmem = pl.BlockSpec(memory_space=pltpu.VMEM)
    hbm = lambda x: pltpu.with_memory_space_constraint(x, pltpu.HBM)
    vmem = lambda x: pltpu.with_memory_space_constraint(x, pltpu.VMEM)
    wide = array(F32, length, channels)
    narrow = array(BF16, length, channels)
    scratch = pltpu.VMEM((length, SIZE), F32)
    half_rows = pltpu.VMEM((length, channels // 2), BF16)
    rows = pltpu.VMEM((length, channels), BF16)
    wide_rows = pltpu.VMEM((length, channels), F32)
    dma = pltpu.SemaphoreType.DMA
    token_shape = array(F32, 8, SIZE)
    states_shape = array(F32, heads // 2, SIZE, SIZE)
    shards = (CHIPS, SIZE // 2, SIZE)
    square = 2 * heads * length * length * SIZE

    def cost(flops):
        return pl.CostEstimate(flops=flops, bytes_accessed=6 << 20, transcendentals=0)

    other_sums, consts = whole_call(
        first_sums_kernel, [states_shape, array(F32, 8, channels)],
        [hbm(rates), hbm(gain.reshape(1, channels)), hbm(keys), hbm(values)], in_specs=[anywhere] * 4,
        scratch_shapes=[pltpu.SMEM((heads,), F32), pltpu.VMEM((1, channels), F32), half_rows, half_rows, dma((heads + 2,))],
    )
    received = swap(other_sums)
    keep = whole_call(own_sums_kernel, states_shape, [consts, keys, values])
    sums = whole_call(
        lambda *refs: chip_sum_kernel(length, False, *refs), array(F32, *shards), [consts, keep, received]
    )
    parts = exchange(sums)
    total = whole_call(
        lambda *refs: totals_kernel(length, False, *refs), array(F32, *shards[1:]), [consts, parts]
    )
    intra, token = whole_call(
        intra_kernel, [wide, token_shape], [consts, queries, keys, values, total], cost_estimate=cost(2 * square)
    )
    near = onward(total, 2)
    nearest, far = onward(total, 1), onward(total, 3)
    folded = whole_call(
        lambda *refs: fold_forward_kernel(length, *refs), array(F32, *shards),
        [consts, parts, nearest, near, far, token],
    )
    mine, give = whole_call(
        lambda *refs: states_kernel(length, False, *refs), [states_shape, states_shape],
        [consts, exchange(folded), keep, received],
    )
    other = swap(give)
    stats_shape = (head_devices, 2 * length // SIZE, SIZE)
    mixed, stats = whole_call(
        mixed_kernel, [wide, array(F32, *stats_shape)],
        [consts, queries, mine, other, intra, cotangent], scratch_shapes=[scratch, scratch],
    )
    stats = lax.all_to_all(stats, "head", 0, 0)

    sums_shape = array(F32, heads // 2, SIZE + EXTRA, SIZE)
    shards = (CHIPS, SIZE // 2 + EXTRA, SIZE)

    def back_sums(mine):
        return whole_call(
            lambda *refs: back_sum_kernel(mine, total_channels, *refs), sums_shape,
            [consts, stats, mixed, cotangent, queries], scratch_shapes=[scratch, scratch],
        )

    received = swap(back_sums(False))
    keep = back_sums(True)
    sums = whole_call(
        lambda *refs: chip_sum_kernel(length, True, *refs), array(F32, *shards), [consts, keep, received]
    )
    parts = exchange(sums)
    groups = lax.axis_size("seq") // (2 * CHIPS)
    totals = whole_call(
        lambda *refs: totals_kernel(length, True, *refs), array(F32, groups, *shards[1:]), [consts, parts]
    )
    part = pltpu.VMEM((length, channels), F32)
    attended, query_grad, key_part, value_part, token = whole_call(
        lambda *refs: grads_kernel(total_channels, *refs), [narrow, narrow, part, part, token_shape],
        [consts, stats, hbm(mixed), cotangent, queries, keys, values, mine, other, totals],
        in_specs=[in_vmem, in_vmem, anywhere] + [in_vmem] * 6 + [anywhere],
        out_specs=[anywhere] * 2 + [in_vmem] * 3,
        scratch_shapes=[scratch, scratch, wide_rows, rows, rows, rows, dma((heads,)), dma((2 * heads,))],
        cost_estimate=cost(6 * square),
    )
    folded = whole_call(
        lambda *refs: fold_back_kernel(length, *refs), array(F32, *shards),
        [consts, parts, among_groups(totals), token],
    )
    mine, give = whole_call(
        lambda *refs: states_kernel(length, True, *refs), [sums_shape, sums_shape],
        [consts, exchange(folded), keep, received],
    )
    other = swap(give)

    def finish(is_mine, back, *begun):
        return whole_call(
            lambda *refs: finish_kernel(is_mine, *refs), [narrow, narrow, array(F32, 1, channels)],
            [consts, back, keys, values, vmem(key_part), vmem(value_part), *begun],
            in_specs=[in_vmem] * 6 + [in_vmem, anywhere, anywhere][: len(begun)],
            out_specs=[anywhere] * 2 + [in_vmem],
            scratch_shapes=[half_rows, half_rows, dma((heads,))],
            input_output_aliases={7: 0, 8: 1} if begun else {},
        )

    key_grad, value_grad, _ = finish(True, mine)
    key_grad, value_grad, gain_grad = finish(False, other, mine, key_grad, value_grad)
    return attended, query_grad, key_grad, value_grad, gain_grad.reshape(channels)


def solution(mesh):
    placed = (
        P("seq", "head"),
        P("seq", "head"),
        P("seq", "head"),
        P("head"),
        P("head"),
        P("seq", "head"),
    )
    return jax.shard_map(
        body,
        mesh=mesh,
        in_specs=placed,
        out_specs=(
            P("seq", "head"),
            P("seq", "head"),
            P("seq", "head"),
            P("seq", "head"),
            P("head"),
        ),
        check_vma=False,
    )
```

```python
import jax
import jax.numpy as jnp
from jax import lax
from jax.experimental import pallas as pl
from jax.experimental.pallas import tpu as pltpu
from jax.sharding import PartitionSpec as P

epsilon = 1e-06
F32, BF16 = jnp.float32, jnp.bfloat16
GROUP = 8
EXTRA = 8
VMEM_LIMIT = 16 * 1024 * 1024


def dot(a, b, over_a, over_b):
    return lax.dot_general(a, b, (((over_a,), (over_b,)), ((), ())), preferred_element_type=F32)


def split(x):
    high = x.astype(BF16)
    return high, (x - high.astype(F32)).astype(BF16)


def dot_split(a, x, over_a, over_x):
    parts = jnp.concatenate(split(x), axis=1 - over_x)
    both = dot(a, parts, over_a, over_x)
    return both[:, : both.shape[1] // 2] + both[:, both.shape[1] // 2 :]


def rows_of(length, width=128):
    return lax.broadcasted_iota(jnp.int32, (length, width), 0).astype(F32)


def head_in_of(rate, length):
    base = jnp.exp(-rate * (rows_of(128) + 1.0))
    return jnp.concatenate([base * jnp.exp(-rate * start) for start in range(0, length, 128)], axis=0)


def tail_out_of(rate, length):
    base = jnp.exp(-rate * (127.0 - rows_of(128)))
    return jnp.concatenate([base * jnp.exp(-rate * (length - 128 - start)) for start in range(0, length, 128)], axis=0)


def tile_weights(rate):
    rows, lanes = rows_of(128), lax.broadcasted_iota(jnp.int32, (1, 128), 1).astype(F32)
    distance = rows - lanes
    near = jnp.where(distance >= 0, jnp.exp(-rate * jnp.maximum(distance, 0.0)), 0.0)
    far = jnp.exp(-rate * (rows + 1.0)) * jnp.exp(-rate * (128 - 1.0 - lanes))
    step = jnp.exp(-rate * 128)
    farther = far * step

    def square(a, b, c, d):
        return jnp.concatenate([jnp.concatenate([a, b], axis=1), jnp.concatenate([c, d], axis=1)], axis=0)

    return square(near, jnp.zeros_like(near), far, near), square(farther, far, farther * step, farther)


def column(h, size):
    return pl.ds(h * size, size)


GAIN, RATE = 0, 1


def block_sum_kernel(rates_in, gain_in, keys, values, out, consts, rates, gain, key_rows, value_rows, arrived):
    length = keys.shape[0]
    heads = rates.shape[0]
    size = keys.shape[1] // heads
    small = [
        pltpu.make_async_copy(rates_in, rates, arrived.at[2 * heads]),
        pltpu.make_async_copy(gain_in, gain, arrived.at[2 * heads + 1]),
    ]
    copies = []
    for h in range(heads):
        cols = column(h, size)
        copies.append(
            [
                pltpu.make_async_copy(source.at[:, cols], rows.at[:, cols], arrived.at[2 * h + i])
                for i, (source, rows) in enumerate(((values, value_rows), (keys, key_rows)))
            ]
        )
        for copy in copies[-1]:
            copy.start()
        if h == 0:
            for copy in small:
                copy.start()
    for copy in small:
        copy.wait()
    for h in range(heads):
        cols = column(h, size)
        rate = jnp.full((1, size), rates[h], F32)
        consts[:, cols] = jnp.concatenate([gain[:, cols], rate, jnp.zeros((6, size), F32)], axis=0)
        tail = tail_out_of(rate, length)
        for copy in copies[h]:
            copy.wait()
        scaled = value_rows[:, cols].astype(F32) * tail
        out[pl.ds(2 * h, 2)] = dot_split(key_rows[:, cols], scaled, 0, 0).reshape(2, size // 2, size)


def weighted(a, b, t, s, weight):
    return (dot(a[t, :], b[s, :], 1, 1) * weight).astype(BF16)


def intra_kernel(consts, queries, keys, values, total, out, token):
    length = queries.shape[0]
    size = 128
    half = length // 2
    first, second = pl.ds(0, half), pl.ds(half, half)
    for h in range(queries.shape[1] // size):
        cols = column(h, size)
        same, across = tile_weights(consts[pl.ds(RATE, 1), cols])
        q, k, v = (ref.at[:, cols] for ref in (queries, keys, values))
        out[first, cols] = dot(weighted(q, k, first, first, same), v[first, :], 1, 0)
        out[second, cols] = dot(weighted(q, k, second, first, across), v[first, :], 1, 0) + dot(
            weighted(q, k, second, second, same), v[second, :], 1, 0
        )
    token[...] = jnp.zeros_like(token)


def mixed_kernel(consts, queries, state, intra, cotangent, mixed, stats, square, inner):
    length = queries.shape[0]
    size = 128
    heads = queries.shape[1] // size
    for h in range(heads):
        cols = column(h, size)
        state_in = state[pl.ds(2 * h, 2)].reshape(size, size)
        value = intra[:, cols] + head_in_of(consts[pl.ds(RATE, 1), cols], length) * dot_split(queries[:, cols], state_in, 1, 0)
        mixed[:, cols] = value
        new_square, new_inner = value * value, cotangent[:, cols].astype(F32) * consts[pl.ds(GAIN, 1), cols] * value
        if h > 0:
            new_square, new_inner = new_square + square[...], new_inner + inner[...]
        square[...] = new_square
        inner[...] = new_inner
    pieces = []
    for ref in (square, inner):
        for start in range(0, length, 128):
            pieces.append(jnp.sum(ref[pl.ds(start, 128), :].T, axis=0, keepdims=True))
    tile = jnp.concatenate(pieces, axis=0)
    stats[...] = jnp.broadcast_to(tile[None], stats.shape)


def token_scales(received, channels, inv_out, coef_out):
    total = jnp.sum(received[...], axis=0)
    chunks = total.shape[0] // 2
    inv = lax.rsqrt(total[:chunks] / channels + epsilon)
    coef = inv * inv * inv * total[chunks:] / channels
    for chunk in range(chunks):
        rows = pl.ds(chunk * 128, 128)
        inv_out[rows, :] = jnp.broadcast_to(inv[chunk : chunk + 1], (128, 128)).T
        coef_out[rows, :] = jnp.broadcast_to(coef[chunk : chunk + 1], (128, 128)).T


def mixed_grad_of(consts, cols, upstream, value, inv, coef):
    return (inv * (upstream * consts[pl.ds(GAIN, 1), cols]) - value * coef).astype(BF16)


def back_sum_kernel(channels, consts, received, mixed, cotangent, queries, sums_out, inv, coef, sums, sent):
    length = queries.shape[0]
    size = 128
    heads = queries.shape[1] // size
    token_scales(received, channels, inv, coef)
    stores = []
    for h in range(heads):
        cols = column(h, size)
        shards = pl.ds(2 * h, 2)
        upstream = cotangent[:, cols].astype(F32)
        value = mixed[:, cols]
        mixed_grad = mixed_grad_of(consts, cols, upstream, value, inv[...], coef[...])
        scaled = mixed_grad.astype(F32) * head_in_of(consts[pl.ds(RATE, 1), cols], length)
        sums[shards, pl.ds(0, size // 2), :] = dot_split(queries[:, cols], scaled, 0, 0).reshape(2, size // 2, size)
        gain_grad = jnp.sum(upstream * (value * inv[...]), axis=0, keepdims=True)
        sums[shards, pl.ds(size // 2, EXTRA), :] = jnp.broadcast_to(gain_grad[None], (2, EXTRA, size))
        stores.append(pltpu.make_async_copy(sums.at[shards], sums_out.at[shards], sent.at[h]))
        stores[-1].start()
    for store in stores:
        store.wait()


def grads_kernel(
    channels, consts, received, mixed_in, cotangent, queries, keys, values, state,
    attended_out, query_out, key_part, value_part, token,
    inv, coef, mixed, grad, attended, query_grad, arrived, sent,
):
    length = queries.shape[0]
    size = 128
    heads = queries.shape[1] // size
    half = length // 2
    first, second = pl.ds(0, half), pl.ds(half, half)
    copies, stores = [], []
    for h in range(heads):
        copies.append(pltpu.make_async_copy(mixed_in.at[:, column(h, size)], mixed.at[:, column(h, size)], arrived.at[h]))
        copies[-1].start()
    token[...] = jnp.zeros_like(token)
    token_scales(received, channels, inv, coef)
    for h in range(heads):
        cols = column(h, size)
        rate = consts[pl.ds(RATE, 1), cols]
        state_in = state[pl.ds(2 * h, 2)].reshape(size, size)
        same, across = tile_weights(rate)
        copies[h].wait()
        value = mixed[:, cols]
        attended[:, cols] = (value * inv[...] * consts[pl.ds(GAIN, 1), cols]).astype(BF16)
        grad[:, cols] = mixed_grad_of(consts, cols, cotangent[:, cols].astype(F32), value, inv[...], coef[...])
        q, k, v, g = (ref.at[:, cols] for ref in (queries, keys, values, grad))
        state_part = head_in_of(rate, length) * dot_split(g[...], state_in, 1, 1)
        upper = weighted(g, v, first, first, same)
        lower = weighted(g, v, second, first, across)
        final = weighted(g, v, second, second, same)
        query_grad[first, cols] = (dot(upper, k[first, :], 1, 0) + state_part[:half]).astype(BF16)
        query_grad[second, cols] = (
            dot(lower, k[first, :], 1, 0) + dot(final, k[second, :], 1, 0) + state_part[half:]
        ).astype(BF16)
        for i, (rows, target) in enumerate(((attended, attended_out), (query_grad, query_out))):
            stores.append(pltpu.make_async_copy(rows.at[:, cols], target.at[:, cols], sent.at[2 * h + i]))
            stores[-1].start()
        key_part[first, cols] = dot(upper, q[first, :], 0, 0) + dot(lower, q[second, :], 0, 0)
        key_part[second, cols] = dot(final, q[second, :], 0, 0)
        upper = weighted(q, k, first, first, same)
        lower = weighted(q, k, second, first, across)
        final = weighted(q, k, second, second, same)
        value_part[first, cols] = dot(upper, g[first, :], 0, 0) + dot(lower, g[second, :], 0, 0)
        value_part[second, cols] = dot(final, g[second, :], 0, 0)
    for store in stores:
        store.wait()


def finish_kernel(
    consts, back, keys, values, key_part, value_part, key_grad, value_grad, gain_grad, key_rows, value_rows, sent
):
    length = keys.shape[0]
    size = 128
    heads = keys.shape[1] // size
    half = size // 2
    copies = []
    for h in range(heads):
        cols = column(h, size)
        back_in = back[pl.ds(2 * h, 2), pl.ds(0, half), :].reshape(size, size)
        gain_grad[:, cols] = back[2 * h, pl.ds(half, 1), :]
        tail = tail_out_of(consts[pl.ds(RATE, 1), cols], length)
        key_rows[:, cols] = (key_part[:, cols] + tail * dot_split(values[:, cols], back_in, 1, 1)).astype(BF16)
        value_rows[:, cols] = (value_part[:, cols] + tail * dot_split(keys[:, cols], back_in, 1, 0)).astype(BF16)
        for i, (rows, target) in enumerate(((key_rows, key_grad), (value_rows, value_grad))):
            copy = pltpu.make_async_copy(rows.at[:, cols], target.at[:, cols], sent.at[2 * h + i])
            copy.start()
            copies.append(copy)
    for copy in copies:
        copy.wait()


def fold_factors(consts, length):
    member = lax.axis_index("seq") % GROUP
    head = member * (consts.shape[1] // 128) // GROUP
    rate = consts[pl.ds(RATE, 1), pl.ds(pl.multiple_of(head * 128, 128), 128)]
    return jnp.exp(-rate * length), jnp.exp(-rate * (length * GROUP))


def totals_kernel(length, consts, parts, token, out):
    factor, _ = fold_factors(consts, length)
    rows = parts.shape[1] - EXTRA
    total = parts[GROUP - 1, :rows]
    for k in range(GROUP - 2, -1, -1):
        total = factor * total + parts[k, :rows]
    out[:rows] = total
    out[rows:] = sum(parts[k, rows:] for k in range(GROUP))


def forward_totals_kernel(length, consts, parts, out):
    factor, _ = fold_factors(consts, length)
    total = parts[0]
    for k in range(1, GROUP):
        total = factor * total + parts[k]
    out[...] = total


def join_kernel(length, consts, total, before, out):
    _, group_factor = fold_factors(consts, length)
    out[...] = total[...] + group_factor * before[...]


def fold_forward_kernel(length, consts, parts, nearest, near, far, token, out):
    factor, group_factor = fold_factors(consts, length)
    carry = nearest[...] + near[...] + group_factor * far[...]
    for k in range(GROUP):
        out[k] = carry
        carry = factor * carry + parts[k]


def fold_back_kernel(length, consts, parts, arrived, out):
    factor, group_factor = fold_factors(consts, length)
    rows = parts.shape[1] - EXTRA
    group = lax.axis_index("seq") // GROUP
    carry = jnp.zeros((rows, parts.shape[2]), F32)
    for g in range(arrived.shape[0] - 1, 0, -1):
        carry = jnp.where(group < g, group_factor * carry + arrived[g, :rows], carry)
    extra = sum(arrived[g, rows:] for g in range(arrived.shape[0]))
    for k in range(GROUP - 1, -1, -1):
        out[k, :rows] = carry
        out[k, rows:] = extra
        carry = factor * carry + parts[k, :rows]


def whole_call(kernel, out_shape, operands, in_specs=None, out_specs=None, **rest):
    vmem = pl.BlockSpec(memory_space=pltpu.VMEM)
    if in_specs is None:
        in_specs = [vmem] * len(operands)
    if out_specs is None:
        out_specs = jax.tree.map(lambda _: vmem, out_shape)
    return pl.pallas_call(
        kernel,
        in_specs=in_specs,
        out_specs=out_specs,
        out_shape=out_shape,
        compiler_params=pltpu.CompilerParams(vmem_limit_bytes=VMEM_LIMIT),
        **rest,
    )(*operands)


def send(x, pairs):
    return lax.ppermute(x, "seq", [(a * GROUP + j, b * GROUP + j) for a, b in pairs for j in range(GROUP)])


def scan_forward(x, consts, length, beside):
    groups = lax.axis_size("seq") // GROUP
    members = [[g * GROUP + j for j in range(GROUP)] for g in range(groups)]
    parts = lax.all_to_all(x, "seq", 0, 0, axis_index_groups=members)
    one = jax.ShapeDtypeStruct(x.shape[1:], F32)
    total = whole_call(lambda *refs: forward_totals_kernel(length, *refs), one, [consts, parts])
    result, token = beside(total)
    nearest = send(total, [(0, 1)])
    total = whole_call(lambda *refs: join_kernel(length, *refs), one, [consts, total, nearest])
    near = send(total, [(1, 2), (2, 3)])
    far = send(total, [(1, 3)])
    out = whole_call(lambda *refs: fold_forward_kernel(length, *refs), like(x), [consts, parts, nearest, near, far, token])
    return lax.all_to_all(out, "seq", 0, 0, axis_index_groups=members), result


def scan_back(x, consts, length, token):
    groups = lax.axis_size("seq") // GROUP
    members = [[g * GROUP + j for j in range(GROUP)] for g in range(groups)]
    across = [[g * GROUP + j for g in range(groups)] for j in range(GROUP)]
    parts = lax.all_to_all(x, "seq", 0, 0, axis_index_groups=members)
    totals = whole_call(
        lambda *refs: totals_kernel(length, *refs), jax.ShapeDtypeStruct(x.shape[1:], F32),
        [consts, parts, token],
    )
    arrived = lax.all_gather(totals, "seq", axis_index_groups=across)
    out = whole_call(lambda *refs: fold_back_kernel(length, *refs), like(x), [consts, parts, arrived])
    return lax.all_to_all(out, "seq", 0, 0, axis_index_groups=members)


def like(x):
    return jax.ShapeDtypeStruct(x.shape, x.dtype)


def body(queries, keys, values, rates, gain, cotangent):
    length, channels = queries.shape
    heads = rates.shape[0]
    size = channels // heads
    head_devices = lax.axis_size("head")
    total_channels = channels * head_devices

    smem = pl.BlockSpec(memory_space=pltpu.SMEM)
    stats_shape = (head_devices, 2 * length // 128, 128)
    scratch = pltpu.VMEM((length, size), F32)

    def array(kind, *shape):
        return jax.ShapeDtypeStruct(shape, kind)

    square = 2 * heads * length * length * size
    wide = array(F32, length, channels)
    narrow = array(BF16, length, channels)

    hbm = lambda x: pltpu.with_memory_space_constraint(x, pltpu.HBM)
    vmem = lambda x: pltpu.with_memory_space_constraint(x, pltpu.VMEM)
    anywhere = pl.BlockSpec(memory_space=pl.ANY)
    in_vmem = pl.BlockSpec(memory_space=pltpu.VMEM)
    rows_scratch = pltpu.VMEM((length, channels), BF16)
    copies = pltpu.SemaphoreType.DMA((2 * heads,))
    sums_shape = (2 * heads, size // 2, size)
    sums, consts = whole_call(
        block_sum_kernel, [array(F32, 2 * heads, size // 2, size), array(F32, 8, channels)],
        [hbm(rates), hbm(gain.reshape(1, channels)), hbm(keys), hbm(values)], in_specs=[anywhere] * 4,
        scratch_shapes=[
            pltpu.SMEM((heads,), F32), pltpu.VMEM((1, channels), F32), rows_scratch, rows_scratch,
            pltpu.SemaphoreType.DMA((2 * heads + 2,)),
        ],
    )

    def cost(flops):
        return pl.CostEstimate(flops=flops, bytes_accessed=6 << 20, transcendentals=0)

    def beside(total):
        return whole_call(
            intra_kernel, [wide, array(F32, 8, 128)], [consts, queries, keys, values, total], cost_estimate=cost(2 * square)
        )

    state_in, intra = scan_forward(sums, consts, length, beside)
    mixed, stats = whole_call(
        mixed_kernel, [wide, array(F32, *stats_shape)],
        [consts, queries, state_in, intra, cotangent], scratch_shapes=[scratch, scratch],
    )
    received = lax.all_to_all(stats, "head", 0, 0)
    sums_shape = (2 * heads, size // 2 + EXTRA, size)
    back_sums = whole_call(
        lambda *refs: back_sum_kernel(total_channels, *refs), pltpu.HBM(sums_shape, F32),
        [consts, received, mixed, cotangent, queries], out_specs=anywhere,
        scratch_shapes=[scratch, scratch, pltpu.VMEM(sums_shape, F32), pltpu.SemaphoreType.DMA((heads,))],
    )
    part = pltpu.VMEM((length, channels), F32)
    attended, query_grad, key_part, value_part, token = whole_call(
        lambda *refs: grads_kernel(total_channels, *refs), [narrow, narrow, part, part, array(F32, 8, 128)],
        [consts, received, hbm(mixed), cotangent, queries, keys, values, state_in],
        in_specs=[in_vmem, in_vmem, anywhere] + [in_vmem] * 5,
        out_specs=[anywhere, anywhere, in_vmem, in_vmem, in_vmem],
        scratch_shapes=[
            scratch, scratch, pltpu.VMEM((length, channels), F32), rows_scratch, rows_scratch, rows_scratch, copies, copies,
        ],
        cost_estimate=cost(6 * square),
    )
    back_in = scan_back(back_sums, consts, length, token)
    key_grad, value_grad, gain_grad = whole_call(
        finish_kernel, [narrow, narrow, array(F32, 1, channels)],
        [consts, back_in, keys, values, vmem(key_part), vmem(value_part)],
        out_specs=[anywhere, anywhere, in_vmem], scratch_shapes=[rows_scratch, rows_scratch, copies],
    )
    return attended, query_grad, key_grad, value_grad, gain_grad.reshape(channels)


def solution(mesh):
    placed = (
        P("seq", "head"),
        P("seq", "head"),
        P("seq", "head"),
        P("head"),
        P("head"),
        P("seq", "head"),
    )
    return jax.shard_map(
        body,
        mesh=mesh,
        in_specs=placed,
        out_specs=(
            P("seq", "head"),
            P("seq", "head"),
            P("seq", "head"),
            P("seq", "head"),
            P("head"),
        ),
        check_vma=False,
    )
```

```python
import jax
import jax.numpy as jnp
from jax import lax
from jax.experimental import pallas as pl
from jax.experimental.pallas import tpu as pltpu
from jax.sharding import PartitionSpec as P

epsilon = 1e-06
F32, BF16 = jnp.float32, jnp.bfloat16
GROUP = 8
EXTRA = 8
VMEM_LIMIT = 16 * 1024 * 1024


def dot(a, b, over_a, over_b):
    return lax.dot_general(a, b, (((over_a,), (over_b,)), ((), ())), preferred_element_type=F32)


def split(x):
    high = x.astype(BF16)
    return high, (x - high.astype(F32)).astype(BF16)


def dot_split(a, x, over_a, over_x):
    parts = jnp.concatenate(split(x), axis=1 - over_x)
    both = dot(a, parts, over_a, over_x)
    return both[:, : both.shape[1] // 2] + both[:, both.shape[1] // 2 :]


def rows_of(length, width=128):
    return lax.broadcasted_iota(jnp.int32, (length, width), 0).astype(F32)


def head_in_of(rate, length):
    base = jnp.exp(-rate * (rows_of(128) + 1.0))
    return jnp.concatenate([base * jnp.exp(-rate * start) for start in range(0, length, 128)], axis=0)


def tail_out_of(rate, length):
    base = jnp.exp(-rate * (127.0 - rows_of(128)))
    return jnp.concatenate([base * jnp.exp(-rate * (length - 128 - start)) for start in range(0, length, 128)], axis=0)


def tile_weights(rate):
    rows, lanes = rows_of(128), lax.broadcasted_iota(jnp.int32, (1, 128), 1).astype(F32)
    distance = rows - lanes
    near = jnp.where(distance >= 0, jnp.exp(-rate * jnp.maximum(distance, 0.0)), 0.0)
    far = jnp.exp(-rate * (rows + 1.0)) * jnp.exp(-rate * (128 - 1.0 - lanes))
    step = jnp.exp(-rate * 128)
    farther = far * step

    def square(a, b, c, d):
        return jnp.concatenate([jnp.concatenate([a, b], axis=1), jnp.concatenate([c, d], axis=1)], axis=0)

    return square(near, jnp.zeros_like(near), far, near), square(farther, far, farther * step, farther)


def column(h, size):
    return pl.ds(h * size, size)


GAIN, RATE = 0, 1


def block_sum_kernel(rates_in, gain_in, keys, values, out, consts, rates, gain, key_rows, value_rows, arrived):
    length = keys.shape[0]
    heads = rates.shape[0]
    size = keys.shape[1] // heads
    small = [
        pltpu.make_async_copy(rates_in, rates, arrived.at[2 * heads]),
        pltpu.make_async_copy(gain_in, gain, arrived.at[2 * heads + 1]),
    ]
    copies = []
    for h in range(heads):
        cols = column(h, size)
        copies.append(
            [
                pltpu.make_async_copy(source.at[:, cols], rows.at[:, cols], arrived.at[2 * h + i])
                for i, (source, rows) in enumerate(((values, value_rows), (keys, key_rows)))
            ]
        )
        for copy in copies[-1]:
            copy.start()
        if h == 0:
            for copy in small:
                copy.start()
    for copy in small:
        copy.wait()
    for h in range(heads):
        cols = column(h, size)
        rate = jnp.full((1, size), rates[h], F32)
        consts[:, cols] = jnp.concatenate([gain[:, cols], rate, jnp.zeros((6, size), F32)], axis=0)
        tail = tail_out_of(rate, length)
        for copy in copies[h]:
            copy.wait()
        scaled = value_rows[:, cols].astype(F32) * tail
        out[pl.ds(2 * h, 2)] = dot_split(key_rows[:, cols], scaled, 0, 0).reshape(2, size // 2, size)


def weighted(a, b, t, s, weight):
    return (dot(a[t, :], b[s, :], 1, 1) * weight).astype(BF16)


def intra_kernel(consts, queries, keys, values, total, out, token):
    length = queries.shape[0]
    size = 128
    half = length // 2
    first, second = pl.ds(0, half), pl.ds(half, half)
    for h in range(queries.shape[1] // size):
        cols = column(h, size)
        same, across = tile_weights(consts[pl.ds(RATE, 1), cols])
        q, k, v = (ref.at[:, cols] for ref in (queries, keys, values))
        out[first, cols] = dot(weighted(q, k, first, first, same), v[first, :], 1, 0)
        out[second, cols] = dot(weighted(q, k, second, first, across), v[first, :], 1, 0) + dot(
            weighted(q, k, second, second, same), v[second, :], 1, 0
        )
    token[...] = jnp.zeros_like(token)


def mixed_kernel(consts, queries, state, intra, cotangent, mixed, stats, square, inner):
    length = queries.shape[0]
    size = 128
    heads = queries.shape[1] // size
    for h in range(heads):
        cols = column(h, size)
        state_in = state[pl.ds(2 * h, 2)].reshape(size, size)
        value = intra[:, cols] + head_in_of(consts[pl.ds(RATE, 1), cols], length) * dot_split(queries[:, cols], state_in, 1, 0)
        mixed[:, cols] = value
        new_square, new_inner = value * value, cotangent[:, cols].astype(F32) * consts[pl.ds(GAIN, 1), cols] * value
        if h > 0:
            new_square, new_inner = new_square + square[...], new_inner + inner[...]
        square[...] = new_square
        inner[...] = new_inner
    pieces = []
    for ref in (square, inner):
        for start in range(0, length, 128):
            pieces.append(jnp.sum(ref[pl.ds(start, 128), :].T, axis=0, keepdims=True))
    tile = jnp.concatenate(pieces, axis=0)
    stats[...] = jnp.broadcast_to(tile[None], stats.shape)


def token_scales(received, channels, inv_out, coef_out):
    total = jnp.sum(received[...], axis=0)
    chunks = total.shape[0] // 2
    inv = lax.rsqrt(total[:chunks] / channels + epsilon)
    coef = inv * inv * inv * total[chunks:] / channels
    for chunk in range(chunks):
        rows = pl.ds(chunk * 128, 128)
        inv_out[rows, :] = jnp.broadcast_to(inv[chunk : chunk + 1], (128, 128)).T
        coef_out[rows, :] = jnp.broadcast_to(coef[chunk : chunk + 1], (128, 128)).T


def mixed_grad_of(consts, cols, upstream, value, inv, coef):
    return (inv * (upstream * consts[pl.ds(GAIN, 1), cols]) - value * coef).astype(BF16)


def back_sum_kernel(channels, consts, received, mixed, cotangent, queries, sums_out, gains, inv, coef, sums, sent):
    length = queries.shape[0]
    size = 128
    heads = queries.shape[1] // size
    token_scales(received, channels, inv, coef)
    stores = []
    gains[...] = jnp.zeros_like(gains)
    for h in range(heads):
        cols = column(h, size)
        shards = pl.ds(2 * h, 2)
        upstream = cotangent[:, cols].astype(F32)
        value = mixed[:, cols]
        mixed_grad = mixed_grad_of(consts, cols, upstream, value, inv[...], coef[...])
        scaled = mixed_grad.astype(F32) * head_in_of(consts[pl.ds(RATE, 1), cols], length)
        sums[shards] = dot_split(queries[:, cols], scaled, 0, 0).reshape(2, size // 2, size)
        gains[pl.ds(h, 1), :] = jnp.sum(upstream * (value * inv[...]), axis=0, keepdims=True)
        stores.append(pltpu.make_async_copy(sums.at[shards], sums_out.at[shards], sent.at[h]))
        stores[-1].start()
    for store in stores:
        store.wait()


def grads_kernel(
    channels, consts, received, mixed_in, cotangent_in, queries, keys, values, state,
    attended_out, query_out, key_part, value_part, token,
    inv, coef, mixed, cotangent, grad, attended, query_grad, arrived, sent,
):
    length = queries.shape[0]
    size = 128
    heads = queries.shape[1] // size
    half = length // 2
    first, second = pl.ds(0, half), pl.ds(half, half)
    copies, stores = [], []
    for h in range(heads):
        cols = column(h, size)
        copies.append(
            [
                pltpu.make_async_copy(source.at[:, cols], rows.at[:, cols], arrived.at[2 * h + i])
                for i, (source, rows) in enumerate(((mixed_in, mixed), (cotangent_in, cotangent)))
            ]
        )
        for copy in copies[-1]:
            copy.start()
    token[...] = jnp.zeros_like(token)
    token_scales(received, channels, inv, coef)
    for h in range(heads):
        cols = column(h, size)
        rate = consts[pl.ds(RATE, 1), cols]
        state_in = state[pl.ds(2 * h, 2)].reshape(size, size)
        same, across = tile_weights(rate)
        for copy in copies[h]:
            copy.wait()
        value = mixed[:, cols]
        attended[:, cols] = (value * inv[...] * consts[pl.ds(GAIN, 1), cols]).astype(BF16)
        grad[:, cols] = mixed_grad_of(consts, cols, cotangent[:, cols].astype(F32), value, inv[...], coef[...])
        q, k, v, g = (ref.at[:, cols] for ref in (queries, keys, values, grad))
        state_part = head_in_of(rate, length) * dot_split(g[...], state_in, 1, 1)
        upper = weighted(g, v, first, first, same)
        lower = weighted(g, v, second, first, across)
        final = weighted(g, v, second, second, same)
        query_grad[first, cols] = (dot(upper, k[first, :], 1, 0) + state_part[:half]).astype(BF16)
        query_grad[second, cols] = (
            dot(lower, k[first, :], 1, 0) + dot(final, k[second, :], 1, 0) + state_part[half:]
        ).astype(BF16)
        for i, (rows, target) in enumerate(((attended, attended_out), (query_grad, query_out))):
            stores.append(pltpu.make_async_copy(rows.at[:, cols], target.at[:, cols], sent.at[2 * h + i]))
            stores[-1].start()
        key_part[first, cols] = dot(upper, q[first, :], 0, 0) + dot(lower, q[second, :], 0, 0)
        key_part[second, cols] = dot(final, q[second, :], 0, 0)
        upper = weighted(q, k, first, first, same)
        lower = weighted(q, k, second, first, across)
        final = weighted(q, k, second, second, same)
        value_part[first, cols] = dot(upper, g[first, :], 0, 0) + dot(lower, g[second, :], 0, 0)
        value_part[second, cols] = dot(final, g[second, :], 0, 0)
    for store in stores:
        store.wait()


def finish_kernel(
    consts, back, keys, values, key_part, value_part, key_grad, value_grad, gain_grad, key_rows, value_rows, sent
):
    length = keys.shape[0]
    size = 128
    heads = keys.shape[1] // size
    half = size // 2
    copies = []
    for h in range(heads):
        cols = column(h, size)
        back_in = back[pl.ds(2 * h, 2), pl.ds(0, half), :].reshape(size, size)
        gain_grad[:, cols] = sum(back[k, pl.ds(half + h, 1), :] for k in range(GROUP))
        tail = tail_out_of(consts[pl.ds(RATE, 1), cols], length)
        key_rows[:, cols] = (key_part[:, cols] + tail * dot_split(values[:, cols], back_in, 1, 1)).astype(BF16)
        value_rows[:, cols] = (value_part[:, cols] + tail * dot_split(keys[:, cols], back_in, 1, 0)).astype(BF16)
        for i, (rows, target) in enumerate(((key_rows, key_grad), (value_rows, value_grad))):
            copy = pltpu.make_async_copy(rows.at[:, cols], target.at[:, cols], sent.at[2 * h + i])
            copy.start()
            copies.append(copy)
    for copy in copies:
        copy.wait()


def fold_factors(consts, length):
    member = lax.axis_index("seq") % GROUP
    head = member * (consts.shape[1] // 128) // GROUP
    rate = consts[pl.ds(RATE, 1), pl.ds(pl.multiple_of(head * 128, 128), 128)]
    return jnp.exp(-rate * length), jnp.exp(-rate * (length * GROUP))


def totals_kernel(length, consts, parts, gains, token, out):
    factor, _ = fold_factors(consts, length)
    rows = parts.shape[1]
    total = parts[GROUP - 1]
    for k in range(GROUP - 2, -1, -1):
        total = factor * total + parts[k]
    out[:rows] = total
    out[rows:] = gains[...]


def forward_totals_kernel(length, consts, parts, out):
    factor, _ = fold_factors(consts, length)
    total = parts[0]
    for k in range(1, GROUP):
        total = factor * total + parts[k]
    out[...] = total


def join_kernel(length, consts, total, before, out):
    _, group_factor = fold_factors(consts, length)
    out[...] = total[...] + group_factor * before[...]


def fold_forward_kernel(length, consts, parts, nearest, near, far, token, out):
    factor, group_factor = fold_factors(consts, length)
    carry = nearest[...] + near[...] + group_factor * far[...]
    for k in range(GROUP):
        out[k] = carry
        carry = factor * carry + parts[k]


def fold_back_kernel(length, consts, parts, arrived, out):
    factor, group_factor = fold_factors(consts, length)
    rows = parts.shape[1]
    group = lax.axis_index("seq") // GROUP
    carry = jnp.zeros(parts.shape[1:], F32)
    for g in range(arrived.shape[0] - 1, 0, -1):
        carry = jnp.where(group < g, group_factor * carry + arrived[g, :rows], carry)
    extra = sum(arrived[g, rows:] for g in range(arrived.shape[0]))
    for k in range(GROUP - 1, -1, -1):
        out[k, :rows] = carry
        out[k, rows:] = extra
        carry = factor * carry + parts[k]


def whole_call(kernel, out_shape, operands, in_specs=None, out_specs=None, **rest):
    vmem = pl.BlockSpec(memory_space=pltpu.VMEM)
    if in_specs is None:
        in_specs = [vmem] * len(operands)
    if out_specs is None:
        out_specs = jax.tree.map(lambda _: vmem, out_shape)
    return pl.pallas_call(
        kernel,
        in_specs=in_specs,
        out_specs=out_specs,
        out_shape=out_shape,
        compiler_params=pltpu.CompilerParams(vmem_limit_bytes=VMEM_LIMIT),
        **rest,
    )(*operands)


def send(x, pairs):
    return lax.ppermute(x, "seq", [(a * GROUP + j, b * GROUP + j) for a, b in pairs for j in range(GROUP)])


def scan_forward(x, consts, length, beside):
    groups = lax.axis_size("seq") // GROUP
    members = [[g * GROUP + j for j in range(GROUP)] for g in range(groups)]
    parts = lax.all_to_all(x, "seq", 0, 0, axis_index_groups=members)
    one = jax.ShapeDtypeStruct(x.shape[1:], F32)
    total = whole_call(lambda *refs: forward_totals_kernel(length, *refs), one, [consts, parts])
    result, token = beside(total)
    nearest = send(total, [(0, 1)])
    total = whole_call(lambda *refs: join_kernel(length, *refs), one, [consts, total, nearest])
    near = send(total, [(1, 2), (2, 3)])
    far = send(total, [(1, 3)])
    out = whole_call(lambda *refs: fold_forward_kernel(length, *refs), like(x), [consts, parts, nearest, near, far, token])
    return lax.all_to_all(out, "seq", 0, 0, axis_index_groups=members), result


def scan_back(x, gains, consts, length, token):
    groups = lax.axis_size("seq") // GROUP
    members = [[g * GROUP + j for j in range(GROUP)] for g in range(groups)]
    across = [[g * GROUP + j for g in range(groups)] for j in range(GROUP)]
    parts = lax.all_to_all(x, "seq", 0, 0, axis_index_groups=members)
    totals = whole_call(
        lambda *refs: totals_kernel(length, *refs), jax.ShapeDtypeStruct((x.shape[1] + EXTRA, x.shape[2]), F32),
        [consts, parts, gains, token],
    )
    arrived = lax.all_gather(totals, "seq", axis_index_groups=across)
    out = whole_call(
        lambda *refs: fold_back_kernel(length, *refs),
        jax.ShapeDtypeStruct((GROUP,) + arrived.shape[1:], F32),
        [consts, parts, arrived],
    )
    return lax.all_to_all(out, "seq", 0, 0, axis_index_groups=members)


def like(x):
    return jax.ShapeDtypeStruct(x.shape, x.dtype)


def body(queries, keys, values, rates, gain, cotangent):
    length, channels = queries.shape
    heads = rates.shape[0]
    size = channels // heads
    head_devices = lax.axis_size("head")
    total_channels = channels * head_devices

    smem = pl.BlockSpec(memory_space=pltpu.SMEM)
    stats_shape = (head_devices, 2 * length // 128, 128)
    scratch = pltpu.VMEM((length, size), F32)

    def array(kind, *shape):
        return jax.ShapeDtypeStruct(shape, kind)

    square = 2 * heads * length * length * size
    wide = array(F32, length, channels)
    narrow = array(BF16, length, channels)

    hbm = lambda x: pltpu.with_memory_space_constraint(x, pltpu.HBM)
    vmem = lambda x: pltpu.with_memory_space_constraint(x, pltpu.VMEM)
    anywhere = pl.BlockSpec(memory_space=pl.ANY)
    in_vmem = pl.BlockSpec(memory_space=pltpu.VMEM)
    rows_scratch = pltpu.VMEM((length, channels), BF16)
    copies = pltpu.SemaphoreType.DMA((2 * heads,))
    sums_shape = (2 * heads, size // 2, size)
    sums, consts = whole_call(
        block_sum_kernel, [array(F32, 2 * heads, size // 2, size), array(F32, 8, channels)],
        [hbm(rates), hbm(gain.reshape(1, channels)), hbm(keys), hbm(values)], in_specs=[anywhere] * 4,
        scratch_shapes=[
            pltpu.SMEM((heads,), F32), pltpu.VMEM((1, channels), F32), rows_scratch, rows_scratch,
            pltpu.SemaphoreType.DMA((2 * heads + 2,)),
        ],
    )

    def cost(flops):
        return pl.CostEstimate(flops=flops, bytes_accessed=6 << 20, transcendentals=0)

    def beside(total):
        return whole_call(
            intra_kernel, [wide, array(F32, 8, 128)], [consts, queries, keys, values, total], cost_estimate=cost(2 * square)
        )

    state_in, intra = scan_forward(sums, consts, length, beside)
    mixed, stats = whole_call(
        mixed_kernel, [wide, array(F32, *stats_shape)],
        [consts, queries, state_in, intra, cotangent], scratch_shapes=[scratch, scratch],
    )
    received = lax.all_to_all(stats, "head", 0, 0)
    sums_shape = (2 * heads, size // 2, size)
    back_sums, gains = whole_call(
        lambda *refs: back_sum_kernel(total_channels, *refs), [pltpu.HBM(sums_shape, F32), array(F32, EXTRA, size)],
        [consts, received, mixed, cotangent, queries], out_specs=[anywhere, in_vmem],
        scratch_shapes=[scratch, scratch, pltpu.VMEM(sums_shape, F32), pltpu.SemaphoreType.DMA((heads,))],
    )
    part = pltpu.VMEM((length, channels), F32)
    attended, query_grad, key_part, value_part, token = whole_call(
        lambda *refs: grads_kernel(total_channels, *refs), [narrow, narrow, part, part, array(F32, 8, 128)],
        [consts, received, hbm(mixed), hbm(cotangent), queries, keys, values, state_in],
        in_specs=[in_vmem, in_vmem, anywhere, anywhere] + [in_vmem] * 4,
        out_specs=[anywhere, anywhere, in_vmem, in_vmem, in_vmem],
        scratch_shapes=[
            scratch, scratch, pltpu.VMEM((length, channels), F32), rows_scratch, rows_scratch, rows_scratch,
            rows_scratch, copies, copies,
        ],
        cost_estimate=cost(6 * square),
    )
    back_in = scan_back(back_sums, gains, consts, length, token)
    key_grad, value_grad, gain_grad = whole_call(
        finish_kernel, [narrow, narrow, array(F32, 1, channels)],
        [consts, back_in, keys, values, vmem(key_part), vmem(value_part)],
        out_specs=[anywhere, anywhere, in_vmem], scratch_shapes=[rows_scratch, rows_scratch, copies],
    )
    return attended, query_grad, key_grad, value_grad, gain_grad.reshape(channels)


def solution(mesh):
    placed = (
        P("seq", "head"),
        P("seq", "head"),
        P("seq", "head"),
        P("head"),
        P("head"),
        P("seq", "head"),
    )
    return jax.shard_map(
        body,
        mesh=mesh,
        in_specs=placed,
        out_specs=(
            P("seq", "head"),
            P("seq", "head"),
            P("seq", "head"),
            P("seq", "head"),
            P("head"),
        ),
        check_vma=False,
    )
```

```python
import jax
import jax.numpy as jnp
from jax import lax
from jax.experimental import pallas as pl
from jax.experimental.pallas import tpu as pltpu
from jax.sharding import PartitionSpec as P

epsilon = 1e-06
F32, BF16 = jnp.float32, jnp.bfloat16
GROUP = 8
EXTRA = 8
VMEM_LIMIT = 16 * 1024 * 1024


def dot(a, b, over_a, over_b):
    return lax.dot_general(a, b, (((over_a,), (over_b,)), ((), ())), preferred_element_type=F32)


def split(x):
    high = x.astype(BF16)
    return high, (x - high.astype(F32)).astype(BF16)


def dot_split(a, x, over_a, over_x):
    parts = jnp.concatenate(split(x), axis=1 - over_x)
    both = dot(a, parts, over_a, over_x)
    return both[:, : both.shape[1] // 2] + both[:, both.shape[1] // 2 :]


def rows_of(length, width=128):
    return lax.broadcasted_iota(jnp.int32, (length, width), 0).astype(F32)


def head_in_of(rate, length):
    base = jnp.exp(-rate * (rows_of(128) + 1.0))
    return jnp.concatenate([base * jnp.exp(-rate * start) for start in range(0, length, 128)], axis=0)


def tail_out_of(rate, length):
    base = jnp.exp(-rate * (127.0 - rows_of(128)))
    return jnp.concatenate([base * jnp.exp(-rate * (length - 128 - start)) for start in range(0, length, 128)], axis=0)


def tile_weights(rate):
    rows, lanes = rows_of(128), lax.broadcasted_iota(jnp.int32, (1, 128), 1).astype(F32)
    distance = rows - lanes
    near = jnp.where(distance >= 0, jnp.exp(-rate * jnp.maximum(distance, 0.0)), 0.0)
    far = jnp.exp(-rate * (rows + 1.0)) * jnp.exp(-rate * (128 - 1.0 - lanes))
    step = jnp.exp(-rate * 128)
    farther = far * step

    def square(a, b, c, d):
        return jnp.concatenate([jnp.concatenate([a, b], axis=1), jnp.concatenate([c, d], axis=1)], axis=0)

    return square(near, jnp.zeros_like(near), far, near), square(farther, far, farther * step, farther)


def column(h, size):
    return pl.ds(h * size, size)


GAIN, RATE = 0, 1


def block_sum_kernel(rates_in, gain_in, keys, values, out, consts, rates, gain, key_rows, value_rows, arrived):
    length = keys.shape[0]
    heads = rates.shape[0]
    size = keys.shape[1] // heads
    small = [
        pltpu.make_async_copy(rates_in, rates, arrived.at[2 * heads]),
        pltpu.make_async_copy(gain_in, gain, arrived.at[2 * heads + 1]),
    ]
    copies = []
    for h in range(heads):
        cols = column(h, size)
        copies.append(
            [
                pltpu.make_async_copy(source.at[:, cols], rows.at[:, cols], arrived.at[2 * h + i])
                for i, (source, rows) in enumerate(((values, value_rows), (keys, key_rows)))
            ]
        )
        for copy in copies[-1]:
            copy.start()
        if h == 0:
            for copy in small:
                copy.start()
    for copy in small:
        copy.wait()
    for h in range(heads):
        cols = column(h, size)
        rate = jnp.full((1, size), rates[h], F32)
        consts[:, cols] = jnp.concatenate([gain[:, cols], rate, jnp.zeros((6, size), F32)], axis=0)
        tail = tail_out_of(rate, length)
        for copy in copies[h]:
            copy.wait()
        scaled = value_rows[:, cols].astype(F32) * tail
        out[pl.ds(2 * h, 2)] = dot_split(key_rows[:, cols], scaled, 0, 0).reshape(2, size // 2, size)


def weighted(a, b, t, s, weight):
    return (dot(a[t, :], b[s, :], 1, 1) * weight).astype(BF16)


def intra_kernel(consts, queries, keys, values, total, out, token):
    length = queries.shape[0]
    size = 128
    half = length // 2
    first, second = pl.ds(0, half), pl.ds(half, half)
    for h in range(queries.shape[1] // size):
        cols = column(h, size)
        same, across = tile_weights(consts[pl.ds(RATE, 1), cols])
        q, k, v = (ref.at[:, cols] for ref in (queries, keys, values))
        out[first, cols] = dot(weighted(q, k, first, first, same), v[first, :], 1, 0)
        out[second, cols] = dot(weighted(q, k, second, first, across), v[first, :], 1, 0) + dot(
            weighted(q, k, second, second, same), v[second, :], 1, 0
        )
    token[...] = jnp.zeros_like(token)


def mixed_kernel(consts, queries, state, intra, cotangent, mixed, stats, square, inner):
    length = queries.shape[0]
    size = 128
    heads = queries.shape[1] // size
    for h in range(heads):
        cols = column(h, size)
        state_in = state[pl.ds(2 * h, 2)].reshape(size, size)
        value = intra[:, cols] + head_in_of(consts[pl.ds(RATE, 1), cols], length) * dot_split(queries[:, cols], state_in, 1, 0)
        mixed[:, cols] = value
        new_square, new_inner = value * value, cotangent[:, cols].astype(F32) * consts[pl.ds(GAIN, 1), cols] * value
        if h > 0:
            new_square, new_inner = new_square + square[...], new_inner + inner[...]
        square[...] = new_square
        inner[...] = new_inner
    pieces = []
    for ref in (square, inner):
        for start in range(0, length, 128):
            pieces.append(jnp.sum(ref[pl.ds(start, 128), :].T, axis=0, keepdims=True))
    tile = jnp.concatenate(pieces, axis=0)
    stats[...] = jnp.broadcast_to(tile[None], stats.shape)


def token_scales(received, channels, inv_out, coef_out):
    total = jnp.sum(received[...], axis=0)
    chunks = total.shape[0] // 2
    inv = lax.rsqrt(total[:chunks] / channels + epsilon)
    coef = inv * inv * inv * total[chunks:] / channels
    for chunk in range(chunks):
        rows = pl.ds(chunk * 128, 128)
        inv_out[rows, :] = jnp.broadcast_to(inv[chunk : chunk + 1], (128, 128)).T
        coef_out[rows, :] = jnp.broadcast_to(coef[chunk : chunk + 1], (128, 128)).T


def mixed_grad_of(consts, cols, upstream, value, inv, coef):
    return (inv * (upstream * consts[pl.ds(GAIN, 1), cols]) - value * coef).astype(BF16)


def back_sum_kernel(channels, consts, received, mixed, cotangent, queries, sums_out, gains, inv, coef, sums, sent):
    length = queries.shape[0]
    size = 128
    heads = queries.shape[1] // size
    token_scales(received, channels, inv, coef)
    stores = []
    gains[...] = jnp.zeros_like(gains)
    for h in range(heads):
        cols = column(h, size)
        shards = pl.ds(2 * h, 2)
        upstream = cotangent[:, cols].astype(F32)
        value = mixed[:, cols]
        mixed_grad = mixed_grad_of(consts, cols, upstream, value, inv[...], coef[...])
        scaled = mixed_grad.astype(F32) * head_in_of(consts[pl.ds(RATE, 1), cols], length)
        sums[shards] = dot_split(queries[:, cols], scaled, 0, 0).reshape(2, size // 2, size)
        gains[pl.ds(h, 1), :] = jnp.sum(upstream * (value * inv[...]), axis=0, keepdims=True)
        stores.append(pltpu.make_async_copy(sums.at[shards], sums_out.at[shards], sent.at[h]))
        stores[-1].start()
    for store in stores:
        store.wait()


def grads_kernel(
    channels, consts, received, mixed_in, cotangent_in, queries, keys, values, state,
    attended_out, query_out, key_part, value_part,
    inv, coef, mixed, cotangent, grad, attended, query_grad, arrived, sent,
):
    length = queries.shape[0]
    size = 128
    heads = queries.shape[1] // size
    half = length // 2
    first, second = pl.ds(0, half), pl.ds(half, half)
    copies, stores = [], []
    for h in range(heads):
        cols = column(h, size)
        copies.append(
            [
                pltpu.make_async_copy(source.at[:, cols], rows.at[:, cols], arrived.at[2 * h + i])
                for i, (source, rows) in enumerate(((mixed_in, mixed), (cotangent_in, cotangent)))
            ]
        )
        for copy in copies[-1]:
            copy.start()
    token_scales(received, channels, inv, coef)
    for h in range(heads):
        cols = column(h, size)
        rate = consts[pl.ds(RATE, 1), cols]
        state_in = state[pl.ds(2 * h, 2)].reshape(size, size)
        same, across = tile_weights(rate)
        for copy in copies[h]:
            copy.wait()
        value = mixed[:, cols]
        attended[:, cols] = (value * inv[...] * consts[pl.ds(GAIN, 1), cols]).astype(BF16)
        grad[:, cols] = mixed_grad_of(consts, cols, cotangent[:, cols].astype(F32), value, inv[...], coef[...])
        q, k, v, g = (ref.at[:, cols] for ref in (queries, keys, values, grad))
        state_part = head_in_of(rate, length) * dot_split(g[...], state_in, 1, 1)
        upper = weighted(g, v, first, first, same)
        lower = weighted(g, v, second, first, across)
        final = weighted(g, v, second, second, same)
        query_grad[first, cols] = (dot(upper, k[first, :], 1, 0) + state_part[:half]).astype(BF16)
        query_grad[second, cols] = (
            dot(lower, k[first, :], 1, 0) + dot(final, k[second, :], 1, 0) + state_part[half:]
        ).astype(BF16)
        for i, (rows, target) in enumerate(((attended, attended_out), (query_grad, query_out))):
            stores.append(pltpu.make_async_copy(rows.at[:, cols], target.at[:, cols], sent.at[2 * h + i]))
            stores[-1].start()
        key_part[first, cols] = dot(upper, q[first, :], 0, 0) + dot(lower, q[second, :], 0, 0)
        key_part[second, cols] = dot(final, q[second, :], 0, 0)
        upper = weighted(q, k, first, first, same)
        lower = weighted(q, k, second, first, across)
        final = weighted(q, k, second, second, same)
        value_part[first, cols] = dot(upper, g[first, :], 0, 0) + dot(lower, g[second, :], 0, 0)
        value_part[second, cols] = dot(final, g[second, :], 0, 0)
    for store in stores:
        store.wait()


def finish_kernel(
    consts, back, keys, values, key_part, value_part, key_grad, value_grad, gain_grad, key_rows, value_rows, sent
):
    length = keys.shape[0]
    size = 128
    heads = keys.shape[1] // size
    half = size // 2
    copies = []
    for h in range(heads):
        cols = column(h, size)
        back_in = back[pl.ds(2 * h, 2), pl.ds(0, half), :].reshape(size, size)
        gain_grad[:, cols] = sum(back[k, pl.ds(half + h, 1), :] for k in range(GROUP))
        tail = tail_out_of(consts[pl.ds(RATE, 1), cols], length)
        key_rows[:, cols] = (key_part[:, cols] + tail * dot_split(values[:, cols], back_in, 1, 1)).astype(BF16)
        value_rows[:, cols] = (value_part[:, cols] + tail * dot_split(keys[:, cols], back_in, 1, 0)).astype(BF16)
        for i, (rows, target) in enumerate(((key_rows, key_grad), (value_rows, value_grad))):
            copy = pltpu.make_async_copy(rows.at[:, cols], target.at[:, cols], sent.at[2 * h + i])
            copy.start()
            copies.append(copy)
    for copy in copies:
        copy.wait()


def fold_factors(consts, length):
    member = lax.axis_index("seq") % GROUP
    head = member * (consts.shape[1] // 128) // GROUP
    rate = consts[pl.ds(RATE, 1), pl.ds(pl.multiple_of(head * 128, 128), 128)]
    return jnp.exp(-rate * length), jnp.exp(-rate * (length * GROUP))


def totals_kernel(length, consts, parts, gains, *refs):
    out = refs[len(refs) // 2]
    factor, _ = fold_factors(consts, length)
    rows = parts.shape[1]
    total = parts[GROUP - 1]
    for k in range(GROUP - 2, -1, -1):
        total = factor * total + parts[k]
    out[:rows] = total
    out[rows:] = gains[...]


def forward_totals_kernel(length, consts, parts, out):
    factor, _ = fold_factors(consts, length)
    total = parts[0]
    for k in range(1, GROUP):
        total = factor * total + parts[k]
    out[...] = total


def join_kernel(length, consts, total, before, out):
    _, group_factor = fold_factors(consts, length)
    out[...] = total[...] + group_factor * before[...]


def fold_forward_kernel(length, consts, parts, nearest, near, far, token, out):
    factor, group_factor = fold_factors(consts, length)
    carry = nearest[...] + near[...] + group_factor * far[...]
    for k in range(GROUP):
        out[k] = carry
        carry = factor * carry + parts[k]


def fold_back_kernel(length, consts, parts, arrived, *refs):
    out = refs[len(refs) // 2]
    factor, group_factor = fold_factors(consts, length)
    rows = parts.shape[1]
    group = lax.axis_index("seq") // GROUP
    carry = jnp.zeros(parts.shape[1:], F32)
    for g in range(arrived.shape[0] - 1, 0, -1):
        carry = jnp.where(group < g, group_factor * carry + arrived[g, :rows], carry)
    extra = sum(arrived[g, rows:] for g in range(arrived.shape[0]))
    for k in range(GROUP - 1, -1, -1):
        out[k, :rows] = carry
        out[k, rows:] = extra
        carry = factor * carry + parts[k]


def whole_call(kernel, out_shape, operands, in_specs=None, out_specs=None, **rest):
    vmem = pl.BlockSpec(memory_space=pltpu.VMEM)
    if in_specs is None:
        in_specs = [vmem] * len(operands)
    if out_specs is None:
        out_specs = jax.tree.map(lambda _: vmem, out_shape)
    return pl.pallas_call(
        kernel,
        in_specs=in_specs,
        out_specs=out_specs,
        out_shape=out_shape,
        compiler_params=pltpu.CompilerParams(vmem_limit_bytes=VMEM_LIMIT),
        **rest,
    )(*operands)


def send(x, pairs):
    return lax.ppermute(x, "seq", [(a * GROUP + j, b * GROUP + j) for a, b in pairs for j in range(GROUP)])


def scan_forward(x, consts, length, beside):
    groups = lax.axis_size("seq") // GROUP
    members = [[g * GROUP + j for j in range(GROUP)] for g in range(groups)]
    parts = lax.all_to_all(x, "seq", 0, 0, axis_index_groups=members)
    one = jax.ShapeDtypeStruct(x.shape[1:], F32)
    total = whole_call(lambda *refs: forward_totals_kernel(length, *refs), one, [consts, parts])
    result, token = beside(total)
    nearest = send(total, [(0, 1)])
    total = whole_call(lambda *refs: join_kernel(length, *refs), one, [consts, total, nearest])
    near = send(total, [(1, 2), (2, 3)])
    far = send(total, [(1, 3)])
    out = whole_call(lambda *refs: fold_forward_kernel(length, *refs), like(x), [consts, parts, nearest, near, far, token])
    return lax.all_to_all(out, "seq", 0, 0, axis_index_groups=members), result


def scan_back(x, gains, consts, length, kept):
    groups = lax.axis_size("seq") // GROUP
    members = [[g * GROUP + j for j in range(GROUP)] for g in range(groups)]
    across = [[g * GROUP + j for g in range(groups)] for j in range(GROUP)]
    parts = lax.all_to_all(x, "seq", 0, 0, axis_index_groups=members)
    totals, *kept = passing(
        lambda *refs: totals_kernel(length, *refs), array(F32, x.shape[1] + EXTRA, x.shape[2]), [consts, parts, gains], kept
    )
    arrived = lax.all_gather(totals, "seq", axis_index_groups=across)
    out, *kept = passing(
        lambda *refs: fold_back_kernel(length, *refs), array(F32, GROUP, *arrived.shape[1:]), [consts, parts, arrived], kept
    )
    return lax.all_to_all(out, "seq", 0, 0, axis_index_groups=members), kept


def passing(kernel, out_shape, operands, kept):
    return whole_call(
        kernel, [out_shape] + [pltpu.VMEM(x.shape, x.dtype) for x in kept], operands + [in_vmem_space(x) for x in kept],
        input_output_aliases={len(operands) + i: 1 + i for i in range(len(kept))},
    )


def in_vmem_space(x):
    return pltpu.with_memory_space_constraint(x, pltpu.VMEM)


def array(kind, *shape):
    return jax.ShapeDtypeStruct(shape, kind)


def like(x):
    return jax.ShapeDtypeStruct(x.shape, x.dtype)


def body(queries, keys, values, rates, gain, cotangent):
    length, channels = queries.shape
    heads = rates.shape[0]
    size = channels // heads
    head_devices = lax.axis_size("head")
    total_channels = channels * head_devices

    smem = pl.BlockSpec(memory_space=pltpu.SMEM)
    stats_shape = (head_devices, 2 * length // 128, 128)
    scratch = pltpu.VMEM((length, size), F32)

    square = 2 * heads * length * length * size
    wide = array(F32, length, channels)
    narrow = array(BF16, length, channels)

    hbm = lambda x: pltpu.with_memory_space_constraint(x, pltpu.HBM)
    anywhere = pl.BlockSpec(memory_space=pl.ANY)
    in_vmem = pl.BlockSpec(memory_space=pltpu.VMEM)
    rows_scratch = pltpu.VMEM((length, channels), BF16)
    copies = pltpu.SemaphoreType.DMA((2 * heads,))
    sums_shape = (2 * heads, size // 2, size)
    sums, consts = whole_call(
        block_sum_kernel, [array(F32, 2 * heads, size // 2, size), array(F32, 8, channels)],
        [hbm(rates), hbm(gain.reshape(1, channels)), hbm(keys), hbm(values)], in_specs=[anywhere] * 4,
        scratch_shapes=[
            pltpu.SMEM((heads,), F32), pltpu.VMEM((1, channels), F32), rows_scratch, rows_scratch,
            pltpu.SemaphoreType.DMA((2 * heads + 2,)),
        ],
    )

    def cost(flops):
        return pl.CostEstimate(flops=flops, bytes_accessed=6 << 20, transcendentals=0)

    def beside(total):
        return whole_call(
            intra_kernel, [wide, array(F32, 8, 128)], [consts, queries, keys, values, total], cost_estimate=cost(2 * square)
        )

    state_in, intra = scan_forward(sums, consts, length, beside)
    mixed, stats = whole_call(
        mixed_kernel, [wide, array(F32, *stats_shape)],
        [consts, queries, state_in, intra, cotangent], scratch_shapes=[scratch, scratch],
    )
    received = lax.all_to_all(stats, "head", 0, 0)
    sums_shape = (2 * heads, size // 2, size)
    back_sums, gains = whole_call(
        lambda *refs: back_sum_kernel(total_channels, *refs), [pltpu.HBM(sums_shape, F32), array(F32, EXTRA, size)],
        [consts, received, mixed, cotangent, queries], out_specs=[anywhere, in_vmem],
        scratch_shapes=[scratch, scratch, pltpu.VMEM(sums_shape, F32), pltpu.SemaphoreType.DMA((heads,))],
    )
    part = pltpu.VMEM((length, channels), F32)
    attended, query_grad, key_part, value_part = whole_call(
        lambda *refs: grads_kernel(total_channels, *refs), [narrow, narrow, part, part],
        [consts, received, hbm(mixed), hbm(cotangent), queries, keys, values, state_in],
        in_specs=[in_vmem, in_vmem, anywhere, anywhere] + [in_vmem] * 4,
        out_specs=[anywhere, anywhere, in_vmem, in_vmem],
        scratch_shapes=[
            scratch, scratch, pltpu.VMEM((length, channels), F32), rows_scratch, rows_scratch, rows_scratch,
            rows_scratch, copies, copies,
        ],
        cost_estimate=cost(6 * square),
    )
    back_in, (key_part, value_part) = scan_back(back_sums, gains, consts, length, [key_part, value_part])
    key_grad, value_grad, gain_grad = whole_call(
        finish_kernel, [narrow, narrow, array(F32, 1, channels)],
        [consts, back_in, keys, values, in_vmem_space(key_part), in_vmem_space(value_part)],
        out_specs=[anywhere, anywhere, in_vmem], scratch_shapes=[rows_scratch, rows_scratch, copies],
    )
    return attended, query_grad, key_grad, value_grad, gain_grad.reshape(channels)


def solution(mesh):
    placed = (
        P("seq", "head"),
        P("seq", "head"),
        P("seq", "head"),
        P("head"),
        P("head"),
        P("seq", "head"),
    )
    return jax.shard_map(
        body,
        mesh=mesh,
        in_specs=placed,
        out_specs=(
            P("seq", "head"),
            P("seq", "head"),
            P("seq", "head"),
            P("seq", "head"),
            P("head"),
        ),
        check_vma=False,
    )
```

```python
import jax
import jax.numpy as jnp
from jax import lax
from jax.experimental import pallas as pl
from jax.experimental.pallas import tpu as pltpu
from jax.sharding import PartitionSpec as P

epsilon = 1e-06
F32, BF16 = jnp.float32, jnp.bfloat16
GROUP = 8
EXTRA = 8
VMEM_LIMIT = 16 * 1024 * 1024


def dot(a, b, over_a, over_b):
    return lax.dot_general(a, b, (((over_a,), (over_b,)), ((), ())), preferred_element_type=F32)


def split(x):
    high = x.astype(BF16)
    return high, (x - high.astype(F32)).astype(BF16)


def dot_split(a, x, over_a, over_x):
    parts = jnp.concatenate(split(x), axis=1 - over_x)
    both = dot(a, parts, over_a, over_x)
    return both[:, : both.shape[1] // 2] + both[:, both.shape[1] // 2 :]


def rows_of(length, width=128):
    return lax.broadcasted_iota(jnp.int32, (length, width), 0).astype(F32)


def head_in_of(rate, length):
    base = jnp.exp(-rate * (rows_of(128) + 1.0))
    return jnp.concatenate([base * jnp.exp(-rate * start) for start in range(0, length, 128)], axis=0)


def tail_out_of(rate, length):
    base = jnp.exp(-rate * (127.0 - rows_of(128)))
    return jnp.concatenate([base * jnp.exp(-rate * (length - 128 - start)) for start in range(0, length, 128)], axis=0)


def tile_weights(rate):
    rows, lanes = rows_of(128), lax.broadcasted_iota(jnp.int32, (1, 128), 1).astype(F32)
    distance = rows - lanes
    near = jnp.where(distance >= 0, jnp.exp(-rate * jnp.maximum(distance, 0.0)), 0.0)
    far = jnp.exp(-rate * (rows + 1.0)) * jnp.exp(-rate * (128 - 1.0 - lanes))
    step = jnp.exp(-rate * 128)
    farther = far * step

    def square(a, b, c, d):
        return jnp.concatenate([jnp.concatenate([a, b], axis=1), jnp.concatenate([c, d], axis=1)], axis=0)

    return square(near, jnp.zeros_like(near), far, near), square(farther, far, farther * step, farther)


def column(h, size):
    return pl.ds(h * size, size)


GAIN, RATE = 0, 1


def block_sum_kernel(rates_in, gain_in, keys, values, out, consts, rates, gain, key_rows, value_rows, arrived):
    length = keys.shape[0]
    heads = rates.shape[0]
    size = keys.shape[1] // heads
    small = [
        pltpu.make_async_copy(rates_in, rates, arrived.at[2 * heads]),
        pltpu.make_async_copy(gain_in, gain, arrived.at[2 * heads + 1]),
    ]
    copies = []
    for h in range(heads):
        cols = column(h, size)
        copies.append(
            [
                pltpu.make_async_copy(source.at[:, cols], rows.at[:, cols], arrived.at[2 * h + i])
                for i, (source, rows) in enumerate(((values, value_rows), (keys, key_rows)))
            ]
        )
        for copy in copies[-1]:
            copy.start()
        if h == 0:
            for copy in small:
                copy.start()
    for copy in small:
        copy.wait()
    for h in range(heads):
        cols = column(h, size)
        rate = jnp.full((1, size), rates[h], F32)
        consts[:, cols] = jnp.concatenate([gain[:, cols], rate, jnp.zeros((6, size), F32)], axis=0)
        tail = tail_out_of(rate, length)
        for copy in copies[h]:
            copy.wait()
        scaled = value_rows[:, cols].astype(F32) * tail
        out[pl.ds(2 * h, 2)] = dot_split(key_rows[:, cols], scaled, 0, 0).reshape(2, size // 2, size)


def weighted(a, b, t, s, weight):
    return (dot(a[t, :], b[s, :], 1, 1) * weight).astype(BF16)


def intra_kernel(consts, queries, keys, values, total, out, total_out):
    length = queries.shape[0]
    size = 128
    half = length // 2
    first, second = pl.ds(0, half), pl.ds(half, half)
    for h in range(queries.shape[1] // size):
        cols = column(h, size)
        same, across = tile_weights(consts[pl.ds(RATE, 1), cols])
        q, k, v = (ref.at[:, cols] for ref in (queries, keys, values))
        out[first, cols] = dot(weighted(q, k, first, first, same), v[first, :], 1, 0)
        out[second, cols] = dot(weighted(q, k, second, first, across), v[first, :], 1, 0) + dot(
            weighted(q, k, second, second, same), v[second, :], 1, 0
        )
    total_out[...] = total[...]


def mixed_kernel(consts, queries, state, intra, cotangent, mixed, stats, square, inner):
    length = queries.shape[0]
    size = 128
    heads = queries.shape[1] // size
    for h in range(heads):
        cols = column(h, size)
        state_in = state[pl.ds(2 * h, 2)].reshape(size, size)
        value = intra[:, cols] + head_in_of(consts[pl.ds(RATE, 1), cols], length) * dot_split(queries[:, cols], state_in, 1, 0)
        mixed[:, cols] = value
        new_square, new_inner = value * value, cotangent[:, cols].astype(F32) * consts[pl.ds(GAIN, 1), cols] * value
        if h > 0:
            new_square, new_inner = new_square + square[...], new_inner + inner[...]
        square[...] = new_square
        inner[...] = new_inner
    pieces = []
    for ref in (square, inner):
        for start in range(0, length, 128):
            pieces.append(jnp.sum(ref[pl.ds(start, 128), :].T, axis=0, keepdims=True))
    tile = jnp.concatenate(pieces, axis=0)
    stats[...] = jnp.broadcast_to(tile[None], stats.shape)


def token_scales(received, channels, inv_out, coef_out):
    total = jnp.sum(received[...], axis=0)
    chunks = total.shape[0] // 2
    inv = lax.rsqrt(total[:chunks] / channels + epsilon)
    coef = inv * inv * inv * total[chunks:] / channels
    for chunk in range(chunks):
        rows = pl.ds(chunk * 128, 128)
        inv_out[rows, :] = jnp.broadcast_to(inv[chunk : chunk + 1], (128, 128)).T
        coef_out[rows, :] = jnp.broadcast_to(coef[chunk : chunk + 1], (128, 128)).T


def mixed_grad_of(consts, cols, upstream, value, inv, coef):
    return (inv * (upstream * consts[pl.ds(GAIN, 1), cols]) - value * coef).astype(BF16)


def back_sum_kernel(channels, consts, received, mixed, cotangent, queries, sums_out, gains, inv, coef, sums, sent):
    length = queries.shape[0]
    size = 128
    heads = queries.shape[1] // size
    token_scales(received, channels, inv, coef)
    stores = []
    gains[...] = jnp.zeros_like(gains)
    for h in range(heads):
        cols = column(h, size)
        shards = pl.ds(2 * h, 2)
        upstream = cotangent[:, cols].astype(F32)
        value = mixed[:, cols]
        mixed_grad = mixed_grad_of(consts, cols, upstream, value, inv[...], coef[...])
        scaled = mixed_grad.astype(F32) * head_in_of(consts[pl.ds(RATE, 1), cols], length)
        sums[shards] = dot_split(queries[:, cols], scaled, 0, 0).reshape(2, size // 2, size)
        gains[pl.ds(h, 1), :] = jnp.sum(upstream * (value * inv[...]), axis=0, keepdims=True)
        stores.append(pltpu.make_async_copy(sums.at[shards], sums_out.at[shards], sent.at[h]))
        stores[-1].start()
    for store in stores:
        store.wait()


def grads_kernel(
    channels, consts, received, mixed_in, cotangent_in, queries_in, keys_in, values_in, state,
    attended_out, query_out, key_part, value_part,
    inv, coef, mixed, cotangent, queries, keys, values, grad, attended, query_grad, arrived, sent,
):
    length = queries.shape[0]
    size = 128
    heads = queries.shape[1] // size
    half = length // 2
    first, second = pl.ds(0, half), pl.ds(half, half)
    copies, stores = [], []
    for h in range(heads):
        cols = column(h, size)
        copies.append(
            [
                pltpu.make_async_copy(source.at[:, cols], rows.at[:, cols], arrived.at[5 * h + i])
                for i, (source, rows) in enumerate(
                    (
                        (mixed_in, mixed),
                        (cotangent_in, cotangent),
                        (values_in, values),
                        (keys_in, keys),
                        (queries_in, queries),
                    )
                )
            ]
        )
        for copy in copies[-1]:
            copy.start()
    token_scales(received, channels, inv, coef)
    for h in range(heads):
        cols = column(h, size)
        rate = consts[pl.ds(RATE, 1), cols]
        state_in = state[pl.ds(2 * h, 2)].reshape(size, size)
        same, across = tile_weights(rate)
        for copy in copies[h]:
            copy.wait()
        value = mixed[:, cols]
        attended[:, cols] = (value * inv[...] * consts[pl.ds(GAIN, 1), cols]).astype(BF16)
        grad[:, cols] = mixed_grad_of(consts, cols, cotangent[:, cols].astype(F32), value, inv[...], coef[...])
        q, k, v, g = (ref.at[:, cols] for ref in (queries, keys, values, grad))
        state_part = head_in_of(rate, length) * dot_split(g[...], state_in, 1, 1)
        upper = weighted(g, v, first, first, same)
        lower = weighted(g, v, second, first, across)
        final = weighted(g, v, second, second, same)
        query_grad[first, cols] = (dot(upper, k[first, :], 1, 0) + state_part[:half]).astype(BF16)
        query_grad[second, cols] = (
            dot(lower, k[first, :], 1, 0) + dot(final, k[second, :], 1, 0) + state_part[half:]
        ).astype(BF16)
        for i, (rows, target) in enumerate(((attended, attended_out), (query_grad, query_out))):
            stores.append(pltpu.make_async_copy(rows.at[:, cols], target.at[:, cols], sent.at[2 * h + i]))
            stores[-1].start()
        key_part[first, cols] = dot(upper, q[first, :], 0, 0) + dot(lower, q[second, :], 0, 0)
        key_part[second, cols] = dot(final, q[second, :], 0, 0)
        upper = weighted(q, k, first, first, same)
        lower = weighted(q, k, second, first, across)
        final = weighted(q, k, second, second, same)
        value_part[first, cols] = dot(upper, g[first, :], 0, 0) + dot(lower, g[second, :], 0, 0)
        value_part[second, cols] = dot(final, g[second, :], 0, 0)
    for store in stores:
        store.wait()


def finish_kernel(
    consts, back, keys, values, key_part, value_part, key_grad, value_grad, gain_grad, key_rows, value_rows, sent
):
    length = keys.shape[0]
    size = 128
    heads = keys.shape[1] // size
    half = size // 2
    copies = []
    for h in range(heads):
        cols = column(h, size)
        back_in = back[pl.ds(2 * h, 2), pl.ds(0, half), :].reshape(size, size)
        gain_grad[:, cols] = sum(back[k, pl.ds(half + h, 1), :] for k in range(GROUP))
        tail = tail_out_of(consts[pl.ds(RATE, 1), cols], length)
        key_rows[:, cols] = (key_part[:, cols] + tail * dot_split(values[:, cols], back_in, 1, 1)).astype(BF16)
        value_rows[:, cols] = (value_part[:, cols] + tail * dot_split(keys[:, cols], back_in, 1, 0)).astype(BF16)
        for i, (rows, target) in enumerate(((key_rows, key_grad), (value_rows, value_grad))):
            copy = pltpu.make_async_copy(rows.at[:, cols], target.at[:, cols], sent.at[2 * h + i])
            copy.start()
            copies.append(copy)
    for copy in copies:
        copy.wait()


def fold_factors(consts, length):
    member = lax.axis_index("seq") % GROUP
    head = member * (consts.shape[1] // 128) // GROUP
    rate = consts[pl.ds(RATE, 1), pl.ds(pl.multiple_of(head * 128, 128), 128)]
    return jnp.exp(-rate * length), jnp.exp(-rate * (length * GROUP))


def totals_kernel(length, consts, parts, gains, *refs):
    out = refs[len(refs) // 2]
    factor, _ = fold_factors(consts, length)
    rows = parts.shape[1]
    total = parts[GROUP - 1]
    for k in range(GROUP - 2, -1, -1):
        total = factor * total + parts[k]
    out[:rows] = total
    out[rows:] = gains[...]


def forward_totals_kernel(length, consts, parts, out):
    factor, _ = fold_factors(consts, length)
    total = parts[0]
    for k in range(1, GROUP):
        total = factor * total + parts[k]
    out[...] = total


def join_kernel(length, consts, total, before, out):
    _, group_factor = fold_factors(consts, length)
    out[...] = total[...] + group_factor * before[...]


def fold_forward_kernel(length, consts, parts, nearest, near, far, out):
    factor, group_factor = fold_factors(consts, length)
    carry = nearest[...] + near[...] + group_factor * far[...]
    for k in range(GROUP):
        out[k] = carry
        carry = factor * carry + parts[k]


def fold_back_kernel(length, consts, parts, arrived, *refs):
    out = refs[len(refs) // 2]
    factor, group_factor = fold_factors(consts, length)
    rows = parts.shape[1]
    group = lax.axis_index("seq") // GROUP
    carry = jnp.zeros(parts.shape[1:], F32)
    for g in range(arrived.shape[0] - 1, 0, -1):
        carry = jnp.where(group < g, group_factor * carry + arrived[g, :rows], carry)
    extra = sum(arrived[g, rows:] for g in range(arrived.shape[0]))
    for k in range(GROUP - 1, -1, -1):
        out[k, :rows] = carry
        out[k, rows:] = extra
        carry = factor * carry + parts[k]


def whole_call(kernel, out_shape, operands, in_specs=None, out_specs=None, **rest):
    vmem = pl.BlockSpec(memory_space=pltpu.VMEM)
    if in_specs is None:
        in_specs = [vmem] * len(operands)
    if out_specs is None:
        out_specs = jax.tree.map(lambda _: vmem, out_shape)
    return pl.pallas_call(
        kernel,
        in_specs=in_specs,
        out_specs=out_specs,
        out_shape=out_shape,
        compiler_params=pltpu.CompilerParams(vmem_limit_bytes=VMEM_LIMIT),
        **rest,
    )(*operands)


def send(x, pairs):
    return lax.ppermute(x, "seq", [(a * GROUP + j, b * GROUP + j) for a, b in pairs for j in range(GROUP)])


def scan_forward(x, consts, length, beside):
    groups = lax.axis_size("seq") // GROUP
    members = [[g * GROUP + j for j in range(GROUP)] for g in range(groups)]
    parts = lax.all_to_all(x, "seq", 0, 0, axis_index_groups=members)
    one = jax.ShapeDtypeStruct(x.shape[1:], F32)
    total = whole_call(lambda *refs: forward_totals_kernel(length, *refs), one, [consts, parts])
    nearest = send(total, [(0, 1)])
    total = whole_call(lambda *refs: join_kernel(length, *refs), one, [consts, total, nearest])
    near = send(total, [(1, 2), (2, 3)])
    result, total = beside(total)
    far = send(total, [(1, 3)])
    out = whole_call(lambda *refs: fold_forward_kernel(length, *refs), like(x), [consts, parts, nearest, near, far])
    return lax.all_to_all(out, "seq", 0, 0, axis_index_groups=members), result


def scan_back(x, gains, consts, length, kept):
    groups = lax.axis_size("seq") // GROUP
    members = [[g * GROUP + j for j in range(GROUP)] for g in range(groups)]
    across = [[g * GROUP + j for g in range(groups)] for j in range(GROUP)]
    parts = lax.all_to_all(x, "seq", 0, 0, axis_index_groups=members)
    totals, *kept = passing(
        lambda *refs: totals_kernel(length, *refs), array(F32, x.shape[1] + EXTRA, x.shape[2]), [consts, parts, gains], kept
    )
    arrived = lax.all_gather(totals, "seq", axis_index_groups=across)
    out, *kept = passing(
        lambda *refs: fold_back_kernel(length, *refs), array(F32, GROUP, *arrived.shape[1:]), [consts, parts, arrived], kept
    )
    return lax.all_to_all(out, "seq", 0, 0, axis_index_groups=members), kept


def passing(kernel, out_shape, operands, kept):
    return whole_call(
        kernel, [out_shape] + [pltpu.VMEM(x.shape, x.dtype) for x in kept], operands + [in_vmem_space(x) for x in kept],
        input_output_aliases={len(operands) + i: 1 + i for i in range(len(kept))},
    )


def in_vmem_space(x):
    return pltpu.with_memory_space_constraint(x, pltpu.VMEM)


def array(kind, *shape):
    return jax.ShapeDtypeStruct(shape, kind)


def like(x):
    return jax.ShapeDtypeStruct(x.shape, x.dtype)


def body(queries, keys, values, rates, gain, cotangent):
    length, channels = queries.shape
    heads = rates.shape[0]
    size = channels // heads
    head_devices = lax.axis_size("head")
    total_channels = channels * head_devices

    smem = pl.BlockSpec(memory_space=pltpu.SMEM)
    stats_shape = (head_devices, 2 * length // 128, 128)
    scratch = pltpu.VMEM((length, size), F32)

    square = 2 * heads * length * length * size
    wide = array(F32, length, channels)
    narrow = array(BF16, length, channels)

    hbm = lambda x: pltpu.with_memory_space_constraint(x, pltpu.HBM)
    anywhere = pl.BlockSpec(memory_space=pl.ANY)
    in_vmem = pl.BlockSpec(memory_space=pltpu.VMEM)
    rows_scratch = pltpu.VMEM((length, channels), BF16)
    copies = pltpu.SemaphoreType.DMA((2 * heads,))
    sums_shape = (2 * heads, size // 2, size)
    sums, consts = whole_call(
        block_sum_kernel, [array(F32, 2 * heads, size // 2, size), array(F32, 8, channels)],
        [hbm(rates), hbm(gain.reshape(1, channels)), hbm(keys), hbm(values)], in_specs=[anywhere] * 4,
        scratch_shapes=[
            pltpu.SMEM((heads,), F32), pltpu.VMEM((1, channels), F32), rows_scratch, rows_scratch,
            pltpu.SemaphoreType.DMA((2 * heads + 2,)),
        ],
    )

    def cost(flops):
        return pl.CostEstimate(flops=flops, bytes_accessed=6 << 20, transcendentals=0)

    def beside(total):
        return whole_call(
            intra_kernel, [wide, array(F32, *total.shape)], [consts, queries, keys, values, total], cost_estimate=cost(2 * square)
        )

    state_in, intra = scan_forward(sums, consts, length, beside)
    mixed, stats = whole_call(
        mixed_kernel, [wide, array(F32, *stats_shape)],
        [consts, queries, state_in, intra, cotangent], scratch_shapes=[scratch, scratch],
    )
    received = lax.all_to_all(stats, "head", 0, 0)
    sums_shape = (2 * heads, size // 2, size)
    back_sums, gains = whole_call(
        lambda *refs: back_sum_kernel(total_channels, *refs), [pltpu.HBM(sums_shape, F32), array(F32, EXTRA, size)],
        [consts, received, mixed, cotangent, queries], out_specs=[anywhere, in_vmem],
        scratch_shapes=[scratch, scratch, pltpu.VMEM(sums_shape, F32), pltpu.SemaphoreType.DMA((heads,))],
    )
    part = pltpu.VMEM((length, channels), F32)
    attended, query_grad, key_part, value_part = whole_call(
        lambda *refs: grads_kernel(total_channels, *refs), [narrow, narrow, part, part],
        [consts, received, hbm(mixed), hbm(cotangent), hbm(queries), hbm(keys), hbm(values), state_in],
        in_specs=[in_vmem] * 2 + [anywhere] * 5 + [in_vmem],
        out_specs=[anywhere, anywhere, in_vmem, in_vmem],
        scratch_shapes=[
            scratch, scratch, pltpu.VMEM((length, channels), F32), rows_scratch, rows_scratch, rows_scratch,
            rows_scratch, rows_scratch, rows_scratch, rows_scratch, pltpu.SemaphoreType.DMA((5 * heads,)), copies,
        ],
        cost_estimate=cost(6 * square),
    )
    back_in, (key_part, value_part) = scan_back(back_sums, gains, consts, length, [key_part, value_part])
    key_grad, value_grad, gain_grad = whole_call(
        finish_kernel, [narrow, narrow, array(F32, 1, channels)],
        [consts, back_in, keys, values, in_vmem_space(key_part), in_vmem_space(value_part)],
        out_specs=[anywhere, anywhere, in_vmem], scratch_shapes=[rows_scratch, rows_scratch, copies],
    )
    return attended, query_grad, key_grad, value_grad, gain_grad.reshape(channels)


def solution(mesh):
    placed = (
        P("seq", "head"),
        P("seq", "head"),
        P("seq", "head"),
        P("head"),
        P("head"),
        P("seq", "head"),
    )
    return jax.shard_map(
        body,
        mesh=mesh,
        in_specs=placed,
        out_specs=(
            P("seq", "head"),
            P("seq", "head"),
            P("seq", "head"),
            P("seq", "head"),
            P("head"),
        ),
        check_vma=False,
    )
```

```python
import jax
import jax.numpy as jnp
from jax import lax
from jax.experimental import pallas as pl
from jax.experimental.pallas import tpu as pltpu
from jax.sharding import PartitionSpec as P

epsilon = 1e-06
F32, BF16 = jnp.float32, jnp.bfloat16
GROUP = 8
EXTRA = 8
VMEM_LIMIT = 16 * 1024 * 1024


def dot(a, b, over_a, over_b):
    return lax.dot_general(a, b, (((over_a,), (over_b,)), ((), ())), preferred_element_type=F32)


def split(x):
    high = x.astype(BF16)
    return high, (x - high.astype(F32)).astype(BF16)


def dot_split(a, x, over_a, over_x):
    parts = jnp.concatenate(split(x), axis=1 - over_x)
    both = dot(a, parts, over_a, over_x)
    return both[:, : both.shape[1] // 2] + both[:, both.shape[1] // 2 :]


def rows_of(length, width=128):
    return lax.broadcasted_iota(jnp.int32, (length, width), 0).astype(F32)


def head_in_of(rate, length):
    base = jnp.exp(-rate * (rows_of(128) + 1.0))
    return jnp.concatenate([base * jnp.exp(-rate * start) for start in range(0, length, 128)], axis=0)


def tail_out_of(rate, length):
    base = jnp.exp(-rate * (127.0 - rows_of(128)))
    return jnp.concatenate([base * jnp.exp(-rate * (length - 128 - start)) for start in range(0, length, 128)], axis=0)


def tile_weights(rate):
    rows, lanes = rows_of(128), lax.broadcasted_iota(jnp.int32, (1, 128), 1).astype(F32)
    distance = rows - lanes
    near = jnp.where(distance >= 0, jnp.exp(-rate * jnp.maximum(distance, 0.0)), 0.0)
    far = jnp.exp(-rate * (rows + 1.0)) * jnp.exp(-rate * (128 - 1.0 - lanes))
    step = jnp.exp(-rate * 128)
    farther = far * step

    def square(a, b, c, d):
        return jnp.concatenate([jnp.concatenate([a, b], axis=1), jnp.concatenate([c, d], axis=1)], axis=0)

    return square(near, jnp.zeros_like(near), far, near), square(farther, far, farther * step, farther)


def column(h, size):
    return pl.ds(h * size, size)


GAIN, RATE = 0, 1


def block_sum_kernel(rates_in, gain_in, keys, values, out, consts, rates, gain, key_rows, value_rows, arrived):
    length = keys.shape[0]
    heads = rates.shape[0]
    size = keys.shape[1] // heads
    small = [
        pltpu.make_async_copy(rates_in, rates, arrived.at[2 * heads]),
        pltpu.make_async_copy(gain_in, gain, arrived.at[2 * heads + 1]),
    ]
    copies = []
    for h in range(heads):
        cols = column(h, size)
        copies.append(
            [
                pltpu.make_async_copy(source.at[:, cols], rows.at[:, cols], arrived.at[2 * h + i])
                for i, (source, rows) in enumerate(((values, value_rows), (keys, key_rows)))
            ]
        )
        for copy in copies[-1]:
            copy.start()
        if h == 0:
            for copy in small:
                copy.start()
    for copy in small:
        copy.wait()
    for h in range(heads):
        cols = column(h, size)
        rate = jnp.full((1, size), rates[h], F32)
        consts[:, cols] = jnp.concatenate([gain[:, cols], rate, jnp.zeros((6, size), F32)], axis=0)
        tail = tail_out_of(rate, length)
        for copy in copies[h]:
            copy.wait()
        scaled = value_rows[:, cols].astype(F32) * tail
        out[pl.ds(2 * h, 2)] = dot_split(key_rows[:, cols], scaled, 0, 0).reshape(2, size // 2, size)


def weighted(a, b, t, s, weight):
    return (dot(a[t, :], b[s, :], 1, 1) * weight).astype(BF16)


def intra_kernel(consts, queries, keys, values, total, out, token):
    length = queries.shape[0]
    size = 128
    half = length // 2
    first, second = pl.ds(0, half), pl.ds(half, half)
    for h in range(queries.shape[1] // size):
        cols = column(h, size)
        same, across = tile_weights(consts[pl.ds(RATE, 1), cols])
        q, k, v = (ref.at[:, cols] for ref in (queries, keys, values))
        out[first, cols] = dot(weighted(q, k, first, first, same), v[first, :], 1, 0)
        out[second, cols] = dot(weighted(q, k, second, first, across), v[first, :], 1, 0) + dot(
            weighted(q, k, second, second, same), v[second, :], 1, 0
        )
    token[...] = jnp.zeros_like(token)


def mixed_kernel(consts, queries, state, intra, cotangent, mixed, stats, square, inner):
    length = queries.shape[0]
    size = 128
    heads = queries.shape[1] // size
    for h in range(heads):
        cols = column(h, size)
        state_in = state[pl.ds(2 * h, 2)].reshape(size, size)
        value = intra[:, cols] + head_in_of(consts[pl.ds(RATE, 1), cols], length) * dot_split(queries[:, cols], state_in, 1, 0)
        mixed[:, cols] = value
        new_square, new_inner = value * value, cotangent[:, cols].astype(F32) * consts[pl.ds(GAIN, 1), cols] * value
        if h > 0:
            new_square, new_inner = new_square + square[...], new_inner + inner[...]
        square[...] = new_square
        inner[...] = new_inner
    pieces = []
    for ref in (square, inner):
        for start in range(0, length, 128):
            pieces.append(jnp.sum(ref[pl.ds(start, 128), :].T, axis=0, keepdims=True))
    tile = jnp.concatenate(pieces, axis=0)
    stats[...] = jnp.broadcast_to(tile[None], stats.shape)


def token_scales(received, channels, inv_out, coef_out):
    total = jnp.sum(received[...], axis=0)
    chunks = total.shape[0] // 2
    inv = lax.rsqrt(total[:chunks] / channels + epsilon)
    coef = inv * inv * inv * total[chunks:] / channels
    for chunk in range(chunks):
        rows = pl.ds(chunk * 128, 128)
        inv_out[rows, :] = jnp.broadcast_to(inv[chunk : chunk + 1], (128, 128)).T
        coef_out[rows, :] = jnp.broadcast_to(coef[chunk : chunk + 1], (128, 128)).T


def mixed_grad_of(consts, cols, upstream, value, inv, coef):
    return (inv * (upstream * consts[pl.ds(GAIN, 1), cols]) - value * coef).astype(BF16)


def back_sum_kernel(channels, consts, received, mixed, cotangent, queries, sums_out, gains, inv, coef, sums, sent):
    length = queries.shape[0]
    size = 128
    heads = queries.shape[1] // size
    token_scales(received, channels, inv, coef)
    stores = []
    gains[...] = jnp.zeros_like(gains)
    for h in range(heads):
        cols = column(h, size)
        shards = pl.ds(2 * h, 2)
        upstream = cotangent[:, cols].astype(F32)
        value = mixed[:, cols]
        mixed_grad = mixed_grad_of(consts, cols, upstream, value, inv[...], coef[...])
        scaled = mixed_grad.astype(F32) * head_in_of(consts[pl.ds(RATE, 1), cols], length)
        sums[shards] = dot_split(queries[:, cols], scaled, 0, 0).reshape(2, size // 2, size)
        gains[pl.ds(h, 1), :] = jnp.sum(upstream * (value * inv[...]), axis=0, keepdims=True)
        stores.append(pltpu.make_async_copy(sums.at[shards], sums_out.at[shards], sent.at[h]))
        stores[-1].start()
    for store in stores:
        store.wait()


def grads_kernel(
    channels, consts, received, mixed_in, cotangent_in, queries_in, keys_in, values_in, state,
    attended_out, query_out, key_part, value_part,
    inv, coef, mixed, cotangent, queries, keys, values, grad, attended, query_grad, arrived, sent,
):
    length = queries.shape[0]
    size = 128
    heads = queries.shape[1] // size
    half = length // 2
    first, second = pl.ds(0, half), pl.ds(half, half)
    copies, stores = [], []
    for h in range(heads):
        cols = column(h, size)
        copies.append(
            [
                pltpu.make_async_copy(source.at[:, cols], rows.at[:, cols], arrived.at[5 * h + i])
                for i, (source, rows) in enumerate(
                    (
                        (mixed_in, mixed),
                        (cotangent_in, cotangent),
                        (values_in, values),
                        (keys_in, keys),
                        (queries_in, queries),
                    )
                )
            ]
        )
        for copy in copies[-1]:
            copy.start()
    token_scales(received, channels, inv, coef)
    for h in range(heads):
        cols = column(h, size)
        rate = consts[pl.ds(RATE, 1), cols]
        state_in = state[pl.ds(2 * h, 2)].reshape(size, size)
        same, across = tile_weights(rate)
        for copy in copies[h]:
            copy.wait()
        value = mixed[:, cols]
        attended[:, cols] = (value * inv[...] * consts[pl.ds(GAIN, 1), cols]).astype(BF16)
        grad[:, cols] = mixed_grad_of(consts, cols, cotangent[:, cols].astype(F32), value, inv[...], coef[...])
        q, k, v, g = (ref.at[:, cols] for ref in (queries, keys, values, grad))
        state_part = head_in_of(rate, length) * dot_split(g[...], state_in, 1, 1)
        upper = weighted(g, v, first, first, same)
        lower = weighted(g, v, second, first, across)
        final = weighted(g, v, second, second, same)
        query_grad[first, cols] = (dot(upper, k[first, :], 1, 0) + state_part[:half]).astype(BF16)
        query_grad[second, cols] = (
            dot(lower, k[first, :], 1, 0) + dot(final, k[second, :], 1, 0) + state_part[half:]
        ).astype(BF16)
        for i, (rows, target) in enumerate(((attended, attended_out), (query_grad, query_out))):
            stores.append(pltpu.make_async_copy(rows.at[:, cols], target.at[:, cols], sent.at[2 * h + i]))
            stores[-1].start()
        key_part[first, cols] = dot(upper, q[first, :], 0, 0) + dot(lower, q[second, :], 0, 0)
        key_part[second, cols] = dot(final, q[second, :], 0, 0)
        upper = weighted(q, k, first, first, same)
        lower = weighted(q, k, second, first, across)
        final = weighted(q, k, second, second, same)
        value_part[first, cols] = dot(upper, g[first, :], 0, 0) + dot(lower, g[second, :], 0, 0)
        value_part[second, cols] = dot(final, g[second, :], 0, 0)
    for store in stores:
        store.wait()


def finish_kernel(
    consts, back, keys, values, key_part, value_part, key_grad, value_grad, gain_grad, key_rows, value_rows, sent
):
    length = keys.shape[0]
    size = 128
    heads = keys.shape[1] // size
    half = size // 2
    copies = []
    for h in range(heads):
        cols = column(h, size)
        back_in = back[pl.ds(2 * h, 2), pl.ds(0, half), :].reshape(size, size)
        gain_grad[:, cols] = sum(back[k, pl.ds(half + h, 1), :] for k in range(GROUP))
        tail = tail_out_of(consts[pl.ds(RATE, 1), cols], length)
        key_rows[:, cols] = (key_part[:, cols] + tail * dot_split(values[:, cols], back_in, 1, 1)).astype(BF16)
        value_rows[:, cols] = (value_part[:, cols] + tail * dot_split(keys[:, cols], back_in, 1, 0)).astype(BF16)
        for i, (rows, target) in enumerate(((key_rows, key_grad), (value_rows, value_grad))):
            copy = pltpu.make_async_copy(rows.at[:, cols], target.at[:, cols], sent.at[2 * h + i])
            copy.start()
            copies.append(copy)
    for copy in copies:
        copy.wait()


def fold_factors(consts, length):
    member = lax.axis_index("seq") % GROUP
    head = member * (consts.shape[1] // 128) // GROUP
    rate = consts[pl.ds(RATE, 1), pl.ds(pl.multiple_of(head * 128, 128), 128)]
    return jnp.exp(-rate * length), jnp.exp(-rate * (length * GROUP))


def totals_kernel(length, consts, parts, gains, *refs):
    out = refs[len(refs) // 2]
    factor, _ = fold_factors(consts, length)
    rows = parts.shape[1]
    total = parts[GROUP - 1]
    for k in range(GROUP - 2, -1, -1):
        total = factor * total + parts[k]
    out[:rows] = total
    out[rows:] = gains[...]


def forward_totals_kernel(length, consts, parts, out):
    factor, _ = fold_factors(consts, length)
    total = parts[0]
    for k in range(1, GROUP):
        total = factor * total + parts[k]
    out[...] = total


def join_kernel(length, consts, total, before, out):
    _, group_factor = fold_factors(consts, length)
    out[...] = total[...] + group_factor * before[...]


def copy_kernel(x, out):
    out[...] = x[...]


def fold_forward_kernel(length, consts, parts, nearest, near, far, token, out):
    factor, group_factor = fold_factors(consts, length)
    carry = nearest[...] + near[...] + group_factor * far[...]
    for k in range(GROUP):
        out[k] = carry
        carry = factor * carry + parts[k]


def fold_back_kernel(length, consts, parts, arrived, *refs):
    out = refs[len(refs) // 2]
    factor, group_factor = fold_factors(consts, length)
    rows = parts.shape[1]
    group = lax.axis_index("seq") // GROUP
    carry = jnp.zeros(parts.shape[1:], F32)
    for g in range(arrived.shape[0] - 1, 0, -1):
        carry = jnp.where(group < g, group_factor * carry + arrived[g, :rows], carry)
    extra = sum(arrived[g, rows:] for g in range(arrived.shape[0]))
    for k in range(GROUP - 1, -1, -1):
        out[k, :rows] = carry
        out[k, rows:] = extra
        carry = factor * carry + parts[k]


def whole_call(kernel, out_shape, operands, in_specs=None, out_specs=None, **rest):
    vmem = pl.BlockSpec(memory_space=pltpu.VMEM)
    if in_specs is None:
        in_specs = [vmem] * len(operands)
    if out_specs is None:
        out_specs = jax.tree.map(lambda _: vmem, out_shape)
    return pl.pallas_call(
        kernel,
        in_specs=in_specs,
        out_specs=out_specs,
        out_shape=out_shape,
        compiler_params=pltpu.CompilerParams(vmem_limit_bytes=VMEM_LIMIT),
        **rest,
    )(*operands)


def send(x, pairs):
    return lax.ppermute(x, "seq", [(a * GROUP + j, b * GROUP + j) for a, b in pairs for j in range(GROUP)])


def scan_forward(x, consts, length, beside):
    groups = lax.axis_size("seq") // GROUP
    members = [[g * GROUP + j for j in range(GROUP)] for g in range(groups)]
    parts = lax.all_to_all(x, "seq", 0, 0, axis_index_groups=members)
    one = jax.ShapeDtypeStruct(x.shape[1:], F32)
    total = whole_call(lambda *refs: forward_totals_kernel(length, *refs), one, [consts, parts])
    nearest = send(total, [(0, 1)])
    total = whole_call(lambda *refs: join_kernel(length, *refs), one, [consts, total, nearest])
    near = send(total, [(1, 2), (2, 3)])
    total = whole_call(copy_kernel, one, [total])
    far = send(total, [(1, 3)])
    result, token = beside(total)
    out = whole_call(lambda *refs: fold_forward_kernel(length, *refs), like(x), [consts, parts, nearest, near, far, token])
    return lax.all_to_all(out, "seq", 0, 0, axis_index_groups=members), result


def scan_back(x, gains, consts, length, kept):
    groups = lax.axis_size("seq") // GROUP
    members = [[g * GROUP + j for j in range(GROUP)] for g in range(groups)]
    across = [[g * GROUP + j for g in range(groups)] for j in range(GROUP)]
    parts = lax.all_to_all(x, "seq", 0, 0, axis_index_groups=members)
    totals, *kept = passing(
        lambda *refs: totals_kernel(length, *refs), array(F32, x.shape[1] + EXTRA, x.shape[2]), [consts, parts, gains], kept
    )
    arrived = lax.all_gather(totals, "seq", axis_index_groups=across)
    out, *kept = passing(
        lambda *refs: fold_back_kernel(length, *refs), array(F32, GROUP, *arrived.shape[1:]), [consts, parts, arrived], kept
    )
    return lax.all_to_all(out, "seq", 0, 0, axis_index_groups=members), kept


def passing(kernel, out_shape, operands, kept):
    return whole_call(
        kernel, [out_shape] + [pltpu.VMEM(x.shape, x.dtype) for x in kept], operands + [in_vmem_space(x) for x in kept],
        input_output_aliases={len(operands) + i: 1 + i for i in range(len(kept))},
    )


def in_vmem_space(x):
    return pltpu.with_memory_space_constraint(x, pltpu.VMEM)


def array(kind, *shape):
    return jax.ShapeDtypeStruct(shape, kind)


def like(x):
    return jax.ShapeDtypeStruct(x.shape, x.dtype)


def body(queries, keys, values, rates, gain, cotangent):
    length, channels = queries.shape
    heads = rates.shape[0]
    size = channels // heads
    head_devices = lax.axis_size("head")
    total_channels = channels * head_devices

    smem = pl.BlockSpec(memory_space=pltpu.SMEM)
    stats_shape = (head_devices, 2 * length // 128, 128)
    scratch = pltpu.VMEM((length, size), F32)

    square = 2 * heads * length * length * size
    wide = array(F32, length, channels)
    narrow = array(BF16, length, channels)

    hbm = lambda x: pltpu.with_memory_space_constraint(x, pltpu.HBM)
    anywhere = pl.BlockSpec(memory_space=pl.ANY)
    in_vmem = pl.BlockSpec(memory_space=pltpu.VMEM)
    rows_scratch = pltpu.VMEM((length, channels), BF16)
    copies = pltpu.SemaphoreType.DMA((2 * heads,))
    sums_shape = (2 * heads, size // 2, size)
    sums, consts = whole_call(
        block_sum_kernel, [array(F32, 2 * heads, size // 2, size), array(F32, 8, channels)],
        [hbm(rates), hbm(gain.reshape(1, channels)), hbm(keys), hbm(values)], in_specs=[anywhere] * 4,
        scratch_shapes=[
            pltpu.SMEM((heads,), F32), pltpu.VMEM((1, channels), F32), rows_scratch, rows_scratch,
            pltpu.SemaphoreType.DMA((2 * heads + 2,)),
        ],
    )

    def cost(flops):
        return pl.CostEstimate(flops=flops, bytes_accessed=6 << 20, transcendentals=0)

    def beside(total):
        return whole_call(
            intra_kernel, [wide, array(F32, 8, 128)], [consts, queries, keys, values, total], cost_estimate=cost(2 * square)
        )

    state_in, intra = scan_forward(sums, consts, length, beside)
    mixed, stats = whole_call(
        mixed_kernel, [wide, array(F32, *stats_shape)],
        [consts, queries, state_in, intra, cotangent], scratch_shapes=[scratch, scratch],
    )
    received = lax.all_to_all(stats, "head", 0, 0)
    sums_shape = (2 * heads, size // 2, size)
    back_sums, gains = whole_call(
        lambda *refs: back_sum_kernel(total_channels, *refs), [pltpu.HBM(sums_shape, F32), array(F32, EXTRA, size)],
        [consts, received, mixed, cotangent, queries], out_specs=[anywhere, in_vmem],
        scratch_shapes=[scratch, scratch, pltpu.VMEM(sums_shape, F32), pltpu.SemaphoreType.DMA((heads,))],
    )
    part = pltpu.VMEM((length, channels), F32)
    attended, query_grad, key_part, value_part = whole_call(
        lambda *refs: grads_kernel(total_channels, *refs), [narrow, narrow, part, part],
        [consts, received, hbm(mixed), hbm(cotangent), hbm(queries), hbm(keys), hbm(values), state_in],
        in_specs=[in_vmem] * 2 + [anywhere] * 5 + [in_vmem],
        out_specs=[anywhere, anywhere, in_vmem, in_vmem],
        scratch_shapes=[
            scratch, scratch, pltpu.VMEM((length, channels), F32), rows_scratch, rows_scratch, rows_scratch,
            rows_scratch, rows_scratch, rows_scratch, rows_scratch, pltpu.SemaphoreType.DMA((5 * heads,)), copies,
        ],
        cost_estimate=cost(6 * square),
    )
    back_in, (key_part, value_part) = scan_back(back_sums, gains, consts, length, [key_part, value_part])
    key_grad, value_grad, gain_grad = whole_call(
        finish_kernel, [narrow, narrow, array(F32, 1, channels)],
        [consts, back_in, keys, values, in_vmem_space(key_part), in_vmem_space(value_part)],
        out_specs=[anywhere, anywhere, in_vmem], scratch_shapes=[rows_scratch, rows_scratch, copies],
    )
    return attended, query_grad, key_grad, value_grad, gain_grad.reshape(channels)


def solution(mesh):
    placed = (
        P("seq", "head"),
        P("seq", "head"),
        P("seq", "head"),
        P("head"),
        P("head"),
        P("seq", "head"),
    )
    return jax.shard_map(
        body,
        mesh=mesh,
        in_specs=placed,
        out_specs=(
            P("seq", "head"),
            P("seq", "head"),
            P("seq", "head"),
            P("seq", "head"),
            P("head"),
        ),
        check_vma=False,
    )
```

```python
import jax
import jax.numpy as jnp
from jax import lax
from jax.experimental import pallas as pl
from jax.experimental.pallas import tpu as pltpu
from jax.sharding import PartitionSpec as P

epsilon = 1e-06
F32, BF16 = jnp.float32, jnp.bfloat16
GROUP = 8
EXTRA = 8
VMEM_LIMIT = 16 * 1024 * 1024


def dot(a, b, over_a, over_b):
    return lax.dot_general(a, b, (((over_a,), (over_b,)), ((), ())), preferred_element_type=F32)


def split(x):
    high = x.astype(BF16)
    return high, (x - high.astype(F32)).astype(BF16)


def dot_split(a, x, over_a, over_x):
    parts = jnp.concatenate(split(x), axis=1 - over_x)
    both = dot(a, parts, over_a, over_x)
    return both[:, : both.shape[1] // 2] + both[:, both.shape[1] // 2 :]


def rows_of(length, width=128):
    return lax.broadcasted_iota(jnp.int32, (length, width), 0).astype(F32)


def head_in_of(rate, length):
    base = jnp.exp(-rate * (rows_of(128) + 1.0))
    return jnp.concatenate([base * jnp.exp(-rate * start) for start in range(0, length, 128)], axis=0)


def tail_out_of(rate, length):
    base = jnp.exp(-rate * (127.0 - rows_of(128)))
    return jnp.concatenate([base * jnp.exp(-rate * (length - 128 - start)) for start in range(0, length, 128)], axis=0)


def tile_weights(rate):
    rows, lanes = rows_of(128), lax.broadcasted_iota(jnp.int32, (1, 128), 1).astype(F32)
    distance = rows - lanes
    near = jnp.where(distance >= 0, jnp.exp(-rate * jnp.maximum(distance, 0.0)), 0.0)
    far = jnp.exp(-rate * (rows + 1.0)) * jnp.exp(-rate * (128 - 1.0 - lanes))
    step = jnp.exp(-rate * 128)
    farther = far * step

    def square(a, b, c, d):
        return jnp.concatenate([jnp.concatenate([a, b], axis=1), jnp.concatenate([c, d], axis=1)], axis=0)

    return square(near, jnp.zeros_like(near), far, near), square(farther, far, farther * step, farther)


def column(h, size):
    return pl.ds(h * size, size)


GAIN, RATE = 0, 1


def block_sum_kernel(rates_in, gain_in, keys, values, out, consts, rates, gain, key_rows, value_rows, arrived):
    length = keys.shape[0]
    heads = rates.shape[0]
    size = keys.shape[1] // heads
    small = [
        pltpu.make_async_copy(rates_in, rates, arrived.at[2 * heads]),
        pltpu.make_async_copy(gain_in, gain, arrived.at[2 * heads + 1]),
    ]
    copies = []
    for h in range(heads):
        cols = column(h, size)
        copies.append(
            [
                pltpu.make_async_copy(source.at[:, cols], rows.at[:, cols], arrived.at[2 * h + i])
                for i, (source, rows) in enumerate(((values, value_rows), (keys, key_rows)))
            ]
        )
        for copy in copies[-1]:
            copy.start()
        if h == 0:
            for copy in small:
                copy.start()
    for copy in small:
        copy.wait()
    for h in range(heads):
        cols = column(h, size)
        rate = jnp.full((1, size), rates[h], F32)
        consts[:, cols] = jnp.concatenate([gain[:, cols], rate, jnp.zeros((6, size), F32)], axis=0)
        tail = tail_out_of(rate, length)
        for copy in copies[h]:
            copy.wait()
        scaled = value_rows[:, cols].astype(F32) * tail
        out[pl.ds(2 * h, 2)] = dot_split(key_rows[:, cols], scaled, 0, 0).reshape(2, size // 2, size)


def weighted(a, b, t, s, weight):
    return (dot(a[t, :], b[s, :], 1, 1) * weight).astype(BF16)


def intra_kernel(consts, queries, keys, values, total, out, token):
    length = queries.shape[0]
    size = 128
    half = length // 2
    first, second = pl.ds(0, half), pl.ds(half, half)
    for h in range(queries.shape[1] // size):
        cols = column(h, size)
        same, across = tile_weights(consts[pl.ds(RATE, 1), cols])
        q, k, v = (ref.at[:, cols] for ref in (queries, keys, values))
        out[first, cols] = dot(weighted(q, k, first, first, same), v[first, :], 1, 0)
        out[second, cols] = dot(weighted(q, k, second, first, across), v[first, :], 1, 0) + dot(
            weighted(q, k, second, second, same), v[second, :], 1, 0
        )
    token[...] = jnp.zeros_like(token)


def mixed_kernel(consts, queries, state, intra, cotangent, mixed, stats, square, inner):
    length = queries.shape[0]
    size = 128
    heads = queries.shape[1] // size
    for h in range(heads):
        cols = column(h, size)
        state_in = state[pl.ds(2 * h, 2)].reshape(size, size)
        value = intra[:, cols] + head_in_of(consts[pl.ds(RATE, 1), cols], length) * dot_split(queries[:, cols], state_in, 1, 0)
        mixed[:, cols] = value
        new_square, new_inner = value * value, cotangent[:, cols].astype(F32) * consts[pl.ds(GAIN, 1), cols] * value
        if h > 0:
            new_square, new_inner = new_square + square[...], new_inner + inner[...]
        square[...] = new_square
        inner[...] = new_inner
    pieces = []
    for ref in (square, inner):
        for start in range(0, length, 128):
            pieces.append(jnp.sum(ref[pl.ds(start, 128), :].T, axis=0, keepdims=True))
    tile = jnp.concatenate(pieces, axis=0)
    stats[...] = jnp.broadcast_to(tile[None], stats.shape)


def token_scales(received, channels, inv_out, coef_out):
    total = jnp.sum(received[...], axis=0)
    chunks = total.shape[0] // 2
    inv = lax.rsqrt(total[:chunks] / channels + epsilon)
    coef = inv * inv * inv * total[chunks:] / channels
    for chunk in range(chunks):
        rows = pl.ds(chunk * 128, 128)
        inv_out[rows, :] = jnp.broadcast_to(inv[chunk : chunk + 1], (128, 128)).T
        coef_out[rows, :] = jnp.broadcast_to(coef[chunk : chunk + 1], (128, 128)).T


def mixed_grad_of(consts, cols, upstream, value, inv, coef):
    return (inv * (upstream * consts[pl.ds(GAIN, 1), cols]) - value * coef).astype(BF16)


def back_sum_kernel(channels, consts, received, mixed, cotangent, queries, sums_out, gains, inv, coef, sums, sent):
    length = queries.shape[0]
    size = 128
    heads = queries.shape[1] // size
    token_scales(received, channels, inv, coef)
    stores = []
    gains[...] = jnp.zeros_like(gains)
    for h in range(heads):
        cols = column(h, size)
        shards = pl.ds(2 * h, 2)
        upstream = cotangent[:, cols].astype(F32)
        value = mixed[:, cols]
        mixed_grad = mixed_grad_of(consts, cols, upstream, value, inv[...], coef[...])
        scaled = mixed_grad.astype(F32) * head_in_of(consts[pl.ds(RATE, 1), cols], length)
        sums[shards] = dot_split(queries[:, cols], scaled, 0, 0).reshape(2, size // 2, size)
        stores.append(pltpu.make_async_copy(sums.at[shards], sums_out.at[shards], sent.at[h]))
        stores[-1].start()
    for h in range(heads):
        cols = column(h, size)
        products = cotangent[:, cols].astype(F32) * (mixed[:, cols] * inv[...])
        gains[pl.ds(h, 1), :] = jnp.sum(products, axis=0, keepdims=True)
    for store in stores:
        store.wait()


def grads_kernel(
    channels, consts, received, mixed_in, cotangent_in, queries_in, keys_in, values_in, state,
    attended_out, query_out, key_part, value_part,
    inv, coef, mixed, cotangent, queries, keys, values, grad, attended, query_grad, arrived, sent,
):
    length = queries.shape[0]
    size = 128
    heads = queries.shape[1] // size
    half = length // 2
    first, second = pl.ds(0, half), pl.ds(half, half)
    copies, stores = [], []
    for h in range(heads):
        cols = column(h, size)
        copies.append(
            [
                pltpu.make_async_copy(source.at[:, cols], rows.at[:, cols], arrived.at[5 * h + i])
                for i, (source, rows) in enumerate(
                    (
                        (mixed_in, mixed),
                        (cotangent_in, cotangent),
                        (values_in, values),
                        (keys_in, keys),
                        (queries_in, queries),
                    )
                )
            ]
        )
        for copy in copies[-1]:
            copy.start()
    token_scales(received, channels, inv, coef)
    for h in range(heads):
        cols = column(h, size)
        rate = consts[pl.ds(RATE, 1), cols]
        state_in = state[pl.ds(2 * h, 2)].reshape(size, size)
        same, across = tile_weights(rate)
        for copy in copies[h]:
            copy.wait()
        value = mixed[:, cols]
        attended[:, cols] = (value * inv[...] * consts[pl.ds(GAIN, 1), cols]).astype(BF16)
        grad[:, cols] = mixed_grad_of(consts, cols, cotangent[:, cols].astype(F32), value, inv[...], coef[...])
        q, k, v, g = (ref.at[:, cols] for ref in (queries, keys, values, grad))
        state_part = head_in_of(rate, length) * dot_split(g[...], state_in, 1, 1)
        upper = weighted(g, v, first, first, same)
        lower = weighted(g, v, second, first, across)
        final = weighted(g, v, second, second, same)
        query_grad[first, cols] = (dot(upper, k[first, :], 1, 0) + state_part[:half]).astype(BF16)
        query_grad[second, cols] = (
            dot(lower, k[first, :], 1, 0) + dot(final, k[second, :], 1, 0) + state_part[half:]
        ).astype(BF16)
        for i, (rows, target) in enumerate(((attended, attended_out), (query_grad, query_out))):
            stores.append(pltpu.make_async_copy(rows.at[:, cols], target.at[:, cols], sent.at[2 * h + i]))
            stores[-1].start()
        key_part[first, cols] = dot(upper, q[first, :], 0, 0) + dot(lower, q[second, :], 0, 0)
        key_part[second, cols] = dot(final, q[second, :], 0, 0)
        upper = weighted(q, k, first, first, same)
        lower = weighted(q, k, second, first, across)
        final = weighted(q, k, second, second, same)
        value_part[first, cols] = dot(upper, g[first, :], 0, 0) + dot(lower, g[second, :], 0, 0)
        value_part[second, cols] = dot(final, g[second, :], 0, 0)
    for store in stores:
        store.wait()


def finish_kernel(
    consts, back, keys, values, key_part, value_part, key_grad, value_grad, gain_grad, key_rows, value_rows, sent
):
    length = keys.shape[0]
    size = 128
    heads = keys.shape[1] // size
    half = size // 2
    copies = []
    for h in range(heads):
        cols = column(h, size)
        back_in = back[pl.ds(2 * h, 2), pl.ds(0, half), :].reshape(size, size)
        tail = tail_out_of(consts[pl.ds(RATE, 1), cols], length)
        key_rows[:, cols] = (key_part[:, cols] + tail * dot_split(values[:, cols], back_in, 1, 1)).astype(BF16)
        value_rows[:, cols] = (value_part[:, cols] + tail * dot_split(keys[:, cols], back_in, 1, 0)).astype(BF16)
        for i, (rows, target) in enumerate(((key_rows, key_grad), (value_rows, value_grad))):
            copy = pltpu.make_async_copy(rows.at[:, cols], target.at[:, cols], sent.at[2 * h + i])
            copy.start()
            copies.append(copy)
    for h in range(heads):
        gain_grad[:, column(h, size)] = sum(back[k, pl.ds(half + h, 1), :] for k in range(GROUP))
    for copy in copies:
        copy.wait()


def fold_factors(consts, length):
    member = lax.axis_index("seq") % GROUP
    head = member * (consts.shape[1] // 128) // GROUP
    rate = consts[pl.ds(RATE, 1), pl.ds(pl.multiple_of(head * 128, 128), 128)]
    return jnp.exp(-rate * length), jnp.exp(-rate * (length * GROUP))


def totals_kernel(length, consts, parts, gains, *refs):
    out = refs[len(refs) // 2]
    factor, _ = fold_factors(consts, length)
    rows = parts.shape[1]
    total = parts[GROUP - 1]
    for k in range(GROUP - 2, -1, -1):
        total = factor * total + parts[k]
    out[:rows] = total
    out[rows:] = gains[...]


def forward_totals_kernel(length, consts, parts, out):
    factor, _ = fold_factors(consts, length)
    total = parts[0]
    for k in range(1, GROUP):
        total = factor * total + parts[k]
    out[...] = total


def join_kernel(length, consts, total, before, out):
    _, group_factor = fold_factors(consts, length)
    out[...] = total[...] + group_factor * before[...]


def copy_kernel(x, out):
    out[...] = x[...]


def fold_forward_kernel(length, consts, parts, nearest, near, far, token, out):
    factor, group_factor = fold_factors(consts, length)
    carry = nearest[...] + near[...] + group_factor * far[...]
    for k in range(GROUP):
        out[k] = carry
        carry = factor * carry + parts[k]


def fold_back_kernel(length, consts, parts, arrived, *refs):
    out = refs[len(refs) // 2]
    factor, group_factor = fold_factors(consts, length)
    rows = parts.shape[1]
    group = lax.axis_index("seq") // GROUP
    carry = jnp.zeros(parts.shape[1:], F32)
    for g in range(arrived.shape[0] - 1, 0, -1):
        carry = jnp.where(group < g, group_factor * carry + arrived[g, :rows], carry)
    extra = sum(arrived[g, rows:] for g in range(arrived.shape[0]))
    for k in range(GROUP - 1, -1, -1):
        out[k, :rows] = carry
        out[k, rows:] = extra
        carry = factor * carry + parts[k]


def whole_call(kernel, out_shape, operands, in_specs=None, out_specs=None, **rest):
    vmem = pl.BlockSpec(memory_space=pltpu.VMEM)
    if in_specs is None:
        in_specs = [vmem] * len(operands)
    if out_specs is None:
        out_specs = jax.tree.map(lambda _: vmem, out_shape)
    return pl.pallas_call(
        kernel,
        in_specs=in_specs,
        out_specs=out_specs,
        out_shape=out_shape,
        compiler_params=pltpu.CompilerParams(vmem_limit_bytes=VMEM_LIMIT),
        **rest,
    )(*operands)


def send(x, pairs):
    return lax.ppermute(x, "seq", [(a * GROUP + j, b * GROUP + j) for a, b in pairs for j in range(GROUP)])


def scan_forward(x, consts, length, beside):
    groups = lax.axis_size("seq") // GROUP
    members = [[g * GROUP + j for j in range(GROUP)] for g in range(groups)]
    parts = lax.all_to_all(x, "seq", 0, 0, axis_index_groups=members)
    one = jax.ShapeDtypeStruct(x.shape[1:], F32)
    total = whole_call(lambda *refs: forward_totals_kernel(length, *refs), one, [consts, parts])
    nearest = send(total, [(0, 1)])
    total = whole_call(lambda *refs: join_kernel(length, *refs), one, [consts, total, nearest])
    near = send(total, [(1, 2), (2, 3)])
    total = whole_call(copy_kernel, one, [total])
    far = send(total, [(1, 3)])
    result, token = beside(total)
    out = whole_call(lambda *refs: fold_forward_kernel(length, *refs), like(x), [consts, parts, nearest, near, far, token])
    return lax.all_to_all(out, "seq", 0, 0, axis_index_groups=members), result


def scan_back(x, gains, consts, length, kept):
    groups = lax.axis_size("seq") // GROUP
    members = [[g * GROUP + j for j in range(GROUP)] for g in range(groups)]
    across = [[g * GROUP + j for g in range(groups)] for j in range(GROUP)]
    parts = lax.all_to_all(x, "seq", 0, 0, axis_index_groups=members)
    totals, *kept = passing(
        lambda *refs: totals_kernel(length, *refs), array(F32, x.shape[1] + EXTRA, x.shape[2]), [consts, parts, gains], kept
    )
    arrived = lax.all_gather(totals, "seq", axis_index_groups=across)
    out, *kept = passing(
        lambda *refs: fold_back_kernel(length, *refs), array(F32, GROUP, *arrived.shape[1:]), [consts, parts, arrived], kept
    )
    return lax.all_to_all(out, "seq", 0, 0, axis_index_groups=members), kept


def passing(kernel, out_shape, operands, kept):
    return whole_call(
        kernel, [out_shape] + [pltpu.VMEM(x.shape, x.dtype) for x in kept], operands + [in_vmem_space(x) for x in kept],
        input_output_aliases={len(operands) + i: 1 + i for i in range(len(kept))},
    )


def in_vmem_space(x):
    return pltpu.with_memory_space_constraint(x, pltpu.VMEM)


def array(kind, *shape):
    return jax.ShapeDtypeStruct(shape, kind)


def like(x):
    return jax.ShapeDtypeStruct(x.shape, x.dtype)


def body(queries, keys, values, rates, gain, cotangent):
    length, channels = queries.shape
    heads = rates.shape[0]
    size = channels // heads
    head_devices = lax.axis_size("head")
    total_channels = channels * head_devices

    smem = pl.BlockSpec(memory_space=pltpu.SMEM)
    stats_shape = (head_devices, 2 * length // 128, 128)
    scratch = pltpu.VMEM((length, size), F32)

    square = 2 * heads * length * length * size
    wide = array(F32, length, channels)
    narrow = array(BF16, length, channels)

    hbm = lambda x: pltpu.with_memory_space_constraint(x, pltpu.HBM)
    anywhere = pl.BlockSpec(memory_space=pl.ANY)
    in_vmem = pl.BlockSpec(memory_space=pltpu.VMEM)
    rows_scratch = pltpu.VMEM((length, channels), BF16)
    copies = pltpu.SemaphoreType.DMA((2 * heads,))
    sums_shape = (2 * heads, size // 2, size)
    sums, consts = whole_call(
        block_sum_kernel, [array(F32, 2 * heads, size // 2, size), array(F32, 8, channels)],
        [hbm(rates), hbm(gain.reshape(1, channels)), hbm(keys), hbm(values)], in_specs=[anywhere] * 4,
        scratch_shapes=[
            pltpu.SMEM((heads,), F32), pltpu.VMEM((1, channels), F32), rows_scratch, rows_scratch,
            pltpu.SemaphoreType.DMA((2 * heads + 2,)),
        ],
    )

    def cost(flops):
        return pl.CostEstimate(flops=flops, bytes_accessed=6 << 20, transcendentals=0)

    def beside(total):
        return whole_call(
            intra_kernel, [wide, array(F32, 8, 128)], [consts, queries, keys, values, total], cost_estimate=cost(2 * square)
        )

    state_in, intra = scan_forward(sums, consts, length, beside)
    mixed, stats = whole_call(
        mixed_kernel, [wide, array(F32, *stats_shape)],
        [consts, queries, state_in, intra, cotangent], scratch_shapes=[scratch, scratch],
    )
    received = lax.all_to_all(stats, "head", 0, 0)
    sums_shape = (2 * heads, size // 2, size)
    back_sums, gains = whole_call(
        lambda *refs: back_sum_kernel(total_channels, *refs), [pltpu.HBM(sums_shape, F32), array(F32, EXTRA, size)],
        [consts, received, mixed, cotangent, queries], out_specs=[anywhere, in_vmem],
        scratch_shapes=[scratch, scratch, pltpu.VMEM(sums_shape, F32), pltpu.SemaphoreType.DMA((heads,))],
    )
    part = pltpu.VMEM((length, channels), F32)
    attended, query_grad, key_part, value_part = whole_call(
        lambda *refs: grads_kernel(total_channels, *refs), [narrow, narrow, part, part],
        [consts, received, hbm(mixed), hbm(cotangent), hbm(queries), hbm(keys), hbm(values), state_in],
        in_specs=[in_vmem] * 2 + [anywhere] * 5 + [in_vmem],
        out_specs=[anywhere, anywhere, in_vmem, in_vmem],
        scratch_shapes=[
            scratch, scratch, pltpu.VMEM((length, channels), F32), rows_scratch, rows_scratch, rows_scratch,
            rows_scratch, rows_scratch, rows_scratch, rows_scratch, pltpu.SemaphoreType.DMA((5 * heads,)), copies,
        ],
        cost_estimate=cost(6 * square),
    )
    back_in, (key_part, value_part) = scan_back(back_sums, gains, consts, length, [key_part, value_part])
    key_grad, value_grad, gain_grad = whole_call(
        finish_kernel, [narrow, narrow, array(F32, 1, channels)],
        [consts, back_in, keys, values, in_vmem_space(key_part), in_vmem_space(value_part)],
        out_specs=[anywhere, anywhere, in_vmem], scratch_shapes=[rows_scratch, rows_scratch, copies],
    )
    return attended, query_grad, key_grad, value_grad, gain_grad.reshape(channels)


def solution(mesh):
    placed = (
        P("seq", "head"),
        P("seq", "head"),
        P("seq", "head"),
        P("head"),
        P("head"),
        P("seq", "head"),
    )
    return jax.shard_map(
        body,
        mesh=mesh,
        in_specs=placed,
        out_specs=(
            P("seq", "head"),
            P("seq", "head"),
            P("seq", "head"),
            P("seq", "head"),
            P("head"),
        ),
        check_vma=False,
    )
```

```python
import jax
import jax.numpy as jnp
from jax import lax
from jax.experimental import pallas as pl
from jax.experimental.pallas import tpu as pltpu
from jax.sharding import PartitionSpec as P

epsilon = 1e-06
F32, BF16 = jnp.float32, jnp.bfloat16
GROUP = 8
EXTRA = 8
VMEM_LIMIT = 16 * 1024 * 1024


def dot(a, b, over_a, over_b):
    return lax.dot_general(a, b, (((over_a,), (over_b,)), ((), ())), preferred_element_type=F32)


def split(x):
    high = x.astype(BF16)
    return high, (x - high.astype(F32)).astype(BF16)


def dot_split(a, x, over_a, over_x):
    parts = jnp.concatenate(split(x), axis=1 - over_x)
    both = dot(a, parts, over_a, over_x)
    return both[:, : both.shape[1] // 2] + both[:, both.shape[1] // 2 :]


def rows_of(length, width=128):
    return lax.broadcasted_iota(jnp.int32, (length, width), 0).astype(F32)


def head_in_of(rate, length):
    base = jnp.exp(-rate * (rows_of(128) + 1.0))
    return jnp.concatenate([base * jnp.exp(-rate * start) for start in range(0, length, 128)], axis=0)


def tail_out_of(rate, length):
    base = jnp.exp(-rate * (127.0 - rows_of(128)))
    return jnp.concatenate([base * jnp.exp(-rate * (length - 128 - start)) for start in range(0, length, 128)], axis=0)


def tile_weights(rate):
    rows, lanes = rows_of(128), lax.broadcasted_iota(jnp.int32, (1, 128), 1).astype(F32)
    distance = rows - lanes
    near = jnp.where(distance >= 0, jnp.exp(-rate * jnp.maximum(distance, 0.0)), 0.0)
    far = jnp.exp(-rate * (rows + 1.0)) * jnp.exp(-rate * (128 - 1.0 - lanes))
    step = jnp.exp(-rate * 128)
    farther = far * step

    def square(a, b, c, d):
        return jnp.concatenate([jnp.concatenate([a, b], axis=1), jnp.concatenate([c, d], axis=1)], axis=0)

    return square(near, jnp.zeros_like(near), far, near), square(farther, far, farther * step, farther)


def column(h, size):
    return pl.ds(h * size, size)


GAIN, RATE = 0, 1


def block_sum_kernel(rates_in, gain_in, keys, values, out, consts, rates, gain, key_rows, value_rows, arrived):
    length = keys.shape[0]
    heads = rates.shape[0]
    size = keys.shape[1] // heads
    small = [
        pltpu.make_async_copy(rates_in, rates, arrived.at[2 * heads]),
        pltpu.make_async_copy(gain_in, gain, arrived.at[2 * heads + 1]),
    ]
    small[0].start()
    copies = []
    for h in range(heads):
        cols = column(h, size)
        copies.append(
            [
                pltpu.make_async_copy(source.at[:, cols], rows.at[:, cols], arrived.at[2 * h + i])
                for i, (source, rows) in enumerate(((values, value_rows), (keys, key_rows)))
            ]
        )
        for copy in copies[-1]:
            copy.start()
    small[1].start()
    small[0].wait()
    for h in range(heads):
        cols = column(h, size)
        tail = tail_out_of(jnp.full((1, size), rates[h], F32), length)
        for copy in copies[h]:
            copy.wait()
        scaled = value_rows[:, cols].astype(F32) * tail
        out[pl.ds(2 * h, 2)] = dot_split(key_rows[:, cols], scaled, 0, 0).reshape(2, size // 2, size)
    small[1].wait()
    for h in range(heads):
        cols = column(h, size)
        rate = jnp.full((1, size), rates[h], F32)
        consts[:, cols] = jnp.concatenate([gain[:, cols], rate, jnp.zeros((6, size), F32)], axis=0)


def weighted(a, b, t, s, weight):
    return (dot(a[t, :], b[s, :], 1, 1) * weight).astype(BF16)


def intra_kernel(consts, queries, keys, values, total, out, token):
    length = queries.shape[0]
    size = 128
    half = length // 2
    first, second = pl.ds(0, half), pl.ds(half, half)
    for h in range(queries.shape[1] // size):
        cols = column(h, size)
        same, across = tile_weights(consts[pl.ds(RATE, 1), cols])
        q, k, v = (ref.at[:, cols] for ref in (queries, keys, values))
        out[first, cols] = dot(weighted(q, k, first, first, same), v[first, :], 1, 0)
        out[second, cols] = dot(weighted(q, k, second, first, across), v[first, :], 1, 0) + dot(
            weighted(q, k, second, second, same), v[second, :], 1, 0
        )
    token[...] = jnp.zeros_like(token)


def mixed_kernel(consts, queries, state, intra, cotangent, mixed, stats, square, inner):
    length = queries.shape[0]
    size = 128
    heads = queries.shape[1] // size
    for h in range(heads):
        cols = column(h, size)
        state_in = state[pl.ds(2 * h, 2)].reshape(size, size)
        value = intra[:, cols] + head_in_of(consts[pl.ds(RATE, 1), cols], length) * dot_split(queries[:, cols], state_in, 1, 0)
        mixed[:, cols] = value
        new_square, new_inner = value * value, cotangent[:, cols].astype(F32) * consts[pl.ds(GAIN, 1), cols] * value
        if h > 0:
            new_square, new_inner = new_square + square[...], new_inner + inner[...]
        square[...] = new_square
        inner[...] = new_inner
    pieces = []
    for ref in (square, inner):
        for start in range(0, length, 128):
            pieces.append(jnp.sum(ref[pl.ds(start, 128), :].T, axis=0, keepdims=True))
    tile = jnp.concatenate(pieces, axis=0)
    stats[...] = jnp.broadcast_to(tile[None], stats.shape)


def token_scales(received, channels, inv_out, coef_out):
    total = jnp.sum(received[...], axis=0)
    chunks = total.shape[0] // 2
    inv = lax.rsqrt(total[:chunks] / channels + epsilon)
    coef = inv * inv * inv * total[chunks:] / channels
    for chunk in range(chunks):
        rows = pl.ds(chunk * 128, 128)
        inv_out[rows, :] = jnp.broadcast_to(inv[chunk : chunk + 1], (128, 128)).T
        coef_out[rows, :] = jnp.broadcast_to(coef[chunk : chunk + 1], (128, 128)).T


def mixed_grad_of(consts, cols, upstream, value, inv, coef):
    return (inv * (upstream * consts[pl.ds(GAIN, 1), cols]) - value * coef).astype(BF16)


def back_sum_kernel(channels, consts, received, mixed, cotangent, queries, sums_out, gains, inv, coef, sums, sent):
    length = queries.shape[0]
    size = 128
    heads = queries.shape[1] // size
    token_scales(received, channels, inv, coef)
    stores = []
    gains[...] = jnp.zeros_like(gains)
    for h in range(heads):
        cols = column(h, size)
        shards = pl.ds(2 * h, 2)
        upstream = cotangent[:, cols].astype(F32)
        value = mixed[:, cols]
        mixed_grad = mixed_grad_of(consts, cols, upstream, value, inv[...], coef[...])
        scaled = mixed_grad.astype(F32) * head_in_of(consts[pl.ds(RATE, 1), cols], length)
        sums[shards] = dot_split(queries[:, cols], scaled, 0, 0).reshape(2, size // 2, size)
        stores.append(pltpu.make_async_copy(sums.at[shards], sums_out.at[shards], sent.at[h]))
        stores[-1].start()
    for h in range(heads):
        cols = column(h, size)
        products = cotangent[:, cols].astype(F32) * (mixed[:, cols] * inv[...])
        gains[pl.ds(h, 1), :] = jnp.sum(products, axis=0, keepdims=True)
    for store in stores:
        store.wait()


def grads_kernel(
    channels, consts, received, mixed_in, cotangent_in, queries_in, keys_in, values_in, state,
    attended_out, query_out, key_part, value_part,
    inv, coef, mixed, cotangent, queries, keys, values, grad, attended, query_grad, arrived, sent,
):
    length = queries.shape[0]
    size = 128
    heads = queries.shape[1] // size
    half = length // 2
    first, second = pl.ds(0, half), pl.ds(half, half)
    copies, stores = [], []
    for h in range(heads):
        cols = column(h, size)
        copies.append(
            [
                pltpu.make_async_copy(source.at[:, cols], rows.at[:, cols], arrived.at[5 * h + i])
                for i, (source, rows) in enumerate(
                    (
                        (mixed_in, mixed),
                        (cotangent_in, cotangent),
                        (values_in, values),
                        (keys_in, keys),
                        (queries_in, queries),
                    )
                )
            ]
        )
        for copy in copies[-1]:
            copy.start()
    token_scales(received, channels, inv, coef)
    for h in range(heads):
        cols = column(h, size)
        rate = consts[pl.ds(RATE, 1), cols]
        state_in = state[pl.ds(2 * h, 2)].reshape(size, size)
        same, across = tile_weights(rate)
        for copy in copies[h]:
            copy.wait()
        value = mixed[:, cols]
        attended[:, cols] = (value * inv[...] * consts[pl.ds(GAIN, 1), cols]).astype(BF16)
        grad[:, cols] = mixed_grad_of(consts, cols, cotangent[:, cols].astype(F32), value, inv[...], coef[...])
        q, k, v, g = (ref.at[:, cols] for ref in (queries, keys, values, grad))
        state_part = head_in_of(rate, length) * dot_split(g[...], state_in, 1, 1)
        upper = weighted(g, v, first, first, same)
        lower = weighted(g, v, second, first, across)
        final = weighted(g, v, second, second, same)
        query_grad[first, cols] = (dot(upper, k[first, :], 1, 0) + state_part[:half]).astype(BF16)
        query_grad[second, cols] = (
            dot(lower, k[first, :], 1, 0) + dot(final, k[second, :], 1, 0) + state_part[half:]
        ).astype(BF16)
        for i, (rows, target) in enumerate(((attended, attended_out), (query_grad, query_out))):
            stores.append(pltpu.make_async_copy(rows.at[:, cols], target.at[:, cols], sent.at[2 * h + i]))
            stores[-1].start()
        key_part[first, cols] = dot(upper, q[first, :], 0, 0) + dot(lower, q[second, :], 0, 0)
        key_part[second, cols] = dot(final, q[second, :], 0, 0)
        upper = weighted(q, k, first, first, same)
        lower = weighted(q, k, second, first, across)
        final = weighted(q, k, second, second, same)
        value_part[first, cols] = dot(upper, g[first, :], 0, 0) + dot(lower, g[second, :], 0, 0)
        value_part[second, cols] = dot(final, g[second, :], 0, 0)
    for store in stores:
        store.wait()


def finish_kernel(
    consts, back, keys, values, key_part, value_part, key_grad, value_grad, gain_grad, key_rows, value_rows, sent
):
    length = keys.shape[0]
    size = 128
    heads = keys.shape[1] // size
    half = size // 2
    copies = []
    for h in range(heads):
        cols = column(h, size)
        back_in = back[pl.ds(2 * h, 2), pl.ds(0, half), :].reshape(size, size)
        tail = tail_out_of(consts[pl.ds(RATE, 1), cols], length)
        key_rows[:, cols] = (key_part[:, cols] + tail * dot_split(values[:, cols], back_in, 1, 1)).astype(BF16)
        value_rows[:, cols] = (value_part[:, cols] + tail * dot_split(keys[:, cols], back_in, 1, 0)).astype(BF16)
        for i, (rows, target) in enumerate(((key_rows, key_grad), (value_rows, value_grad))):
            copy = pltpu.make_async_copy(rows.at[:, cols], target.at[:, cols], sent.at[2 * h + i])
            copy.start()
            copies.append(copy)
    for h in range(heads):
        gain_grad[:, column(h, size)] = sum(back[k, pl.ds(half + h, 1), :] for k in range(GROUP))
    for copy in copies:
        copy.wait()


def fold_factors(consts, length):
    member = lax.axis_index("seq") % GROUP
    head = member * (consts.shape[1] // 128) // GROUP
    rate = consts[pl.ds(RATE, 1), pl.ds(pl.multiple_of(head * 128, 128), 128)]
    return jnp.exp(-rate * length), jnp.exp(-rate * (length * GROUP))


def totals_kernel(length, consts, parts, gains, *refs):
    out = refs[len(refs) // 2]
    factor, _ = fold_factors(consts, length)
    rows = parts.shape[1]
    total = parts[GROUP - 1]
    for k in range(GROUP - 2, -1, -1):
        total = factor * total + parts[k]
    out[:rows] = total
    out[rows:] = gains[...]


def forward_totals_kernel(length, consts, parts, out):
    factor, _ = fold_factors(consts, length)
    total = parts[0]
    for k in range(1, GROUP):
        total = factor * total + parts[k]
    out[...] = total


def join_kernel(length, consts, total, before, out):
    _, group_factor = fold_factors(consts, length)
    out[...] = total[...] + group_factor * before[...]


def copy_kernel(x, out):
    out[...] = x[...]


def fold_forward_kernel(length, consts, parts, nearest, near, far, token, out):
    factor, group_factor = fold_factors(consts, length)
    carry = nearest[...] + near[...] + group_factor * far[...]
    for k in range(GROUP):
        out[k] = carry
        carry = factor * carry + parts[k]


def fold_back_kernel(length, consts, parts, arrived, *refs):
    out = refs[len(refs) // 2]
    factor, group_factor = fold_factors(consts, length)
    rows = parts.shape[1]
    group = lax.axis_index("seq") // GROUP
    carry = jnp.zeros(parts.shape[1:], F32)
    for g in range(arrived.shape[0] - 1, 0, -1):
        carry = jnp.where(group < g, group_factor * carry + arrived[g, :rows], carry)
    extra = sum(arrived[g, rows:] for g in range(arrived.shape[0]))
    for k in range(GROUP - 1, -1, -1):
        out[k, :rows] = carry
        out[k, rows:] = extra
        carry = factor * carry + parts[k]


def whole_call(kernel, out_shape, operands, in_specs=None, out_specs=None, **rest):
    vmem = pl.BlockSpec(memory_space=pltpu.VMEM)
    if in_specs is None:
        in_specs = [vmem] * len(operands)
    if out_specs is None:
        out_specs = jax.tree.map(lambda _: vmem, out_shape)
    return pl.pallas_call(
        kernel,
        in_specs=in_specs,
        out_specs=out_specs,
        out_shape=out_shape,
        compiler_params=pltpu.CompilerParams(vmem_limit_bytes=VMEM_LIMIT),
        **rest,
    )(*operands)


def send(x, pairs):
    return lax.ppermute(x, "seq", [(a * GROUP + j, b * GROUP + j) for a, b in pairs for j in range(GROUP)])


def scan_forward(x, consts, length, beside):
    groups = lax.axis_size("seq") // GROUP
    members = [[g * GROUP + j for j in range(GROUP)] for g in range(groups)]
    parts = lax.all_to_all(x, "seq", 0, 0, axis_index_groups=members)
    one = jax.ShapeDtypeStruct(x.shape[1:], F32)
    total = whole_call(lambda *refs: forward_totals_kernel(length, *refs), one, [consts, parts])
    nearest = send(total, [(0, 1)])
    total = whole_call(lambda *refs: join_kernel(length, *refs), one, [consts, total, nearest])
    near = send(total, [(1, 2), (2, 3)])
    total = whole_call(copy_kernel, one, [total])
    far = send(total, [(1, 3)])
    result, token = beside(total)
    out = whole_call(lambda *refs: fold_forward_kernel(length, *refs), like(x), [consts, parts, nearest, near, far, token])
    return lax.all_to_all(out, "seq", 0, 0, axis_index_groups=members), result


def scan_back(x, gains, consts, length, kept):
    groups = lax.axis_size("seq") // GROUP
    members = [[g * GROUP + j for j in range(GROUP)] for g in range(groups)]
    across = [[g * GROUP + j for g in range(groups)] for j in range(GROUP)]
    parts = lax.all_to_all(x, "seq", 0, 0, axis_index_groups=members)
    totals, *kept = passing(
        lambda *refs: totals_kernel(length, *refs), array(F32, x.shape[1] + EXTRA, x.shape[2]), [consts, parts, gains], kept
    )
    arrived = lax.all_gather(totals, "seq", axis_index_groups=across)
    out, *kept = passing(
        lambda *refs: fold_back_kernel(length, *refs), array(F32, GROUP, *arrived.shape[1:]), [consts, parts, arrived], kept
    )
    return lax.all_to_all(out, "seq", 0, 0, axis_index_groups=members), kept


def passing(kernel, out_shape, operands, kept):
    return whole_call(
        kernel, [out_shape] + [pltpu.VMEM(x.shape, x.dtype) for x in kept], operands + [in_vmem_space(x) for x in kept],
        input_output_aliases={len(operands) + i: 1 + i for i in range(len(kept))},
    )


def in_vmem_space(x):
    return pltpu.with_memory_space_constraint(x, pltpu.VMEM)


def array(kind, *shape):
    return jax.ShapeDtypeStruct(shape, kind)


def like(x):
    return jax.ShapeDtypeStruct(x.shape, x.dtype)


def body(queries, keys, values, rates, gain, cotangent):
    length, channels = queries.shape
    heads = rates.shape[0]
    size = channels // heads
    head_devices = lax.axis_size("head")
    total_channels = channels * head_devices

    smem = pl.BlockSpec(memory_space=pltpu.SMEM)
    stats_shape = (head_devices, 2 * length // 128, 128)
    scratch = pltpu.VMEM((length, size), F32)

    square = 2 * heads * length * length * size
    wide = array(F32, length, channels)
    narrow = array(BF16, length, channels)

    hbm = lambda x: pltpu.with_memory_space_constraint(x, pltpu.HBM)
    anywhere = pl.BlockSpec(memory_space=pl.ANY)
    in_vmem = pl.BlockSpec(memory_space=pltpu.VMEM)
    rows_scratch = pltpu.VMEM((length, channels), BF16)
    copies = pltpu.SemaphoreType.DMA((2 * heads,))
    sums_shape = (2 * heads, size // 2, size)
    sums, consts = whole_call(
        block_sum_kernel, [array(F32, 2 * heads, size // 2, size), array(F32, 8, channels)],
        [hbm(rates), hbm(gain.reshape(1, channels)), hbm(keys), hbm(values)], in_specs=[anywhere] * 4,
        scratch_shapes=[
            pltpu.SMEM((heads,), F32), pltpu.VMEM((1, channels), F32), rows_scratch, rows_scratch,
            pltpu.SemaphoreType.DMA((2 * heads + 2,)),
        ],
    )

    def cost(flops):
        return pl.CostEstimate(flops=flops, bytes_accessed=6 << 20, transcendentals=0)

    def beside(total):
        return whole_call(
            intra_kernel, [wide, array(F32, 8, 128)], [consts, queries, keys, values, total], cost_estimate=cost(2 * square)
        )

    state_in, intra = scan_forward(sums, consts, length, beside)
    mixed, stats = whole_call(
        mixed_kernel, [wide, array(F32, *stats_shape)],
        [consts, queries, state_in, intra, cotangent], scratch_shapes=[scratch, scratch],
    )
    received = lax.all_to_all(stats, "head", 0, 0)
    sums_shape = (2 * heads, size // 2, size)
    back_sums, gains = whole_call(
        lambda *refs: back_sum_kernel(total_channels, *refs), [pltpu.HBM(sums_shape, F32), array(F32, EXTRA, size)],
        [consts, received, mixed, cotangent, queries], out_specs=[anywhere, in_vmem],
        scratch_shapes=[scratch, scratch, pltpu.VMEM(sums_shape, F32), pltpu.SemaphoreType.DMA((heads,))],
    )
    part = pltpu.VMEM((length, channels), F32)
    attended, query_grad, key_part, value_part = whole_call(
        lambda *refs: grads_kernel(total_channels, *refs), [narrow, narrow, part, part],
        [consts, received, hbm(mixed), hbm(cotangent), hbm(queries), hbm(keys), hbm(values), state_in],
        in_specs=[in_vmem] * 2 + [anywhere] * 5 + [in_vmem],
        out_specs=[anywhere, anywhere, in_vmem, in_vmem],
        scratch_shapes=[
            scratch, scratch, pltpu.VMEM((length, channels), F32), rows_scratch, rows_scratch, rows_scratch,
            rows_scratch, rows_scratch, rows_scratch, rows_scratch, pltpu.SemaphoreType.DMA((5 * heads,)), copies,
        ],
        cost_estimate=cost(6 * square),
    )
    back_in, (key_part, value_part) = scan_back(back_sums, gains, consts, length, [key_part, value_part])
    key_grad, value_grad, gain_grad = whole_call(
        finish_kernel, [narrow, narrow, array(F32, 1, channels)],
        [consts, back_in, keys, values, in_vmem_space(key_part), in_vmem_space(value_part)],
        out_specs=[anywhere, anywhere, in_vmem], scratch_shapes=[rows_scratch, rows_scratch, copies],
    )
    return attended, query_grad, key_grad, value_grad, gain_grad.reshape(channels)


def solution(mesh):
    placed = (
        P("seq", "head"),
        P("seq", "head"),
        P("seq", "head"),
        P("head"),
        P("head"),
        P("seq", "head"),
    )
    return jax.shard_map(
        body,
        mesh=mesh,
        in_specs=placed,
        out_specs=(
            P("seq", "head"),
            P("seq", "head"),
            P("seq", "head"),
            P("seq", "head"),
            P("head"),
        ),
        check_vma=False,
    )
```

```python
import jax
import jax.numpy as jnp
from jax import lax
from jax.experimental import pallas as pl
from jax.experimental.pallas import tpu as pltpu
from jax.sharding import PartitionSpec as P

epsilon = 1e-06
F32, BF16 = jnp.float32, jnp.bfloat16
GROUP = 8
EXTRA = 8
VMEM_LIMIT = 16 * 1024 * 1024


def dot(a, b, over_a, over_b):
    return lax.dot_general(a, b, (((over_a,), (over_b,)), ((), ())), preferred_element_type=F32)


def split(x):
    high = x.astype(BF16)
    return high, (x - high.astype(F32)).astype(BF16)


def dot_split(a, x, over_a, over_x):
    parts = jnp.concatenate(split(x), axis=1 - over_x)
    both = dot(a, parts, over_a, over_x)
    return both[:, : both.shape[1] // 2] + both[:, both.shape[1] // 2 :]


def rows_of(length, width=128):
    return lax.broadcasted_iota(jnp.int32, (length, width), 0).astype(F32)


def head_in_of(rate, length):
    base = jnp.exp(-rate * (rows_of(128) + 1.0))
    return jnp.concatenate([base * jnp.exp(-rate * start) for start in range(0, length, 128)], axis=0)


def tail_out_of(rate, length):
    base = jnp.exp(-rate * (127.0 - rows_of(128)))
    return jnp.concatenate([base * jnp.exp(-rate * (length - 128 - start)) for start in range(0, length, 128)], axis=0)


def tile_weights(rate):
    rows, lanes = rows_of(128), lax.broadcasted_iota(jnp.int32, (1, 128), 1).astype(F32)
    distance = rows - lanes
    near = jnp.where(distance >= 0, jnp.exp(-rate * jnp.maximum(distance, 0.0)), 0.0)
    far = jnp.exp(-rate * (rows + 1.0)) * jnp.exp(-rate * (128 - 1.0 - lanes))
    step = jnp.exp(-rate * 128)
    farther = far * step

    def square(a, b, c, d):
        return jnp.concatenate([jnp.concatenate([a, b], axis=1), jnp.concatenate([c, d], axis=1)], axis=0)

    return square(near, jnp.zeros_like(near), far, near), square(farther, far, farther * step, farther)


def column(h, size):
    return pl.ds(h * size, size)


GAIN, RATE = 0, 1


def block_sum_kernel(rates_in, gain_in, keys, values, out, consts, rates, gain, key_rows, value_rows, arrived):
    length = keys.shape[0]
    heads = rates.shape[0]
    size = keys.shape[1] // heads
    small = [
        pltpu.make_async_copy(rates_in, rates, arrived.at[2 * heads]),
        pltpu.make_async_copy(gain_in, gain, arrived.at[2 * heads + 1]),
    ]
    small[0].start()
    copies = []
    for h in range(heads):
        cols = column(h, size)
        copies.append(
            [
                pltpu.make_async_copy(source.at[:, cols], rows.at[:, cols], arrived.at[2 * h + i])
                for i, (source, rows) in enumerate(((values, value_rows), (keys, key_rows)))
            ]
        )
        for copy in copies[-1]:
            copy.start()
    small[1].start()
    small[0].wait()
    for h in range(heads):
        cols = column(h, size)
        tail = tail_out_of(jnp.full((1, size), rates[h], F32), length)
        for copy in copies[h]:
            copy.wait()
        scaled = value_rows[:, cols].astype(F32) * tail
        out[pl.ds(2 * h, 2)] = dot_split(key_rows[:, cols], scaled, 0, 0).reshape(2, size // 2, size)
    small[1].wait()
    for h in range(heads):
        cols = column(h, size)
        rate = jnp.full((1, size), rates[h], F32)
        consts[:, cols] = jnp.concatenate([gain[:, cols], rate, jnp.zeros((6, size), F32)], axis=0)


def weighted(a, b, t, s, weight):
    return (dot(a[t, :], b[s, :], 1, 1) * weight).astype(BF16)


def intra_kernel(consts, queries, keys, values, total, out, token):
    length = queries.shape[0]
    size = 128
    half = length // 2
    first, second = pl.ds(0, half), pl.ds(half, half)
    for h in range(queries.shape[1] // size):
        cols = column(h, size)
        same, across = tile_weights(consts[pl.ds(RATE, 1), cols])
        q, k, v = (ref.at[:, cols] for ref in (queries, keys, values))
        out[first, cols] = dot(weighted(q, k, first, first, same), v[first, :], 1, 0)
        out[second, cols] = dot(weighted(q, k, second, first, across), v[first, :], 1, 0) + dot(
            weighted(q, k, second, second, same), v[second, :], 1, 0
        )
    token[...] = jnp.zeros_like(token)


def mixed_kernel(consts, queries, state, intra, cotangent, mixed, stats, square, inner):
    length = queries.shape[0]
    size = 128
    heads = queries.shape[1] // size
    for h in range(heads):
        cols = column(h, size)
        state_in = state[pl.ds(2 * h, 2)].reshape(size, size)
        value = intra[:, cols] + head_in_of(consts[pl.ds(RATE, 1), cols], length) * dot_split(queries[:, cols], state_in, 1, 0)
        mixed[:, cols] = value
        new_square, new_inner = value * value, cotangent[:, cols].astype(F32) * consts[pl.ds(GAIN, 1), cols] * value
        if h > 0:
            new_square, new_inner = new_square + square[...], new_inner + inner[...]
        square[...] = new_square
        inner[...] = new_inner
    pieces = []
    for ref in (square, inner):
        for start in range(0, length, 128):
            pieces.append(jnp.sum(ref[pl.ds(start, 128), :].T, axis=0, keepdims=True))
    tile = jnp.concatenate(pieces, axis=0)
    stats[...] = jnp.broadcast_to(tile[None], stats.shape)


def token_scales(received, channels, inv_out, coef_out):
    total = jnp.sum(received[...], axis=0)
    chunks = total.shape[0] // 2
    inv = lax.rsqrt(total[:chunks] / channels + epsilon)
    coef = inv * inv * inv * total[chunks:] / channels
    for chunk in range(chunks):
        rows = pl.ds(chunk * 128, 128)
        inv_out[rows, :] = jnp.broadcast_to(inv[chunk : chunk + 1], (128, 128)).T
        coef_out[rows, :] = jnp.broadcast_to(coef[chunk : chunk + 1], (128, 128)).T


def mixed_grad_of(consts, cols, upstream, value, inv, coef):
    return (inv * (upstream * consts[pl.ds(GAIN, 1), cols]) - value * coef).astype(BF16)


def back_sum_kernel(channels, consts, received, mixed, cotangent, queries, sums_out, inv, coef, sums, sent):
    length = queries.shape[0]
    size = 128
    heads = queries.shape[1] // size
    token_scales(received, channels, inv, coef)
    stores = []
    for h in range(heads):
        cols = column(h, size)
        shards = pl.ds(2 * h, 2)
        upstream = cotangent[:, cols].astype(F32)
        value = mixed[:, cols]
        mixed_grad = mixed_grad_of(consts, cols, upstream, value, inv[...], coef[...])
        scaled = mixed_grad.astype(F32) * head_in_of(consts[pl.ds(RATE, 1), cols], length)
        sums[shards] = dot_split(queries[:, cols], scaled, 0, 0).reshape(2, size // 2, size)
        stores.append(pltpu.make_async_copy(sums.at[shards], sums_out.at[shards], sent.at[h]))
        stores[-1].start()
    for store in stores:
        store.wait()


def grads_kernel(
    channels, consts, received, mixed_in, cotangent_in, queries_in, keys_in, values_in, state,
    attended_out, query_out, key_part, value_part, gains,
    inv, coef, mixed, cotangent, queries, keys, values, grad, attended, query_grad, arrived, sent,
):
    length = queries.shape[0]
    size = 128
    heads = queries.shape[1] // size
    half = length // 2
    first, second = pl.ds(0, half), pl.ds(half, half)
    copies, stores = [], []
    for h in range(heads):
        cols = column(h, size)
        copies.append(
            [
                pltpu.make_async_copy(source.at[:, cols], rows.at[:, cols], arrived.at[5 * h + i])
                for i, (source, rows) in enumerate(
                    (
                        (mixed_in, mixed),
                        (cotangent_in, cotangent),
                        (values_in, values),
                        (keys_in, keys),
                        (queries_in, queries),
                    )
                )
            ]
        )
        for copy in copies[-1]:
            copy.start()
    gains[...] = jnp.zeros_like(gains)
    token_scales(received, channels, inv, coef)
    for h in range(heads):
        cols = column(h, size)
        rate = consts[pl.ds(RATE, 1), cols]
        state_in = state[pl.ds(2 * h, 2)].reshape(size, size)
        same, across = tile_weights(rate)
        for copy in copies[h]:
            copy.wait()
        value = mixed[:, cols]
        attended[:, cols] = (value * inv[...] * consts[pl.ds(GAIN, 1), cols]).astype(BF16)
        upstream = cotangent[:, cols].astype(F32)
        gains[pl.ds(h, 1), :] = jnp.sum(upstream * (value * inv[...]), axis=0, keepdims=True)
        grad[:, cols] = mixed_grad_of(consts, cols, upstream, value, inv[...], coef[...])
        q, k, v, g = (ref.at[:, cols] for ref in (queries, keys, values, grad))
        state_part = head_in_of(rate, length) * dot_split(g[...], state_in, 1, 1)
        upper = weighted(g, v, first, first, same)
        lower = weighted(g, v, second, first, across)
        final = weighted(g, v, second, second, same)
        query_grad[first, cols] = (dot(upper, k[first, :], 1, 0) + state_part[:half]).astype(BF16)
        query_grad[second, cols] = (
            dot(lower, k[first, :], 1, 0) + dot(final, k[second, :], 1, 0) + state_part[half:]
        ).astype(BF16)
        for i, (rows, target) in enumerate(((attended, attended_out), (query_grad, query_out))):
            stores.append(pltpu.make_async_copy(rows.at[:, cols], target.at[:, cols], sent.at[2 * h + i]))
            stores[-1].start()
        key_part[first, cols] = dot(upper, q[first, :], 0, 0) + dot(lower, q[second, :], 0, 0)
        key_part[second, cols] = dot(final, q[second, :], 0, 0)
        upper = weighted(q, k, first, first, same)
        lower = weighted(q, k, second, first, across)
        final = weighted(q, k, second, second, same)
        value_part[first, cols] = dot(upper, g[first, :], 0, 0) + dot(lower, g[second, :], 0, 0)
        value_part[second, cols] = dot(final, g[second, :], 0, 0)
    for store in stores:
        store.wait()


def finish_kernel(
    consts, back, keys, values, key_part, value_part, key_grad, value_grad, gain_grad, key_rows, value_rows, sent
):
    length = keys.shape[0]
    size = 128
    heads = keys.shape[1] // size
    half = size // 2
    copies = []
    for h in range(heads):
        cols = column(h, size)
        back_in = back[pl.ds(2 * h, 2), pl.ds(0, half), :].reshape(size, size)
        tail = tail_out_of(consts[pl.ds(RATE, 1), cols], length)
        key_rows[:, cols] = (key_part[:, cols] + tail * dot_split(values[:, cols], back_in, 1, 1)).astype(BF16)
        value_rows[:, cols] = (value_part[:, cols] + tail * dot_split(keys[:, cols], back_in, 1, 0)).astype(BF16)
        for i, (rows, target) in enumerate(((key_rows, key_grad), (value_rows, value_grad))):
            copy = pltpu.make_async_copy(rows.at[:, cols], target.at[:, cols], sent.at[2 * h + i])
            copy.start()
            copies.append(copy)
    for h in range(heads):
        gain_grad[:, column(h, size)] = sum(back[k, pl.ds(half + h, 1), :] for k in range(GROUP))
    for copy in copies:
        copy.wait()


def fold_factors(consts, length):
    member = lax.axis_index("seq") % GROUP
    head = member * (consts.shape[1] // 128) // GROUP
    rate = consts[pl.ds(RATE, 1), pl.ds(pl.multiple_of(head * 128, 128), 128)]
    return jnp.exp(-rate * length), jnp.exp(-rate * (length * GROUP))


def totals_kernel(length, consts, parts, gains, *refs):
    out = refs[len(refs) // 2]
    factor, _ = fold_factors(consts, length)
    rows = parts.shape[1]
    total = parts[GROUP - 1]
    for k in range(GROUP - 2, -1, -1):
        total = factor * total + parts[k]
    out[:rows] = total
    out[rows:] = gains[...]


def forward_totals_kernel(length, consts, parts, out):
    factor, _ = fold_factors(consts, length)
    total = parts[0]
    for k in range(1, GROUP):
        total = factor * total + parts[k]
    out[...] = total


def join_kernel(length, consts, total, before, out):
    _, group_factor = fold_factors(consts, length)
    out[...] = total[...] + group_factor * before[...]


def copy_kernel(x, out):
    out[...] = x[...]


def fold_forward_kernel(length, consts, parts, nearest, near, far, token, out):
    factor, group_factor = fold_factors(consts, length)
    carry = nearest[...] + near[...] + group_factor * far[...]
    for k in range(GROUP):
        out[k] = carry
        carry = factor * carry + parts[k]


def fold_back_kernel(length, consts, parts, arrived, *refs):
    out = refs[len(refs) // 2]
    factor, group_factor = fold_factors(consts, length)
    rows = parts.shape[1]
    group = lax.axis_index("seq") // GROUP
    carry = jnp.zeros(parts.shape[1:], F32)
    for g in range(arrived.shape[0] - 1, 0, -1):
        carry = jnp.where(group < g, group_factor * carry + arrived[g, :rows], carry)
    extra = sum(arrived[g, rows:] for g in range(arrived.shape[0]))
    for k in range(GROUP - 1, -1, -1):
        out[k, :rows] = carry
        out[k, rows:] = extra
        carry = factor * carry + parts[k]


def whole_call(kernel, out_shape, operands, in_specs=None, out_specs=None, **rest):
    vmem = pl.BlockSpec(memory_space=pltpu.VMEM)
    if in_specs is None:
        in_specs = [vmem] * len(operands)
    if out_specs is None:
        out_specs = jax.tree.map(lambda _: vmem, out_shape)
    return pl.pallas_call(
        kernel,
        in_specs=in_specs,
        out_specs=out_specs,
        out_shape=out_shape,
        compiler_params=pltpu.CompilerParams(vmem_limit_bytes=VMEM_LIMIT),
        **rest,
    )(*operands)


def send(x, pairs):
    return lax.ppermute(x, "seq", [(a * GROUP + j, b * GROUP + j) for a, b in pairs for j in range(GROUP)])


def scan_forward(x, consts, length, beside):
    groups = lax.axis_size("seq") // GROUP
    members = [[g * GROUP + j for j in range(GROUP)] for g in range(groups)]
    parts = lax.all_to_all(x, "seq", 0, 0, axis_index_groups=members)
    one = jax.ShapeDtypeStruct(x.shape[1:], F32)
    total = whole_call(lambda *refs: forward_totals_kernel(length, *refs), one, [consts, parts])
    nearest = send(total, [(0, 1)])
    total = whole_call(lambda *refs: join_kernel(length, *refs), one, [consts, total, nearest])
    near = send(total, [(1, 2), (2, 3)])
    total = whole_call(copy_kernel, one, [total])
    far = send(total, [(1, 3)])
    result, token = beside(total)
    out = whole_call(lambda *refs: fold_forward_kernel(length, *refs), like(x), [consts, parts, nearest, near, far, token])
    return lax.all_to_all(out, "seq", 0, 0, axis_index_groups=members), result


def scan_back(x, gains, consts, length, kept):
    groups = lax.axis_size("seq") // GROUP
    members = [[g * GROUP + j for j in range(GROUP)] for g in range(groups)]
    across = [[g * GROUP + j for g in range(groups)] for j in range(GROUP)]
    parts = lax.all_to_all(x, "seq", 0, 0, axis_index_groups=members)
    totals, *kept = passing(
        lambda *refs: totals_kernel(length, *refs), array(F32, x.shape[1] + EXTRA, x.shape[2]), [consts, parts, gains], kept
    )
    arrived = lax.all_gather(totals, "seq", axis_index_groups=across)
    out, *kept = passing(
        lambda *refs: fold_back_kernel(length, *refs), array(F32, GROUP, *arrived.shape[1:]), [consts, parts, arrived], kept
    )
    return lax.all_to_all(out, "seq", 0, 0, axis_index_groups=members), kept


def passing(kernel, out_shape, operands, kept):
    return whole_call(
        kernel, [out_shape] + [pltpu.VMEM(x.shape, x.dtype) for x in kept], operands + [in_vmem_space(x) for x in kept],
        input_output_aliases={len(operands) + i: 1 + i for i in range(len(kept))},
    )


def in_vmem_space(x):
    return pltpu.with_memory_space_constraint(x, pltpu.VMEM)


def array(kind, *shape):
    return jax.ShapeDtypeStruct(shape, kind)


def like(x):
    return jax.ShapeDtypeStruct(x.shape, x.dtype)


def body(queries, keys, values, rates, gain, cotangent):
    length, channels = queries.shape
    heads = rates.shape[0]
    size = channels // heads
    head_devices = lax.axis_size("head")
    total_channels = channels * head_devices

    smem = pl.BlockSpec(memory_space=pltpu.SMEM)
    stats_shape = (head_devices, 2 * length // 128, 128)
    scratch = pltpu.VMEM((length, size), F32)

    square = 2 * heads * length * length * size
    wide = array(F32, length, channels)
    narrow = array(BF16, length, channels)

    hbm = lambda x: pltpu.with_memory_space_constraint(x, pltpu.HBM)
    anywhere = pl.BlockSpec(memory_space=pl.ANY)
    in_vmem = pl.BlockSpec(memory_space=pltpu.VMEM)
    rows_scratch = pltpu.VMEM((length, channels), BF16)
    copies = pltpu.SemaphoreType.DMA((2 * heads,))
    sums_shape = (2 * heads, size // 2, size)
    sums, consts = whole_call(
        block_sum_kernel, [array(F32, 2 * heads, size // 2, size), array(F32, 8, channels)],
        [hbm(rates), hbm(gain.reshape(1, channels)), hbm(keys), hbm(values)], in_specs=[anywhere] * 4,
        scratch_shapes=[
            pltpu.SMEM((heads,), F32), pltpu.VMEM((1, channels), F32), rows_scratch, rows_scratch,
            pltpu.SemaphoreType.DMA((2 * heads + 2,)),
        ],
    )

    def cost(flops):
        return pl.CostEstimate(flops=flops, bytes_accessed=6 << 20, transcendentals=0)

    def beside(total):
        return whole_call(
            intra_kernel, [wide, array(F32, 8, 128)], [consts, queries, keys, values, total], cost_estimate=cost(2 * square)
        )

    state_in, intra = scan_forward(sums, consts, length, beside)
    mixed, stats = whole_call(
        mixed_kernel, [wide, array(F32, *stats_shape)],
        [consts, queries, state_in, intra, cotangent], scratch_shapes=[scratch, scratch],
    )
    received = lax.all_to_all(stats, "head", 0, 0)
    sums_shape = (2 * heads, size // 2, size)
    back_sums = whole_call(
        lambda *refs: back_sum_kernel(total_channels, *refs), pltpu.HBM(sums_shape, F32),
        [consts, received, mixed, cotangent, queries], out_specs=anywhere,
        scratch_shapes=[scratch, scratch, pltpu.VMEM(sums_shape, F32), pltpu.SemaphoreType.DMA((heads,))],
    )
    part = pltpu.VMEM((length, channels), F32)
    attended, query_grad, key_part, value_part, gains = whole_call(
        lambda *refs: grads_kernel(total_channels, *refs), [narrow, narrow, part, part, array(F32, EXTRA, size)],
        [consts, received, hbm(mixed), hbm(cotangent), hbm(queries), hbm(keys), hbm(values), state_in],
        in_specs=[in_vmem] * 2 + [anywhere] * 5 + [in_vmem],
        out_specs=[anywhere, anywhere, in_vmem, in_vmem, in_vmem],
        scratch_shapes=[
            scratch, scratch, pltpu.VMEM((length, channels), F32), rows_scratch, rows_scratch, rows_scratch,
            rows_scratch, rows_scratch, rows_scratch, rows_scratch, pltpu.SemaphoreType.DMA((5 * heads,)), copies,
        ],
        cost_estimate=cost(6 * square),
    )
    back_in, (key_part, value_part) = scan_back(back_sums, gains, consts, length, [key_part, value_part])
    key_grad, value_grad, gain_grad = whole_call(
        finish_kernel, [narrow, narrow, array(F32, 1, channels)],
        [consts, back_in, keys, values, in_vmem_space(key_part), in_vmem_space(value_part)],
        out_specs=[anywhere, anywhere, in_vmem], scratch_shapes=[rows_scratch, rows_scratch, copies],
    )
    return attended, query_grad, key_grad, value_grad, gain_grad.reshape(channels)


def solution(mesh):
    placed = (
        P("seq", "head"),
        P("seq", "head"),
        P("seq", "head"),
        P("head"),
        P("head"),
        P("seq", "head"),
    )
    return jax.shard_map(
        body,
        mesh=mesh,
        in_specs=placed,
        out_specs=(
            P("seq", "head"),
            P("seq", "head"),
            P("seq", "head"),
            P("seq", "head"),
            P("head"),
        ),
        check_vma=False,
    )
```
